128 devices in a mesh: rep: 4 (over y), dom: 32 (over x, z, core).
Axes of the slice: x: 4, y: 4, z: 4, core: 2. Of those that a mesh axis runs over, the one named last changes fastest.
Arguments:
- features: bfloat16 [65536, 128], P('dom'), may hold values from -6 to 6
- proj_weight: bfloat16 [128, 256], replicated, may hold values from -0.5 to 0.5
- bias: float32 [256], replicated, may hold values from -3 to 3
- cotangent: bfloat16 [65536, 256], P('dom'), may hold values from -6 to 6
- send_rows: int32 [32, 32, 128], P('dom'), may hold values from 0 to 2047
- send_count: int32 [32, 32], P('dom'), may hold values from 32 to 128, as said below
- hub_blocks: int32 [8], replicated, may hold values from 0 to 511, as said below
- tile_dst: int32 [4, 32, 384], P('rep', 'dom'), may hold values from 0 to 15, as said below
- tile_src: int32 [4, 32, 384], P('rep', 'dom'), may hold values from 0 to 55
- tile_weight: bfloat16 [4, 32, 384, 128, 128], P('rep', 'dom'), may hold values from 0.0019989014 to 0.019897461
Outputs:
- output: bfloat16 [65536, 256], P('dom')
- grad_x: float32 [65536, 128], P('dom')
- grad_w: float32 [128, 256], replicated
The draws below stay inside these ranges and needn't reach their ends.
Inputs may be any that keep to these rules, and one draw needn't show every extreme that they name: `send_count`: for every owner one peer's count is exactly 128 and another's exactly 32. `hub_blocks`: distinct block numbers; the first and the last block are always among them. On every device the pairs (tile_dst, tile_src) of its 384 tiles are distinct.
All inputs are finite; a program needn't handle non-finite values.
Results may differ from the reference program's by a relative error of at most 0.0061.
Values may be sent and summed in bfloat16 or wider, within the bound.
No kernel may reach another device: no remote copies, remote signals or barrier semaphores. Data moves between devices by JAX's collectives and lax.ppermute only.
A program may use at most 128 MiB of HBM per device.

```python
import math
import jax
import jax.numpy as jnp
from jax import lax

FIN = 128
HID = 256
BLK = 128
ROWS = 2048
SEND = 128
HUBS = 8
TILES = 384
NODES = 65536
N_REP = 4
N_DOM = 32


def tile_pairs(key):
    local_blocks = ROWS // BLK
    source_blocks = local_blocks + N_DOM * SEND // BLK + HUBS
    pair_total = local_blocks * source_blocks

    def one_device(device_key):
        first, second = jax.random.split(device_key)
        middle = jax.random.permutation(first, pair_total - 2)[:TILES - 2].astype(jnp.int32) + 1
        ends = jnp.array([0, pair_total - 1], dtype=jnp.int32)
        chosen = jnp.concatenate([ends, middle])
        chosen = chosen[jax.random.permutation(second, TILES)]
        return (chosen // source_blocks, chosen % source_blocks)
    device_keys = jax.random.split(key, N_REP * N_DOM)
    dst_part, src_part = jax.vmap(one_device)(device_keys)
    return (dst_part.reshape(N_REP, N_DOM, TILES).astype(jnp.int32), src_part.reshape(N_REP, N_DOM, TILES).astype(jnp.int32))


def draw_tile_dst(key, part):
    pairs = tile_pairs(key)
    return pairs[0]


def draw_tile_src(key, part):
    pairs = tile_pairs(key)
    return pairs[1]


def draw_send_count(key, part):
    key = jax.random.fold_in(key, 11)
    first, second, third = jax.random.split(key, 3)
    counts = jax.random.randint(first, (N_DOM, N_DOM), SEND // 4, SEND + 1)
    top_peer = jax.random.randint(second, (N_DOM,), 0, N_DOM)
    low_peer = (top_peer + jax.random.randint(third, (N_DOM,), 1, N_DOM)) % N_DOM
    column = jnp.arange(N_DOM, dtype=jnp.int32)[None, :]
    counts = jnp.where(column == low_peer[:, None], SEND // 4, counts)
    counts = jnp.where(column == top_peer[:, None], SEND, counts)
    return counts.astype(jnp.int32)


def draw_hub_blocks(key, part):
    key = jax.random.fold_in(key, 23)
    first, second = jax.random.split(key)
    block_total = NODES // BLK
    middle = jax.random.permutation(first, block_total - 2)[:HUBS - 2].astype(jnp.int32) + 1
    ends = jnp.array([0, block_total - 1], dtype=jnp.int32)
    chosen = jnp.concatenate([ends, middle])
    return chosen[jax.random.permutation(second, HUBS)].astype(jnp.int32)


def place_ends(result, key, low, top_value):
    longest = result.shape.index(max(result.shape))
    spots = []
    for shift in (0, 1):
        where = [jax.random.randint(jax.random.fold_in(key, axis), (), 0, length) for axis, length in enumerate(result.shape)]
        where[longest] = (where[longest] + shift) % result.shape[longest]
        spots.append(tuple(where))
    return result.at[spots[0]].set(low).at[spots[1]].set(top_value)


def shard_levels(stream_key, dims, cuts, smallest, high):
    level = 1.0
    for dim, blocks in cuts:
        draws = jax.random.uniform(jax.random.fold_in(jax.random.fold_in(stream_key, 6), dim), (blocks,), jnp.float32, smallest / len(cuts), high / len(cuts))
        level = level * jnp.repeat(jnp.exp(draws), dims[dim] // blocks).reshape((-1,) + (1,) * (len(dims) - 1 - dim))
    return level


def scatter_about(stream_key, shape, width, limit, shards=(), kind=jnp.bfloat16):
    entries = jax.random.normal(stream_key, shape, jnp.float32) * width
    if len(shards) > 0:
        entries = shard_levels(stream_key, shape, shards, -0.22, 0.18) * entries
    return jnp.clip(entries, min=-limit, max=limit).astype(kind)


def setup_inputs(seed: int = 0) -> dict:
    keys = jax.random.split(jax.random.key(seed), 11)
    return {
        "features": scatter_about(keys[0], (NODES, FIN), 1.0, 6.0, ((0, 32),)),
        "proj_weight": scatter_about(keys[1], (FIN, HID), FIN ** -0.5, 0.5),
        "bias": scatter_about(keys[2], (HID,), 0.5, 3.0, (), jnp.float32),
        "cotangent": scatter_about(keys[3], (NODES, HID), 1.0, 6.0, ((0, 32),)),
        "send_rows": place_ends(jax.random.randint(keys[4], (N_DOM, N_DOM, SEND), 0, ROWS), jax.random.fold_in(keys[4], 1), 0, ROWS - 1).astype(jnp.int32),
        "send_count": draw_send_count(jax.random.fold_in(keys[10], 71), 0),
        "hub_blocks": draw_hub_blocks(jax.random.fold_in(keys[10], 71), 0),
        "tile_dst": draw_tile_dst(jax.random.fold_in(keys[10], 71), 0),
        "tile_src": draw_tile_src(jax.random.fold_in(keys[10], 71), 0),
        "tile_weight": jnp.clip(jnp.exp(math.log(0.019897461) - 2.2979944 * jax.random.uniform(keys[9], (N_REP, N_DOM, TILES, BLK, BLK), jnp.float32) ** shard_levels(keys[9], (N_REP, N_DOM, TILES, BLK, BLK), ((0, 4), (1, 32)), -0.2, 0.2)), 0.0019989014, 0.019897461).astype(jnp.bfloat16),
    }


def tile_forward(blocks, dst_index, src_index, weights, local_blocks):
    picked = blocks[src_index].astype(jnp.float32)
    products = jnp.einsum('tij,tjh->tih', weights.astype(jnp.float32), picked)
    return jax.ops.segment_sum(products, dst_index, num_segments=local_blocks)

def tile_backward(grad_blocks, dst_index, src_index, weights, buffer_blocks):
    picked = grad_blocks[dst_index].astype(jnp.float32)
    products = jnp.einsum('tij,tih->tjh', weights.astype(jnp.float32), picked)
    return jax.ops.segment_sum(products, src_index, num_segments=buffer_blocks)

def reference(features, proj_weight, bias, cotangent, send_rows, send_count, hub_blocks, tile_dst, tile_src, tile_weight):
    local_blocks = ROWS // BLK
    buffer_blocks = local_blocks + N_DOM * SEND // BLK + HUBS
    projected = jnp.dot(features, proj_weight, preferred_element_type=jnp.float32).astype(jnp.bfloat16)
    slot_index = jnp.arange(SEND, dtype=jnp.int32)
    owner_index = jnp.arange(N_DOM, dtype=jnp.int32)
    hub_rows = (hub_blocks[:, None] * BLK + jnp.arange(BLK, dtype=jnp.int32)[None, :]).reshape(-1)
    hub_data = projected[hub_rows]

    def list_rows(dom_index):
        global_rows = owner_index[:, None] * ROWS + send_rows[:, dom_index, :]
        live_slots = slot_index[None, :] < send_count[:, dom_index][:, None]
        return (global_rows, live_slots)

    def sources(dom_index):
        global_rows, live_slots = list_rows(dom_index)
        remote = jnp.where(live_slots[:, :, None], projected[global_rows], jnp.zeros((), projected.dtype))
        local_part = lax.dynamic_slice_in_dim(projected, dom_index * ROWS, ROWS, 0)
        joined = jnp.concatenate([local_part, remote.reshape(N_DOM * SEND, HID), hub_data], 0)
        return joined.reshape(buffer_blocks, BLK, HID)

    def forward_dom(dom_index):
        blocks = sources(dom_index)
        totals = jnp.zeros((local_blocks, BLK, HID), jnp.float32)
        for rep_index in range(N_REP):
            totals = totals + tile_forward(blocks, tile_dst[rep_index, dom_index], tile_src[rep_index, dom_index], tile_weight[rep_index, dom_index], local_blocks)
        return totals.reshape(ROWS, HID)
    z_rows = lax.map(forward_dom, jnp.arange(N_DOM, dtype=jnp.int32)).reshape(NODES, HID)
    pre = z_rows + bias
    activated, pullback = jax.vjp(jax.nn.gelu, pre)
    output = activated.astype(jnp.bfloat16)
    pre_grad = pullback(cotangent.astype(jnp.float32))[0].astype(jnp.bfloat16)
    grad_blocks = pre_grad.reshape(N_DOM, local_blocks, BLK, HID)

    def backward_dom(carried, dom_index):
        global_rows, live_slots = list_rows(dom_index)
        gathered = jnp.zeros((buffer_blocks, BLK, HID), jnp.float32)
        for rep_index in range(N_REP):
            gathered = gathered + tile_backward(grad_blocks[dom_index], tile_dst[rep_index, dom_index], tile_src[rep_index, dom_index], tile_weight[rep_index, dom_index], buffer_blocks)
        flattened = gathered.reshape(buffer_blocks * BLK, HID)
        local_part = flattened[:ROWS]
        remote = flattened[ROWS:ROWS + N_DOM * SEND].reshape(N_DOM, SEND, HID)
        hub_part = flattened[ROWS + N_DOM * SEND:]
        current = lax.dynamic_slice_in_dim(carried, dom_index * ROWS, ROWS, 0)
        carried = lax.dynamic_update_slice_in_dim(carried, current + local_part, dom_index * ROWS, 0)
        masked = jnp.where(live_slots[:, :, None], remote, jnp.zeros((), jnp.float32))
        carried = carried.at[global_rows.reshape(-1)].add(masked.reshape(-1, HID))
        carried = carried.at[hub_rows].add(hub_part)
        return (carried, None)
    dproj, _ = lax.scan(backward_dom, jnp.zeros((NODES, HID), jnp.float32), jnp.arange(N_DOM, dtype=jnp.int32))
    dproj_b = dproj.astype(jnp.bfloat16)
    grad_x = jnp.dot(dproj_b, proj_weight.T, preferred_element_type=jnp.float32)
    grad_w = jnp.dot(features.T, dproj_b, preferred_element_type=jnp.float32) * (1.0 / math.sqrt(NODES))
    return (output, grad_x, grad_w)
```

```python
import functools
import math

import jax
import jax.numpy as jnp
from jax import lax
from jax.experimental import pallas as pl
from jax.experimental.pallas import tpu as pltpu
from jax.sharding import PartitionSpec as P

F32 = jnp.float32
BF16 = jnp.bfloat16
BLK = 128
N_REP = 4
N_DOM = 32
FIN = 128
HID = 256
ROWS = 2048
LOCAL = ROWS // BLK
HUBS = 8
BLOCKS = LOCAL + N_DOM + HUBS
TILES = 384
GROUP = 16
HUB_ROWS = HUBS * BLK // N_DOM
QUARTER = ROWS // N_REP
QB = LOCAL // N_REP
FQ = FIN // N_REP
MSG = FQ + 16
LO = 256
VMEM_LIMIT = 48 * 1024 * 1024

VM = pl.BlockSpec(memory_space=pltpu.VMEM)
SM = pl.BlockSpec(memory_space=pltpu.SMEM)
PARAMS = pltpu.CompilerParams(vmem_limit_bytes=VMEM_LIMIT)


def dot(a, b):
    return jnp.dot(a, b, preferred_element_type=F32)


def halves(x):
    high = x.astype(BF16)
    return high, (x - high.astype(F32)).astype(BF16)


def column(row):
    return jnp.broadcast_to(row, (BLK, BLK)).T


def low_onehot(col):
    low = jnp.where(col < 0, -1, col & (LO - 1))
    lane = lax.broadcasted_iota(jnp.int32, (BLK, BLK), 1)
    return jnp.concatenate(
        [jnp.where(low == lane + k * BLK, 1.0, 0.0) for k in range(LO // BLK)], axis=1
    ).astype(BF16)


def gather_kernel(index_ref, feat_ref, out_ref):
    def step(p, carry):
        col = column(index_ref[pl.ds(p, 1), :])
        hot = low_onehot(col)
        high = lax.shift_right_arithmetic(col, 8)
        total = jnp.zeros((BLK, FIN), F32)
        for pair in range(ROWS // LO // 2):
            left = feat_ref[pl.ds(2 * pair * LO, LO), :]
            right = feat_ref[pl.ds((2 * pair + 1) * LO, LO), :]
            got = dot(hot, jnp.concatenate([left, right], axis=1))
            total = jnp.where(high == 2 * pair, got[:, :FIN], total)
            total = jnp.where(high == 2 * pair + 1, got[:, FIN:], total)
        out_ref[pl.ds(p, 1), pl.ds(0, BLK), :] = total.astype(BF16)[None]
        return carry

    lax.fori_loop(0, N_DOM, step, 0)


def gather_rows(index, features):
    return pl.pallas_call(
        gather_kernel,
        out_shape=jax.ShapeDtypeStruct((N_DOM, BLK + HUB_ROWS, FIN), BF16),
        in_specs=[VM, VM],
        out_specs=VM,
        compiler_params=PARAMS,
        cost_estimate=pl.CostEstimate(flops=4 * 10**9, bytes_accessed=2 * 10**6, transcendentals=0),
        name="gather_rows",
    )(index, features)


def forward_kernel(
    dst_ref, src_ref, rep_ref, feat_ref, recv_ref, w_ref, own_ref, s1_ref, s2_ref, s3_ref, xs, acc
):
    step = pl.program_id(0)

    @pl.when(step == 0)
    def _():
        xs[pl.ds(0, LOCAL)] = feat_ref[...]
        xs[pl.ds(LOCAL, N_DOM)] = recv_ref[:, pl.ds(0, BLK), :]
        per_hub = BLK // HUB_ROWS
        for p in range(N_DOM):
            xs[LOCAL + N_DOM + p // per_hub, pl.ds((p % per_hub) * HUB_ROWS, HUB_ROWS), :] = recv_ref[
                p, pl.ds(BLK, HUB_ROWS), :
            ]
        acc[...] = jnp.zeros_like(acc)

    for base in range(0, GROUP, 4):
        found = []
        for k in range(base, base + 4):
            t = step * GROUP + k
            found.append((dst_ref[t], dot(w_ref[k], xs[src_ref[t]])))
        for d, value in found:
            acc[d] += value

    @pl.when(step == pl.num_programs(0) - 1)
    def _():
        rep = rep_ref[0]
        own_ref[...] = acc[pl.ds(rep * QB, QB)]
        for k, ref in ((1, s1_ref), (2, s2_ref), (3, s3_ref)):
            ref[...] = acc[pl.ds(lax.rem(rep + k, N_REP) * QB, QB)].astype(BF16)


def forward_tiles(dst, src, rep, features, received, weights):
    quarter = (QB, BLK, FIN)
    whole = lambda shape: pl.BlockSpec(shape, lambda i: (0,) * len(shape))
    return pl.pallas_call(
        forward_kernel,
        grid=(TILES // GROUP,),
        out_shape=[jax.ShapeDtypeStruct(quarter, F32)] + [jax.ShapeDtypeStruct(quarter, BF16)] * 3,
        in_specs=[
            SM,
            SM,
            SM,
            whole((LOCAL, BLK, FIN)),
            whole((N_DOM, BLK + HUB_ROWS, FIN)),
            pl.BlockSpec((GROUP, BLK, BLK), lambda i: (i, 0, 0)),
        ],
        out_specs=[whole(quarter)] * 4,
        scratch_shapes=[pltpu.VMEM((BLOCKS, BLK, FIN), BF16), pltpu.VMEM((LOCAL, BLK, FIN), F32)],
        compiler_params=PARAMS,
        cost_estimate=pl.CostEstimate(flops=4 * 10**9, bytes_accessed=14 * 10**6, transcendentals=0),
        name="forward_tiles",
    )(dst, src, rep, features, received, weights)


def middle_kernel(own_ref, a_ref, b_ref, c_ref, w_ref, bias_ref, cot_ref, out_ref, y_ref, gw_ref):
    zx = (own_ref[...] + a_ref[...].astype(F32)) + (b_ref[...].astype(F32) + c_ref[...].astype(F32))
    zx = zx.reshape(QUARTER, FIN)
    weight = w_ref[...]
    zh, zl = halves(zx)
    pre = dot(zh, weight) + dot(zl, weight) + bias_ref[...]
    root = math.sqrt(2.0 / math.pi)
    square = pre * pre
    bent = jnp.tanh(root * (pre + 0.044715 * (square * pre)))
    cdf = 0.5 * (1.0 + bent)
    out_ref[...] = (pre * cdf).astype(BF16)
    slope = cdf + (0.5 * pre) * ((1.0 - bent * bent) * (root * (1.0 + (3 * 0.044715) * square)))
    pre_grad = (cot_ref[...].astype(F32) * slope).astype(BF16)
    yt = lax.dot_general(weight, pre_grad, (((1,), (1,)), ((), ())), preferred_element_type=F32)
    yt = yt.astype(BF16)
    for k in range(QB):
        y_ref[k] = yt[:, k * BLK : (k + 1) * BLK]
    th, tl = halves(zx.T)
    gw = dot(th, pre_grad) + dot(tl, pre_grad)
    for part, piece in enumerate(halves(gw)):
        for c in range(16):
            g, side = c // 2, c % 2
            gw_ref[part * 16 + c] = piece[g * 16 : (g + 1) * 16, side * BLK : (side + 1) * BLK]


def middle(rep, own, a, b, c, weight, bias, cotangent):
    whole = lambda shape: pl.BlockSpec(shape, lambda i, rep_ref: (0,) * len(shape))
    quarter = (QB, BLK, FIN)
    return pl.pallas_call(
        lambda rep_ref, *refs: middle_kernel(*refs),
        grid_spec=pltpu.PrefetchScalarGridSpec(
            num_scalar_prefetch=1,
            grid=(1,),
            in_specs=[whole(quarter)] * 4
            + [
                whole((FIN, HID)),
                whole((1, HID)),
                pl.BlockSpec((QUARTER, HID), lambda i, rep_ref: (rep_ref[0], 0)),
            ],
            out_specs=[whole((QUARTER, HID)), whole((QB, FIN, BLK)), whole((32, 16, BLK))],
        ),
        out_shape=[
            jax.ShapeDtypeStruct((QUARTER, HID), BF16),
            jax.ShapeDtypeStruct((QB, FIN, BLK), BF16),
            jax.ShapeDtypeStruct((32, 16, BLK), BF16),
        ],
        compiler_params=PARAMS,
        name="middle",
    )(rep, own, a, b, c, weight, bias, cotangent)


def backward_kernel(
    dst_ref, src_ref, rep_ref, y0, y1, y2, y3, gw_ref, w_ref, msg_ref, own_ref, s1, s2, s3, ys, acc
):
    step = pl.program_id(0)
    rep = rep_ref[0]

    @pl.when(step == 0)
    def _():
        for k, ref in enumerate((y0, y1, y2, y3)):
            ys[pl.ds(lax.rem(rep + N_REP - k, N_REP) * QB, QB)] = ref[...]
        acc[...] = jnp.zeros_like(acc)

    for base in range(0, GROUP, 4):
        found = []
        for k in range(base, base + 4):
            t = step * GROUP + k
            found.append((src_ref[t], dot(ys[dst_ref[t]], w_ref[k])))
        for s, value in found:
            acc[s] += value

    @pl.when(step == pl.num_programs(0) - 1)
    def _():
        for q in range(N_REP):
            rows = pl.ds(q * FQ, FQ)
            msg_ref[q, :, pl.ds(0, FQ), :] = acc[pl.ds(LOCAL, N_DOM), rows, :].astype(BF16)
            for m in range(16):
                piece = acc[LOCAL + N_DOM + m // 2, pl.ds(q * FQ + (m % 2) * 16, 16), :]
                msg_ref[q, 2 * m, pl.ds(FQ, 16), :] = piece.astype(BF16)
                if m < 8:
                    msg_ref[q, 2 * m + 1, pl.ds(FQ, 16), :] = gw_ref[q * 8 + m]
                else:
                    msg_ref[q, 2 * m + 1, pl.ds(FQ, 16), :] = jnp.zeros((16, BLK), BF16)
        def rows_of(k):
            start = pl.multiple_of(lax.rem(rep + k, N_REP) * FQ, FQ)
            return acc[pl.ds(0, LOCAL), pl.ds(start, FQ), :]
        own_ref[...] = rows_of(0)
        for k, ref in ((1, s1), (2, s2), (3, s3)):
            ref[...] = rows_of(k).astype(BF16)


def backward_tiles(dst, src, rep, ys, gw, weights):
    whole = lambda shape: pl.BlockSpec(shape, lambda i: (0,) * len(shape))
    part = (LOCAL, FQ, BLK)
    return pl.pallas_call(
        backward_kernel,
        grid=(TILES // GROUP,),
        out_shape=[
            jax.ShapeDtypeStruct((N_REP, N_DOM, MSG, BLK), BF16),
            jax.ShapeDtypeStruct(part, F32),
        ]
        + [jax.ShapeDtypeStruct(part, BF16)] * 3,
        in_specs=[SM, SM, SM]
        + [whole((QB, FIN, BLK))] * 4
        + [whole((32, 16, BLK)), pl.BlockSpec((GROUP, BLK, BLK), lambda i: (i, 0, 0))],
        out_specs=[whole((N_REP, N_DOM, MSG, BLK))] + [whole(part)] * 4,
        scratch_shapes=[pltpu.VMEM((LOCAL, FIN, BLK), BF16), pltpu.VMEM((BLOCKS, FIN, BLK), F32)],
        compiler_params=PARAMS,
        cost_estimate=pl.CostEstimate(flops=4 * 10**9, bytes_accessed=14 * 10**6, transcendentals=0),
        name="backward_tiles",
    )(dst, src, rep, *ys, gw, weights)


def scatter_kernel(index_ref, recv_ref, own_ref, a_ref, b_ref, c_ref, out_ref, acc):
    chunks = ROWS // LO
    acc[...] = jnp.zeros_like(acc)

    def step(i, carry):
        hots, sides = [], []
        for j in range(2):
            p = 2 * i + j
            row = index_ref[pl.ds(p, 1), :]
            hots.append(low_onehot(column(row)))
            total = recv_ref[p, pl.ds(0, FQ), :].astype(F32)
            for r in range(1, N_REP):
                total = total + recv_ref[r * N_DOM + p, pl.ds(0, FQ), :].astype(F32)
            high = lax.shift_right_arithmetic(row, 8)
            here = [jnp.where(high == c, total, 0.0) for c in range(chunks)]
            pieces = [halves(h) for h in here]
            sides.append(jnp.concatenate([h for h, _ in pieces] + [l for _, l in pieces], axis=0))
        acc[...] += dot(jnp.concatenate(sides, axis=1), jnp.concatenate(hots, axis=0))
        return carry

    lax.fori_loop(0, N_DOM // 2, step, 0)
    for b in range(LOCAL):
        c, side = b // 2, b % 2
        lanes = pl.ds(side * BLK, BLK)
        here = acc[pl.ds(c * FQ, FQ), lanes] + acc[pl.ds((chunks + c) * FQ, FQ), lanes]
        near = own_ref[b] + a_ref[b].astype(F32) + b_ref[b].astype(F32) + c_ref[b].astype(F32)
        out_ref[b] = here + near


def scatter_rows(index, received, own, a, b, c):
    return pl.pallas_call(
        scatter_kernel,
        out_shape=jax.ShapeDtypeStruct((LOCAL, FQ, BLK), F32),
        in_specs=[VM] * 6,
        out_specs=VM,
        scratch_shapes=[pltpu.VMEM((2 * FIN * 2, LO), F32)],
        compiler_params=PARAMS,
        cost_estimate=pl.CostEstimate(flops=4 * 10**9, bytes_accessed=4 * 10**6, transcendentals=0),
        name="scatter_rows",
    )(index, received, own, a, b, c)


def hub_kernel(dom_ref, hub_ref, part_ref, shared_ref, out_ref):
    out_ref[pl.ds(0, LOCAL * FQ), :] = part_ref[...].reshape(LOCAL * FQ, BLK)
    for h in range(HUBS):
        block = hub_ref[h]

        @pl.when(lax.shift_right_logical(block, 4) == dom_ref[0])
        def _():
            start = pl.multiple_of((block & (LOCAL - 1)) * FQ, FQ)
            for k in range(2):
                out_ref[pl.ds(start + k * 16, 16), :] += shared_ref[4 * h + 2 * k]

    for m in range(8):
        out_ref[pl.ds(LOCAL * FQ + m * 16, 16), :] = shared_ref[2 * m + 1]


def add_hubs(dom, hubs, part, shared):
    return pl.pallas_call(
        hub_kernel,
        out_shape=jax.ShapeDtypeStruct((LOCAL * FQ + 128, BLK), F32),
        in_specs=[SM, SM, VM, VM],
        out_specs=VM,
        compiler_params=PARAMS,
        name="add_hubs",
    )(dom, hubs, part, shared)


def final_kernel(rep_ref, m0, m1, m2, m3, gx_ref, gw_ref, blocks, chunks, *, scale):
    rep = rep_ref[0]
    for k, ref in enumerate((m0, m1, m2, m3)):
        q = lax.rem(rep + N_REP - k, N_REP)
        start = pl.multiple_of(q * FQ, FQ)
        blocks[:, pl.ds(start, FQ), :] = ref[pl.ds(0, LOCAL * FQ), :].reshape(LOCAL, FQ, BLK)
        chunks[pl.ds(q * 8, 8)] = ref[pl.ds(LOCAL * FQ, 128), :].reshape(8, 16, BLK)
    for b in range(LOCAL):
        gx_ref[pl.ds(b * BLK, BLK), :] = blocks[b].T
    for c in range(16):
        g, side = c // 2, c % 2
        gw_ref[pl.ds(g * 16, 16), pl.ds(side * BLK, BLK)] = (chunks[c] + chunks[16 + c]) * scale


def finish(rep, parts, scale):
    return pl.pallas_call(
        functools.partial(final_kernel, scale=scale),
        out_shape=[
            jax.ShapeDtypeStruct((ROWS, FIN), F32),
            jax.ShapeDtypeStruct((FIN, HID), F32),
        ],
        in_specs=[SM] + [VM] * 4,
        out_specs=[VM, VM],
        scratch_shapes=[pltpu.VMEM((LOCAL, FIN, BLK), F32), pltpu.VMEM((32, 16, BLK), F32)],
        compiler_params=PARAMS,
        name="finish",
    )(rep, *parts)


def place_kernel(rep_ref, o0, o1, o2, o3, out_ref):
    for k, ref in enumerate((o0, o1, o2, o3)):
        start = pl.multiple_of(lax.rem(rep_ref[0] + N_REP - k, N_REP) * QUARTER, QUARTER)
        out_ref[pl.ds(start, QUARTER), :] = ref[...]


def place_output(rep, parts):
    return pl.pallas_call(
        place_kernel,
        out_shape=jax.ShapeDtypeStruct((ROWS, HID), BF16),
        in_specs=[SM] + [VM] * 4,
        out_specs=VM,
        compiler_params=PARAMS,
        name="place_output",
    )(rep, *parts)


def turn(value, k):
    return lax.ppermute(value, "rep", [(i, (i + k) % N_REP) for i in range(N_REP)])


def around(value):
    return [value] + [turn(value, k) for k in (1, 2, 3)]


def swap(value, axes):
    return lax.all_to_all(value, axes, split_axis=0, concat_axis=0, tiled=True)


def shards(
    features,
    proj_weight,
    bias,
    cotangent,
    send_rows,
    send_count,
    hub_blocks,
    tile_dst,
    tile_src,
    tile_weight,
):
    dom_here = lax.axis_index("dom")
    rep = lax.axis_index("rep").astype(jnp.int32).reshape(1)
    dom = dom_here.astype(jnp.int32).reshape(1)
    slots = jnp.arange(BLK, dtype=jnp.int32)[None, :]
    index = jnp.where(slots < send_count[0][:, None], send_rows[0], -1)
    blocks = features.reshape(LOCAL, BLK, FIN)
    dst, src, weights = tile_dst[0, 0], tile_src[0, 0], tile_weight[0, 0]

    hub_owner = hub_blocks // LOCAL
    mine = (hub_owner == dom_here)[:, None, None]
    hub_rows = jnp.where(mine, blocks[hub_blocks % LOCAL], jnp.zeros((), BF16))
    spread = swap(hub_rows.reshape(N_DOM, HUB_ROWS, FIN), "dom")
    listed = gather_rows(index, features)
    holder = hub_owner[dom_here // (BLK // HUB_ROWS)]
    piece = lax.dynamic_index_in_dim(spread, holder, 0, keepdims=True)
    piece = jnp.broadcast_to(piece, (N_DOM, HUB_ROWS, FIN))
    outgoing = lax.dynamic_update_slice(listed, piece, (0, BLK, 0))
    received = swap(outgoing, "dom")

    own, s1, s2, s3 = forward_tiles(dst, src, rep, blocks, received, weights)
    a, b, c = turn(s1, 1), turn(s2, 2), turn(s3, 3)
    out_part, y_part, gw_part = middle(
        rep, own, a, b, c, proj_weight, bias.reshape(1, HID), cotangent
    )
    ys = around(y_part)
    message, own, s1, s2, s3 = backward_tiles(dst, src, rep, ys, gw_part, weights)
    returned = swap(message.reshape(N_REP * N_DOM, MSG, BLK), ("rep", "dom"))
    a, b, c = turn(s1, 1), turn(s2, 2), turn(s3, 3)
    output = place_output(rep, around(out_part))

    chunk = jnp.sum(returned[:, FQ:, :].astype(F32), axis=0)
    shared = swap(jnp.broadcast_to(chunk[None], (N_DOM, 16, BLK)), "dom")
    part = scatter_rows(index, returned, own, a, b, c)
    whole = add_hubs(dom, hub_blocks, part, shared)
    grad_x, grad_w = finish(rep, around(whole), 1.0 / math.sqrt(ROWS * N_DOM))
    return (output, grad_x, grad_w)


def solution(mesh):
    in_specs = (
        P("dom", None),
        P(),
        P(),
        P("dom", None),
        P("dom", None, None),
        P("dom", None),
        P(),
        P("rep", "dom", None),
        P("rep", "dom", None),
        P("rep", "dom", None, None, None),
    )
    out_specs = (P("dom", None), P("dom", None), P())
    return jax.shard_map(shards, mesh=mesh, in_specs=in_specs, out_specs=out_specs, check_vma=False)
```

```python
import functools
import math

import jax
import jax.numpy as jnp
from jax import lax
from jax.experimental import pallas as pl
from jax.experimental.pallas import tpu as pltpu
from jax.sharding import PartitionSpec as P

F32 = jnp.float32
BF16 = jnp.bfloat16
BLK = 128
N_REP = 4
N_DOM = 32
FIN = 128
HID = 256
ROWS = 2048
LOCAL = ROWS // BLK
HUBS = 8
BLOCKS = LOCAL + N_DOM + HUBS
TILES = 384
REMOTE = N_DOM
PAIRED_HUBS = HUBS // N_REP
CHUNK = 32
FWD_SLOTS = 512
BWD_SLOTS = 512
QUARTER = ROWS // N_REP
QB = LOCAL // N_REP
FQ = FIN // N_REP
GW_ROWS = FQ * HID // BLK
FOLD = HUBS * FQ
LO = 256
VMEM_LIMIT = 24 * 1024 * 1024

VM = pl.BlockSpec(memory_space=pltpu.VMEM)
SM = pl.BlockSpec(memory_space=pltpu.SMEM)
PARAMS = pltpu.CompilerParams(vmem_limit_bytes=VMEM_LIMIT)
TILE_PARAMS = pltpu.CompilerParams(vmem_limit_bytes=VMEM_LIMIT)


def dot(a, b):
    return jnp.dot(a, b, preferred_element_type=F32)


def halves(x):
    high = x.astype(BF16)
    return high, (x - high.astype(F32)).astype(BF16)


def column(row):
    return jnp.broadcast_to(row, (BLK, BLK)).T


def low_onehot(col):
    low = jnp.where(col < 0, -1, col & (LO - 1))
    lane = lax.broadcasted_iota(jnp.int32, (BLK, BLK), 1)
    return jnp.concatenate(
        [jnp.where(low == lane + k * BLK, 1.0, 0.0) for k in range(LO // BLK)], axis=1
    ).astype(BF16)


def sort_tiles(bucket, operand, empty, edges, out_of, slots):
    sub = lax.broadcasted_iota(jnp.int32, (BLK, BLK), 0)
    lane = lax.broadcasted_iota(jnp.int32, (BLK, BLK), 1)
    line = lane[:1]
    parts = len(bucket)
    cols = [column(b) for b in bucket]
    hots = [jnp.where(c == lane, 1.0, 0.0) for c in cols]
    counts = sum(jnp.sum(h, axis=0, keepdims=True) for h in hots).astype(jnp.int32)
    padded = (counts + 1) & -2
    before = jnp.where(sub < lane, column(padded).astype(F32), 0.0)
    starts = jnp.sum(before, axis=0, keepdims=True).astype(jnp.int32)
    first = jnp.zeros((1, BLK), jnp.int32)
    low = 0
    for n, high in enumerate(edges):
        inside = (line >= low) & (line < high)
        size = jnp.sum(jnp.where(inside, padded, 0).astype(F32), axis=1, keepdims=True).astype(jnp.int32)
        gap = ((size + CHUNK - 1) & -CHUNK) - size
        starts = starts + jnp.where(line >= high, gap, 0)
        total = (size + CHUNK - 1) // CHUNK
        first = first + jnp.where(line > n, total, 0)
        low = high
    begin, end = column(starts), column(starts + padded)
    places = []
    for i in range(parts):
        rank = jnp.sum(jnp.where(hots[i] > 0.0, starts.astype(F32), 0.0), axis=1, keepdims=True)
        for j in range(i + 1):
            same = jnp.broadcast_to(bucket[j], (BLK, BLK)) == cols[i]
            if j == i:
                same = same & (lane < sub)
            rank = rank + jnp.sum(jnp.where(same, 1.0, 0.0), axis=1, keepdims=True)
        places.append(jnp.broadcast_to(rank.astype(jnp.int32), (BLK, BLK)))
    shifted = [column(o - empty).astype(F32) for o in operand]
    tiles, blocks, outs = [], [], []
    for s in range(slots // BLK):
        here = lane + s * BLK
        tile = jnp.zeros((1, BLK), F32)
        block = jnp.zeros((1, BLK), F32)
        for i in range(parts):
            hit = places[i] == here
            tile = tile + jnp.sum(jnp.where(hit, (sub + i * BLK).astype(F32), 0.0), axis=0, keepdims=True)
            block = block + jnp.sum(jnp.where(hit, shifted[i], 0.0), axis=0, keepdims=True)
        inside = (begin <= here) & (here < end)
        out = jnp.sum(jnp.where(inside, out_of(sub).astype(F32), 0.0), axis=0, keepdims=True)
        tiles.append(tile.astype(jnp.int32))
        blocks.append(block.astype(jnp.int32) + empty)
        outs.append(out.astype(jnp.int32))
    return tiles, blocks, outs, first


def order_kernel(dst_ref, src_ref, fwd_ref, bwd_ref):
    parts = TILES // BLK
    dst = [dst_ref[pl.ds(i, 1), :] for i in range(parts)]
    src = [src_ref[pl.ds(i, 1), :] for i in range(parts)]
    bucket = [jnp.where(s < LOCAL, d, d + LOCAL) for d, s in zip(dst, src)]
    operand = [jnp.where(s < LOCAL, s, s - LOCAL) for s in src]
    empty = REMOTE + HUBS
    found = sort_tiles(bucket, operand, empty, (LOCAL, 2 * LOCAL), lambda b: b & (LOCAL - 1), FWD_SLOTS)
    for n, rows in enumerate(found[:3]):
        for s, row in enumerate(rows):
            fwd_ref[n, pl.ds(s, 1), :] = row
    fwd_ref[3, pl.ds(0, 1), :] = found[3]
    far = REMOTE + HUBS
    bucket = [jnp.where(s < LOCAL, s + far, s - LOCAL) for s in src]
    found = sort_tiles(
        bucket, dst, LOCAL, (far, far + LOCAL), lambda b: jnp.where(b < far, b, b - far), BWD_SLOTS
    )
    for n, rows in enumerate(found[:3]):
        for s, row in enumerate(rows):
            bwd_ref[n, pl.ds(s, 1), :] = row
    bwd_ref[3, pl.ds(0, 1), :] = found[3]


def order_tiles(dst, src):
    return pl.pallas_call(
        order_kernel,
        out_shape=[
            jax.ShapeDtypeStruct((4, FWD_SLOTS // BLK, BLK), jnp.int32),
            jax.ShapeDtypeStruct((4, BWD_SLOTS // BLK, BLK), jnp.int32),
        ],
        in_specs=[VM, VM],
        out_specs=[VM, VM],
        compiler_params=PARAMS,
        name="order_tiles",
    )(dst, src)


def run_class(plan_ref, number, product, acc):
    def chunk(i, carry):
        row, col = i // (BLK // CHUNK), lax.rem(i, BLK // CHUNK) * CHUNK
        found = []
        for k in range(0, CHUNK, 2):
            one = (plan_ref[0, row, col + k], plan_ref[1, row, col + k])
            two = (plan_ref[0, row, col + k + 1], plan_ref[1, row, col + k + 1])
            found.append((plan_ref[2, row, col + k], product(one, two)))
        for d, value in found:
            acc[d] += value
        return carry

    lax.fori_loop(plan_ref[3, 0, number], plan_ref[3, 0, number + 1], chunk, 0)


PEERS = 4


def gather_kernel(rows_ref, count_ref, feat_ref, out_ref):
    slot = lax.broadcasted_iota(jnp.int32, (1, BLK), 1)

    def step(i, carry):
        cols = []
        for j in range(PEERS):
            p = PEERS * i + j
            row = jnp.where(slot < count_ref[0, p], rows_ref[pl.ds(p, 1), :], -1)
            cols.append(column(row))
        hot = jnp.concatenate([low_onehot(c) for c in cols], axis=0)
        high = lax.shift_right_arithmetic(jnp.concatenate(cols, axis=0), 8)
        total = jnp.zeros((PEERS * BLK, FIN), F32)
        for pair in range(ROWS // LO // 2):
            left = feat_ref[pl.ds(2 * pair * LO, LO), :]
            right = feat_ref[pl.ds((2 * pair + 1) * LO, LO), :]
            got = dot(hot, jnp.concatenate([left, right], axis=1))
            total = jnp.where(high == 2 * pair, got[:, :FIN], total)
            total = jnp.where(high == 2 * pair + 1, got[:, FIN:], total)
        out_ref[pl.ds(PEERS * i, PEERS)] = total.astype(BF16).reshape(PEERS, BLK, FIN)
        return carry

    lax.fori_loop(0, N_DOM // PEERS, step, 0)


def gather_rows(rows, counts, features):
    return pl.pallas_call(
        gather_kernel,
        out_shape=jax.ShapeDtypeStruct((N_DOM, BLK, FIN), BF16),
        in_specs=[VM, SM, VM],
        out_specs=VM,
        compiler_params=PARAMS,
        cost_estimate=pl.CostEstimate(flops=4 * 10**9, bytes_accessed=2 * 10**6, transcendentals=0),
        name="gather_rows",
    )(rows, counts, features)


def hub_pick_kernel(hub_ref, place_ref, feat_ref, out_ref):
    for k in range(PAIRED_HUBS):
        block = hub_ref[place_ref[0] * PAIRED_HUBS + k]
        mine = lax.shift_right_logical(block, 4) == place_ref[1]

        @pl.when(mine)
        def _():
            out_ref[k] = feat_ref[block & (LOCAL - 1)]

        @pl.when(jnp.logical_not(mine))
        def _():
            out_ref[k] = jnp.zeros((BLK, FIN), BF16)


def pick_hubs(hubs, place, features):
    return pl.pallas_call(
        hub_pick_kernel,
        out_shape=jax.ShapeDtypeStruct((PAIRED_HUBS, BLK, FIN), BF16),
        in_specs=[SM, SM, VM],
        out_specs=VM,
        compiler_params=PARAMS,
        name="pick_hubs",
    )(hubs, place, features)


def forward_product(w_ref, xs):
    def product(one, two):
        left = jnp.concatenate([w_ref[one[0]], w_ref[two[0]]], axis=1)
        return dot(left, jnp.concatenate([xs[one[1]], xs[two[1]]], axis=0))

    return product


def forward_near_kernel(plan_ref, feat_ref, w_ref, acc_ref, xs):
    xs[pl.ds(0, LOCAL)] = feat_ref[...]
    xs[REMOTE + HUBS] = jnp.zeros((BLK, FIN), BF16)
    acc_ref[...] = jnp.zeros_like(acc_ref)
    run_class(plan_ref, 0, forward_product(w_ref, xs), acc_ref)


def forward_near(plan, features, weights):
    return pl.pallas_call(
        forward_near_kernel,
        out_shape=jax.ShapeDtypeStruct((LOCAL, BLK, FIN), F32),
        in_specs=[SM, VM, VM],
        out_specs=VM,
        scratch_shapes=[pltpu.VMEM((REMOTE + HUBS + 1, BLK, FIN), BF16)],
        compiler_params=TILE_PARAMS,
        cost_estimate=pl.CostEstimate(flops=10**9, bytes_accessed=14 * 10**6, transcendentals=0),
        name="forward_near",
    )(plan, features, weights)


def forward_far_kernel(
    plan_ref, rep_ref, near_ref, recv_ref, h0, h1, h2, h3, w_ref, own_ref, s1_ref, s2_ref, s3_ref, xs, acc
):
    rep = rep_ref[0]
    xs[pl.ds(0, REMOTE)] = recv_ref[...]
    for k, ref in enumerate((h0, h1, h2, h3)):
        first = lax.rem(rep + N_REP - k, N_REP) * PAIRED_HUBS
        xs[pl.ds(REMOTE + first, PAIRED_HUBS)] = ref[...]
    xs[REMOTE + HUBS] = jnp.zeros((BLK, FIN), BF16)
    acc[...] = near_ref[...]
    run_class(plan_ref, 1, forward_product(w_ref, xs), acc)
    own_ref[...] = acc[pl.ds(rep * QB, QB)]
    for k, ref in ((1, s1_ref), (2, s2_ref), (3, s3_ref)):
        ref[...] = acc[pl.ds(lax.rem(rep + k, N_REP) * QB, QB)].astype(BF16)


def forward_far(plan, rep, near, received, hubs, weights):
    quarter = (QB, BLK, FIN)
    return pl.pallas_call(
        forward_far_kernel,
        out_shape=[jax.ShapeDtypeStruct(quarter, F32)] + [jax.ShapeDtypeStruct(quarter, BF16)] * 3,
        in_specs=[SM, SM] + [VM] * 7,
        out_specs=[VM] * 4,
        scratch_shapes=[
            pltpu.VMEM((REMOTE + HUBS + 1, BLK, FIN), BF16),
            pltpu.VMEM((LOCAL, BLK, FIN), F32),
        ],
        compiler_params=TILE_PARAMS,
        cost_estimate=pl.CostEstimate(flops=4 * 10**9, bytes_accessed=14 * 10**6, transcendentals=0),
        name="forward_far",
    )(plan, rep, near, received, *hubs, weights)


def middle_kernel(
    rep_ref, own_ref, a_ref, b_ref, c_ref, w_ref, bias_ref, cot_ref, out_ref, y_ref, g0, g1, g2, g3, gw
):
    zx = (own_ref[...] + a_ref[...].astype(F32)) + (b_ref[...].astype(F32) + c_ref[...].astype(F32))
    zx = zx.reshape(QUARTER, FIN)
    weight = w_ref[...]
    zh, zl = halves(zx)
    pre = dot(zh, weight) + dot(zl, weight) + bias_ref[...]
    root = math.sqrt(2.0 / math.pi)
    square = pre * pre
    bent = jnp.tanh(root * (pre + 0.044715 * (square * pre)))
    cdf = 0.5 * (1.0 + bent)
    out_ref[...] = (pre * cdf).astype(BF16)
    slope = cdf + (0.5 * pre) * ((1.0 - bent * bent) * (root * (1.0 + (3 * 0.044715) * square)))
    pre_grad = (cot_ref[...].astype(F32) * slope).astype(BF16)
    yt = lax.dot_general(weight, pre_grad, (((1,), (1,)), ((), ())), preferred_element_type=F32)
    yt = yt.astype(BF16)
    for k in range(QB):
        y_ref[k] = yt[:, k * BLK : (k + 1) * BLK]
    th, tl = halves(zx.T)
    gw[...] = dot(th, pre_grad) + dot(tl, pre_grad)
    for k, ref in enumerate((g0, g1, g2, g3)):
        start = pl.multiple_of(lax.rem(rep_ref[0] + k, N_REP) * FQ, FQ)
        rows = gw[pl.ds(start, FQ), :]
        high, low = halves(jnp.concatenate([rows[:, :BLK], rows[:, BLK:]], axis=0))
        ref[pl.ds(0, GW_ROWS), :] = high
        ref[pl.ds(GW_ROWS, GW_ROWS), :] = low


def middle(rep, own, a, b, c, weight, bias, cotangent):
    whole = lambda shape: pl.BlockSpec(shape, lambda i, rep_ref: (0,) * len(shape))
    quarter = (QB, BLK, FIN)
    gw_shape = (2 * GW_ROWS, BLK)
    return pl.pallas_call(
        middle_kernel,
        grid_spec=pltpu.PrefetchScalarGridSpec(
            num_scalar_prefetch=1,
            grid=(1,),
            in_specs=[whole(quarter)] * 4
            + [
                whole((FIN, HID)),
                whole((1, HID)),
                pl.BlockSpec((QUARTER, HID), lambda i, rep_ref: (rep_ref[0], 0)),
            ],
            out_specs=[whole((QUARTER, HID)), whole((QB, FIN, BLK))] + [whole(gw_shape)] * 4,
            scratch_shapes=[pltpu.VMEM((FIN, HID), F32)],
        ),
        out_shape=[
            jax.ShapeDtypeStruct((QUARTER, HID), BF16),
            jax.ShapeDtypeStruct((QB, FIN, BLK), BF16),
        ]
        + [jax.ShapeDtypeStruct(gw_shape, BF16)] * 4,
        compiler_params=PARAMS,
        name="middle",
    )(rep, own, a, b, c, weight, bias, cotangent)


def backward_product(w_ref, ys):
    def product(one, two):
        left = jnp.concatenate([ys[one[1]], ys[two[1]]], axis=1)
        return dot(left, jnp.concatenate([w_ref[one[0]], w_ref[two[0]]], axis=0))

    return product


def load_ys(rep, refs, ys):
    for k, ref in enumerate(refs):
        ys[pl.ds(lax.rem(rep + N_REP - k, N_REP) * QB, QB)] = ref[...]
    ys[LOCAL] = jnp.zeros((FIN, BLK), BF16)


def backward_far_kernel(
    plan_ref, rep_ref, y0, y1, y2, y3, g0, g1, g2, g3, w_ref, msg_ref, f0, f1, f2, f3, ys, acc
):
    rep = rep_ref[0]
    load_ys(rep, (y0, y1, y2, y3), ys)
    acc[...] = jnp.zeros_like(acc)
    run_class(plan_ref, 0, backward_product(w_ref, ys), acc)
    for q in range(N_REP):
        msg_ref[q] = acc[pl.ds(0, REMOTE), pl.ds(q * FQ, FQ), :].astype(BF16)
    for k, (ref, gw) in enumerate(((f0, g0), (f1, g1), (f2, g2), (f3, g3))):
        start = pl.multiple_of(lax.rem(rep + k, N_REP) * FQ, FQ)
        rows = acc[pl.ds(REMOTE, HUBS), pl.ds(start, FQ), :].reshape(FOLD, BLK)
        ref[pl.ds(0, FOLD), :] = rows.astype(BF16)
        ref[pl.ds(FOLD, 2 * GW_ROWS), :] = gw[...]


def backward_far(plan, rep, ys, gws, weights):
    fold = (FOLD + 2 * GW_ROWS, BLK)
    return pl.pallas_call(
        backward_far_kernel,
        out_shape=[jax.ShapeDtypeStruct((N_REP, N_DOM, FQ, BLK), BF16)]
        + [jax.ShapeDtypeStruct(fold, BF16)] * 4,
        in_specs=[SM, SM] + [VM] * 9,
        out_specs=[VM] * 5,
        scratch_shapes=[
            pltpu.VMEM((LOCAL + 1, FIN, BLK), BF16),
            pltpu.VMEM((REMOTE + HUBS, FIN, BLK), F32),
        ],
        compiler_params=TILE_PARAMS,
        cost_estimate=pl.CostEstimate(flops=4 * 10**9, bytes_accessed=14 * 10**6, transcendentals=0),
        name="backward_far",
    )(plan, rep, *ys, *gws, weights)


def backward_near_kernel(plan_ref, rep_ref, y0, y1, y2, y3, w_ref, own_ref, s1, s2, s3, ys, acc):
    rep = rep_ref[0]
    load_ys(rep, (y0, y1, y2, y3), ys)
    acc[...] = jnp.zeros_like(acc)
    run_class(plan_ref, 1, backward_product(w_ref, ys), acc)

    def rows_of(k):
        start = pl.multiple_of(lax.rem(rep + k, N_REP) * FQ, FQ)
        return acc[:, pl.ds(start, FQ), :]

    own_ref[...] = rows_of(0)
    for k, ref in ((1, s1), (2, s2), (3, s3)):
        ref[...] = rows_of(k).astype(BF16)


def backward_near(plan, rep, ys, weights):
    part = (LOCAL, FQ, BLK)
    return pl.pallas_call(
        backward_near_kernel,
        out_shape=[jax.ShapeDtypeStruct(part, F32)] + [jax.ShapeDtypeStruct(part, BF16)] * 3,
        in_specs=[SM, SM] + [VM] * 5,
        out_specs=[VM] * 4,
        scratch_shapes=[
            pltpu.VMEM((LOCAL + 1, FIN, BLK), BF16),
            pltpu.VMEM((LOCAL, FIN, BLK), F32),
        ],
        compiler_params=TILE_PARAMS,
        cost_estimate=pl.CostEstimate(flops=10**9, bytes_accessed=14 * 10**6, transcendentals=0),
        name="backward_near",
    )(plan, rep, *ys, weights)


SCATTER_PEERS = 8


def fold_kernel(*refs):
    out_ref = refs[-1]
    total = refs[0][...].astype(F32)
    for ref in refs[1:-1]:
        total = total + ref[...].astype(F32)
    out_ref[pl.ds(0, FOLD), :] = total[:FOLD].astype(BF16)
    high, low = halves(total[FOLD : FOLD + GW_ROWS] + total[FOLD + GW_ROWS :])
    out_ref[pl.ds(FOLD, GW_ROWS), :] = high
    out_ref[pl.ds(FOLD + GW_ROWS, GW_ROWS), :] = low


def fold(parts):
    return pl.pallas_call(
        fold_kernel,
        out_shape=jax.ShapeDtypeStruct(parts[0].shape, BF16),
        in_specs=[VM] * len(parts),
        out_specs=VM,
        compiler_params=PARAMS,
        name="fold",
    )(*parts)


def scatter_kernel(
    place_ref, hub_ref, count_ref, rows_ref, recv_ref, own_ref, a_ref, b_ref, c_ref, f0, f1, out_ref, acc, part
):
    chunks = ROWS // LO
    slot = lax.broadcasted_iota(jnp.int32, (1, BLK), 1)
    acc[...] = jnp.zeros_like(acc)

    def step(i, carry):
        hots, sides = [], []
        for j in range(SCATTER_PEERS):
            p = SCATTER_PEERS * i + j
            row = jnp.where(slot < count_ref[0, p], rows_ref[pl.ds(p, 1), :], -1)
            hots.append(low_onehot(column(row)))
            total = recv_ref[p].astype(F32)
            for r in range(1, N_REP):
                total = total + recv_ref[r * N_DOM + p].astype(F32)
            high = lax.shift_right_arithmetic(row, 8)
            pieces = [halves(jnp.where(high == c, total, 0.0)) for c in range(chunks)]
            sides.append(jnp.concatenate([h for h, _ in pieces] + [l for _, l in pieces], axis=0))
        acc[...] += dot(jnp.concatenate(sides, axis=1), jnp.concatenate(hots, axis=0))
        return carry

    lax.fori_loop(0, N_DOM // SCATTER_PEERS, step, 0)
    for b in range(LOCAL):
        c, side = b // 2, b % 2
        lanes = pl.ds(side * BLK, BLK)
        here = acc[pl.ds(c * FQ, FQ), lanes] + acc[pl.ds((chunks + c) * FQ, FQ), lanes]
        near = own_ref[b] + a_ref[b].astype(F32) + b_ref[b].astype(F32) + c_ref[b].astype(F32)
        part[b] = here + near
    for h in range(HUBS):
        block = hub_ref[h]

        @pl.when(lax.shift_right_logical(block, 4) == place_ref[1])
        def _():
            rows = pl.ds(h * FQ, FQ)
            part[block & (LOCAL - 1)] += f0[rows, :].astype(F32) + f1[rows, :].astype(F32)

    out_ref[pl.ds(0, LOCAL * FQ), :] = part[...].reshape(LOCAL * FQ, BLK).astype(BF16)
    total = f0[pl.ds(FOLD, 2 * GW_ROWS), :].astype(F32) + f1[pl.ds(FOLD, 2 * GW_ROWS), :].astype(F32)
    high, low = halves(total[:GW_ROWS] + total[GW_ROWS:])
    out_ref[pl.ds(LOCAL * FQ, GW_ROWS), :] = high
    out_ref[pl.ds(LOCAL * FQ + GW_ROWS, GW_ROWS), :] = low


def scatter_rows(place, hubs, counts, rows, received, own, a, b, c, f0, f1):
    return pl.pallas_call(
        scatter_kernel,
        out_shape=jax.ShapeDtypeStruct((LOCAL * FQ + 2 * GW_ROWS, BLK), BF16),
        in_specs=[SM] * 3 + [VM] * 8,
        out_specs=VM,
        scratch_shapes=[pltpu.VMEM((2 * FIN * 2, LO), F32), pltpu.VMEM((LOCAL, FQ, BLK), F32)],
        compiler_params=PARAMS,
        cost_estimate=pl.CostEstimate(flops=4 * 10**9, bytes_accessed=4 * 10**6, transcendentals=0),
        name="scatter_rows",
    )(place, hubs, counts, rows, received, own, a, b, c, f0, f1)


def final_kernel(rep_ref, m0, m1, m2, m3, gx_ref, gw_ref, blocks, *, scale):
    rep = rep_ref[0]
    for k, ref in enumerate((m0, m1, m2, m3)):
        q = lax.rem(rep + N_REP - k, N_REP)
        start = pl.multiple_of(q * FQ, FQ)
        rows = ref[pl.ds(0, LOCAL * FQ), :].astype(F32)
        blocks[:, pl.ds(start, FQ), :] = rows.reshape(LOCAL, FQ, BLK)
        high = ref[pl.ds(LOCAL * FQ, GW_ROWS), :].astype(F32)
        gw = (high + ref[pl.ds(LOCAL * FQ + GW_ROWS, GW_ROWS), :].astype(F32)) * scale
        gw_ref[pl.ds(start, FQ), :] = jnp.concatenate([gw[:FQ], gw[FQ:]], axis=1)
    for b in range(LOCAL):
        gx_ref[pl.ds(b * BLK, BLK), :] = blocks[b].T


def finish(rep, parts, scale):
    return pl.pallas_call(
        functools.partial(final_kernel, scale=scale),
        out_shape=[
            jax.ShapeDtypeStruct((ROWS, FIN), F32),
            jax.ShapeDtypeStruct((FIN, HID), F32),
        ],
        in_specs=[SM] + [VM] * 4,
        out_specs=[VM, VM],
        scratch_shapes=[pltpu.VMEM((LOCAL, FIN, BLK), F32)],
        compiler_params=PARAMS,
        name="finish",
    )(rep, *parts)


def place_kernel(rep_ref, o0, o1, o2, o3, out_ref):
    for k, ref in enumerate((o0, o1, o2, o3)):
        start = pl.multiple_of(lax.rem(rep_ref[0] + N_REP - k, N_REP) * QUARTER, QUARTER)
        out_ref[pl.ds(start, QUARTER), :] = ref[...]


def place_output(rep, parts):
    return pl.pallas_call(
        place_kernel,
        out_shape=jax.ShapeDtypeStruct((ROWS, HID), BF16),
        in_specs=[SM] + [VM] * 4,
        out_specs=VM,
        compiler_params=PARAMS,
        name="place_output",
    )(rep, *parts)


def turn(value, k):
    return lax.ppermute(value, "rep", [(i, (i + k) % N_REP) for i in range(N_REP)])


def around(value):
    return [value] + [turn(value, k) for k in (1, 2, 3)]


def chips(x, z, core):
    pairs = []
    for i in range(N_DOM):
        to_x, to_z, to_core = (i // 8 + x) % 4, (i // 2 + z) % 4, (i + core) % 2
        pairs.append((i, (to_x * 4 + to_z) * 2 + to_core))
    return pairs


def over_chips(value, axis):
    if axis == "x":
        return [value] + [lax.ppermute(value, "dom", chips(k, 0, 0)) for k in (1, 2, 3)]
    return [value] + [lax.ppermute(value, "dom", chips(0, k, 0)) for k in (1, 2, 3)]


def over_cores(value):
    return [value, lax.ppermute(value, "dom", chips(0, 0, 1))]


def total(parts):
    return functools.reduce(lambda a, b: a + b, parts)


def swap(value, axes):
    return lax.all_to_all(value, axes, split_axis=0, concat_axis=0, tiled=True)


def shards(
    features,
    proj_weight,
    bias,
    cotangent,
    send_rows,
    send_count,
    hub_blocks,
    tile_dst,
    tile_src,
    tile_weight,
):
    rep = lax.axis_index("rep").astype(jnp.int32)
    dom = lax.axis_index("dom").astype(jnp.int32)
    place = jnp.stack([rep, dom])
    blocks = features.reshape(LOCAL, BLK, FIN)
    weights = tile_weight[0, 0]
    rows = send_rows[0]

    listed = gather_rows(rows, send_count, features)
    received = swap(listed, "dom")
    hub = pick_hubs(hub_blocks, place, blocks)
    hub = total(over_cores(hub))
    hub = total(over_chips(hub, "x"))
    hub = total(over_chips(hub, "z"))
    hubs = around(hub)
    fwd, bwd = order_tiles(
        tile_dst[0, 0].reshape(TILES // BLK, BLK), tile_src[0, 0].reshape(TILES // BLK, BLK)
    )
    near = forward_near(fwd, blocks, weights)
    own, s1, s2, s3 = forward_far(fwd, place, near, received, hubs, weights)
    a, b, c = turn(s1, 1), turn(s2, 2), turn(s3, 3)
    out_part, y_part, *gws = middle(
        place, own, a, b, c, proj_weight, bias.reshape(1, HID), cotangent
    )
    ys = around(y_part)
    out_part, ys = lax.optimization_barrier((out_part, ys))
    outs = around(out_part)
    message, *folds = backward_far(bwd, place, ys, gws, weights)
    returned = swap(message.reshape(N_REP * N_DOM, FQ, BLK), ("rep", "dom"))
    shared = fold([folds[0]] + [turn(folds[k], k) for k in (1, 2, 3)])
    shared = fold(over_chips(shared, "z"))
    shared = fold(over_chips(shared, "x"))
    f0, f1 = over_cores(shared)
    own, s1, s2, s3 = backward_near(bwd, place, ys, weights)
    a, b, c = turn(s1, 1), turn(s2, 2), turn(s3, 3)
    output = place_output(place, outs)
    returned, output = lax.optimization_barrier((returned, output))

    part = scatter_rows(place, hub_blocks, send_count, rows, returned, own, a, b, c, f0, f1)
    grad_x, grad_w = finish(place, around(part), 1.0 / math.sqrt(ROWS * N_DOM))
    return (output, grad_x, grad_w)


def solution(mesh):
    in_specs = (
        P("dom", None),
        P(),
        P(),
        P("dom", None),
        P("dom", None, None),
        P("dom", None),
        P(),
        P("rep", "dom", None),
        P("rep", "dom", None),
        P("rep", "dom", None, None, None),
    )
    out_specs = (P("dom", None), P("dom", None), P())
    return jax.shard_map(shards, mesh=mesh, in_specs=in_specs, out_specs=out_specs, check_vma=False)
```

```python
import functools
import math

import jax
import jax.numpy as jnp
from jax import lax
from jax.experimental import pallas as pl
from jax.experimental.pallas import tpu as pltpu
from jax.sharding import PartitionSpec as P

F32 = jnp.float32
BF16 = jnp.bfloat16
BLK = 128
N_REP = 4
N_DOM = 32
FIN = 128
HID = 256
ROWS = 2048
LOCAL = ROWS // BLK
HUBS = 8
BLOCKS = LOCAL + N_DOM + HUBS
TILES = 384
REMOTE = N_DOM
CHUNK = 32
FWD_SLOTS = 640
BWD_SLOTS = 512
QUARTER = ROWS // N_REP
QB = LOCAL // N_REP
FQ = FIN // N_REP
MSG = FQ + 16
HUB_ROWS = HUBS * BLK // N_DOM
LO = 256
VMEM_LIMIT = 24 * 1024 * 1024

VM = pl.BlockSpec(memory_space=pltpu.VMEM)
SM = pl.BlockSpec(memory_space=pltpu.SMEM)
FAR = pl.BlockSpec(memory_space=pltpu.HBM)
PARAMS = pltpu.CompilerParams(vmem_limit_bytes=VMEM_LIMIT)
TILE_PARAMS = PARAMS


def in_hbm(x):
    return pltpu.with_memory_space_constraint(x, pltpu.HBM)


def dot(a, b):
    return jnp.dot(a, b, preferred_element_type=F32)


def halves(x):
    high = x.astype(BF16)
    return high, (x - high.astype(F32)).astype(BF16)


def column(row):
    return jnp.broadcast_to(row, (BLK, BLK)).T


def low_onehot(col):
    low = jnp.where(col < 0, -1, col & (LO - 1))
    lane = lax.broadcasted_iota(jnp.int32, (BLK, BLK), 1)
    return jnp.concatenate(
        [jnp.where(low == lane + k * BLK, 1.0, 0.0) for k in range(LO // BLK)], axis=1
    ).astype(BF16)


def sort_tiles(bucket, operand, empty, edges, out_of, slots):
    sub = lax.broadcasted_iota(jnp.int32, (BLK, BLK), 0)
    lane = lax.broadcasted_iota(jnp.int32, (BLK, BLK), 1)
    line = lane[:1]
    parts = len(bucket)
    cols = [column(b) for b in bucket]
    hots = [jnp.where(c == lane, 1.0, 0.0) for c in cols]
    counts = sum(jnp.sum(h, axis=0, keepdims=True) for h in hots).astype(jnp.int32)
    padded = (counts + 1) & -2
    before = jnp.where(sub < lane, column(padded).astype(F32), 0.0)
    starts = jnp.sum(before, axis=0, keepdims=True).astype(jnp.int32)
    first = jnp.zeros((1, BLK), jnp.int32)
    low = 0
    for n, high in enumerate(edges):
        inside = (line >= low) & (line < high)
        size = jnp.sum(jnp.where(inside, padded, 0).astype(F32), axis=1, keepdims=True).astype(jnp.int32)
        gap = ((size + CHUNK - 1) & -CHUNK) - size
        starts = starts + jnp.where(line >= high, gap, 0)
        total = (size + CHUNK - 1) // CHUNK
        first = first + jnp.where(line > n, total, 0)
        low = high
    begin, end = column(starts), column(starts + padded)
    places = []
    for i in range(parts):
        rank = jnp.sum(jnp.where(hots[i] > 0.0, starts.astype(F32), 0.0), axis=1, keepdims=True)
        for j in range(i + 1):
            same = jnp.broadcast_to(bucket[j], (BLK, BLK)) == cols[i]
            if j == i:
                same = same & (lane < sub)
            rank = rank + jnp.sum(jnp.where(same, 1.0, 0.0), axis=1, keepdims=True)
        places.append(jnp.broadcast_to(rank.astype(jnp.int32), (BLK, BLK)))
    shifted = [column(o - empty).astype(F32) for o in operand]
    tiles, blocks, outs = [], [], []
    for s in range(slots // BLK):
        here = lane + s * BLK
        tile = jnp.zeros((1, BLK), F32)
        block = jnp.zeros((1, BLK), F32)
        for i in range(parts):
            hit = places[i] == here
            tile = tile + jnp.sum(jnp.where(hit, (sub + i * BLK).astype(F32), 0.0), axis=0, keepdims=True)
            block = block + jnp.sum(jnp.where(hit, shifted[i], 0.0), axis=0, keepdims=True)
        inside = (begin <= here) & (here < end)
        out = jnp.sum(jnp.where(inside, out_of(sub).astype(F32), 0.0), axis=0, keepdims=True)
        tiles.append(tile.astype(jnp.int32))
        blocks.append(block.astype(jnp.int32) + empty)
        outs.append(out.astype(jnp.int32))
    return tiles, blocks, outs, first


def order_kernel(dst_ref, src_ref, fwd_ref, bwd_ref):
    parts = TILES // BLK
    dst = [dst_ref[pl.ds(i, 1), :] for i in range(parts)]
    src = [src_ref[pl.ds(i, 1), :] for i in range(parts)]
    hub = LOCAL + REMOTE
    bucket = [d + jnp.where(s < LOCAL, 0, jnp.where(s < hub, LOCAL, 2 * LOCAL)) for d, s in zip(dst, src)]
    operand = [s - jnp.where(s < LOCAL, 0, jnp.where(s < hub, LOCAL, hub)) for s in src]
    edges = (LOCAL, 2 * LOCAL, 3 * LOCAL)
    found = sort_tiles(bucket, operand, REMOTE, edges, lambda b: b & (LOCAL - 1), FWD_SLOTS)
    for n, rows in enumerate(found[:3]):
        for s, row in enumerate(rows):
            fwd_ref[n, pl.ds(s, 1), :] = row
    fwd_ref[3, pl.ds(0, 1), :] = found[3]
    far = REMOTE + HUBS
    bucket = [jnp.where(s < LOCAL, s + far, s - LOCAL) for s in src]
    found = sort_tiles(
        bucket, dst, LOCAL, (far, far + LOCAL), lambda b: jnp.where(b < far, b, b - far), BWD_SLOTS
    )
    for n, rows in enumerate(found[:3]):
        for s, row in enumerate(rows):
            bwd_ref[n, pl.ds(s, 1), :] = row
    bwd_ref[3, pl.ds(0, 1), :] = found[3]


def order_tiles(dst, src):
    return pl.pallas_call(
        order_kernel,
        out_shape=[
            jax.ShapeDtypeStruct((4, FWD_SLOTS // BLK, BLK), jnp.int32),
            jax.ShapeDtypeStruct((4, BWD_SLOTS // BLK, BLK), jnp.int32),
        ],
        in_specs=[VM, VM],
        out_specs=[VM, VM],
        compiler_params=PARAMS,
        name="order_tiles",
    )(dst, src)


AHEAD = 3


def keep(tiles, buckets):
    chunks = -(-(tiles + buckets) // CHUNK)
    return [pltpu.VMEM((chunks * CHUNK, BLK, BLK), BF16), pltpu.SemaphoreType.DMA((chunks,))]


def extent(plan_ref, number):
    begin = plan_ref[3, 0, number]
    return begin, plan_ref[3, 0, number + 1] - begin


def where(i):
    return i // (BLK // CHUNK), lax.rem(i, BLK // CHUNK) * CHUNK


def fetch(plan_ref, number, c, w_ref, held, sems):
    row, col = where(extent(plan_ref, number)[0] + c)
    for k in range(CHUNK):
        tile = plan_ref[0, row, col + k]
        pltpu.make_async_copy(w_ref.at[tile], held.at[c * CHUNK + k], sems.at[c]).start()


def fetch_first(plan_ref, number, w_ref, held, sems):
    def first(c, carry):
        fetch(plan_ref, number, c, w_ref, held, sems)
        return carry

    lax.fori_loop(0, jnp.minimum(extent(plan_ref, number)[1], AHEAD), first, 0)


def run_class(plan_ref, number, w_ref, held, sems, product, acc):
    begin, count = extent(plan_ref, number)

    def chunk(c, carry):
        row, col = where(begin + c)
        if held is not None:
            slots = held.at[pl.ds(c * CHUNK, CHUNK)]
            pltpu.make_async_copy(w_ref.at[pl.ds(0, CHUNK)], slots, sems.at[c]).wait()

            @pl.when(c + AHEAD < count)
            def _():
                fetch(plan_ref, number, c + AHEAD, w_ref, held, sems)

        found = []
        for k in range(0, CHUNK, 2):
            pair = []
            for j in (k, k + 1):
                tile = w_ref[plan_ref[0, row, col + j]] if held is None else held[c * CHUNK + j]
                pair.append((tile, plan_ref[1, row, col + j]))
            one, two = pair
            found.append((plan_ref[2, row, col + k], product(one, two)))
        for d, value in found:
            acc[d] += value
        return carry

    lax.fori_loop(0, count, chunk, 0)


PEERS = 4


def gather_kernel(rows_hbm, count_ref, hub_ref, feat_hbm, out_ref, rows_ref, feat_ref, sems):
    loads = [
        pltpu.make_async_copy(feat_hbm, feat_ref, sems.at[0]),
        pltpu.make_async_copy(rows_hbm, rows_ref, sems.at[1]),
    ]
    for load in loads:
        load.start()
    for load in loads:
        load.wait()
    slot = lax.broadcasted_iota(jnp.int32, (1, BLK), 1)

    def step(i, carry):
        cols = []
        for j in range(PEERS):
            p = PEERS * i + j
            row = jnp.where(slot < count_ref[0, p], rows_ref[pl.ds(p, 1), :], -1)
            cols.append(column(row))
        hot = jnp.concatenate([low_onehot(c) for c in cols], axis=0)
        high = lax.shift_right_arithmetic(jnp.concatenate(cols, axis=0), 8)
        total = jnp.zeros((PEERS * BLK, FIN), F32)
        for pair in range(ROWS // LO // 2):
            left = feat_ref[pl.ds(2 * pair * LO, LO), :]
            right = feat_ref[pl.ds((2 * pair + 1) * LO, LO), :]
            got = dot(hot, jnp.concatenate([left, right], axis=1))
            total = jnp.where(high == 2 * pair, got[:, :FIN], total)
            total = jnp.where(high == 2 * pair + 1, got[:, FIN:], total)
        out_ref[pl.ds(PEERS * i, PEERS), pl.ds(0, BLK), :] = total.astype(BF16).reshape(PEERS, BLK, FIN)
        return carry

    lax.fori_loop(0, N_DOM // PEERS, step, 0)
    per_hub = BLK // HUB_ROWS
    for p in range(N_DOM):
        first = (hub_ref[p // per_hub] & (LOCAL - 1)) * BLK + (p % per_hub) * HUB_ROWS
        first = pl.multiple_of(first, HUB_ROWS)
        out_ref[p, pl.ds(BLK, HUB_ROWS), :] = feat_ref[pl.ds(first, HUB_ROWS), :]


def gather_rows(rows, counts, hubs, features):
    return pl.pallas_call(
        gather_kernel,
        out_shape=jax.ShapeDtypeStruct((N_DOM, BLK + HUB_ROWS, FIN), BF16),
        in_specs=[FAR, SM, SM, FAR],
        out_specs=VM,
        scratch_shapes=[
            pltpu.VMEM((N_DOM, BLK), jnp.int32),
            pltpu.VMEM((ROWS, FIN), BF16),
            pltpu.SemaphoreType.DMA((2,)),
        ],
        compiler_params=PARAMS,
        cost_estimate=pl.CostEstimate(flops=4 * 10**9, bytes_accessed=2 * 10**6, transcendentals=0),
        name="gather_rows",
    )(in_hbm(rows), counts, hubs, in_hbm(features))


def piece_kernel(place_ref, hub_ref, recv_ref, out_ref):
    owner = lax.shift_right_logical(hub_ref[place_ref[1] // (BLK // HUB_ROWS)], 4)
    piece = recv_ref[owner, pl.ds(BLK, HUB_ROWS), :]
    for p in range(N_DOM):
        out_ref[p] = piece


def hub_piece(place, hubs, received):
    return pl.pallas_call(
        piece_kernel,
        out_shape=jax.ShapeDtypeStruct((N_DOM, HUB_ROWS, FIN), BF16),
        in_specs=[SM, SM, VM],
        out_specs=VM,
        compiler_params=PARAMS,
        name="hub_piece",
    )(place, hubs, received)


def forward_product(xs):
    def product(one, two):
        left = jnp.concatenate([one[0], two[0]], axis=1)
        return dot(left, jnp.concatenate([xs[one[1]], xs[two[1]]], axis=0))

    return product


def forward_near_kernel(plan_ref, feat_ref, w_ref, acc_ref, xs, held, sems):
    fetch_first(plan_ref, 0, w_ref, held, sems)
    xs[pl.ds(0, LOCAL)] = feat_ref[...]
    xs[REMOTE] = jnp.zeros((BLK, FIN), BF16)
    acc_ref[...] = jnp.zeros_like(acc_ref)
    run_class(plan_ref, 0, w_ref, held, sems, forward_product(xs), acc_ref)


def forward_remote_kernel(plan_ref, near_ref, recv_ref, w_ref, acc_ref, xs, held, sems):
    fetch_first(plan_ref, 1, w_ref, held, sems)
    xs[pl.ds(0, REMOTE)] = recv_ref[:, pl.ds(0, BLK), :]
    xs[REMOTE] = jnp.zeros((BLK, FIN), BF16)
    acc_ref[...] = near_ref[...]
    run_class(plan_ref, 1, w_ref, held, sems, forward_product(xs), acc_ref)


def forward_hub_kernel(plan_ref, place_ref, far_ref, hub_ref, w_ref, own_ref, s1, s2, s3, xs, acc, held, sems):
    fetch_first(plan_ref, 2, w_ref, held, sems)
    xs[pl.ds(0, HUBS)] = hub_ref[...]
    xs[REMOTE] = jnp.zeros((BLK, FIN), BF16)
    acc[...] = far_ref[...]
    run_class(plan_ref, 2, w_ref, held, sems, forward_product(xs), acc)
    rep = place_ref[0]
    own_ref[...] = acc[pl.ds(rep * QB, QB)]
    for k, ref in ((1, s1), (2, s2), (3, s3)):
        ref[...] = acc[pl.ds(lax.rem(rep + k, N_REP) * QB, QB)].astype(BF16)


FORWARD_XS = pltpu.VMEM((REMOTE + 1, BLK, FIN), BF16)


def forward_near(plan, features, weights):
    return pl.pallas_call(
        forward_near_kernel,
        out_shape=jax.ShapeDtypeStruct((LOCAL, BLK, FIN), F32),
        in_specs=[SM, VM, FAR],
        out_specs=VM,
        scratch_shapes=[FORWARD_XS] + keep(LOCAL * LOCAL, LOCAL),
        compiler_params=TILE_PARAMS,
        cost_estimate=pl.CostEstimate(flops=10**9, bytes_accessed=4 * 10**6, transcendentals=0),
        name="forward_near",
    )(plan, features, weights)


def forward_remote(plan, near, received, weights):
    return pl.pallas_call(
        forward_remote_kernel,
        out_shape=jax.ShapeDtypeStruct((LOCAL, BLK, FIN), F32),
        in_specs=[SM, VM, VM, FAR],
        out_specs=VM,
        scratch_shapes=[FORWARD_XS] + keep(TILES, LOCAL),
        compiler_params=TILE_PARAMS,
        cost_estimate=pl.CostEstimate(flops=4 * 10**9, bytes_accessed=9 * 10**6, transcendentals=0),
        name="forward_remote",
    )(plan, near, received, weights)


def forward_hub(plan, place, far, hubs, weights):
    quarter = (QB, BLK, FIN)
    return pl.pallas_call(
        forward_hub_kernel,
        out_shape=[jax.ShapeDtypeStruct(quarter, F32)] + [jax.ShapeDtypeStruct(quarter, BF16)] * 3,
        in_specs=[SM, SM, VM, VM, FAR],
        out_specs=[VM] * 4,
        scratch_shapes=[FORWARD_XS, pltpu.VMEM((LOCAL, BLK, FIN), F32)] + keep(LOCAL * HUBS, LOCAL),
        compiler_params=TILE_PARAMS,
        cost_estimate=pl.CostEstimate(flops=10**9, bytes_accessed=3 * 10**6, transcendentals=0),
        name="forward_hub",
    )(plan, place, far, hubs, weights)


def middle_kernel(own_ref, a_ref, b_ref, c_ref, w_ref, bias_ref, cot_ref, out_ref, y_ref, gw_ref):
    zx = (own_ref[...] + a_ref[...].astype(F32)) + (b_ref[...].astype(F32) + c_ref[...].astype(F32))
    zx = zx.reshape(QUARTER, FIN)
    weight = w_ref[...]
    zh, zl = halves(zx)
    pre = dot(zh, weight) + dot(zl, weight) + bias_ref[...]
    root = math.sqrt(2.0 / math.pi)
    square = pre * pre
    bent = jnp.tanh(root * (pre + 0.044715 * (square * pre)))
    cdf = 0.5 * (1.0 + bent)
    out_ref[...] = (pre * cdf).astype(BF16)
    slope = cdf + (0.5 * pre) * ((1.0 - bent * bent) * (root * (1.0 + (3 * 0.044715) * square)))
    pre_grad = (cot_ref[...].astype(F32) * slope).astype(BF16)
    yt = lax.dot_general(weight, pre_grad, (((1,), (1,)), ((), ())), preferred_element_type=F32)
    yt = yt.astype(BF16)
    for k in range(QB):
        y_ref[k] = yt[:, k * BLK : (k + 1) * BLK]
    th, tl = halves(zx.T)
    gw = dot(th, pre_grad) + dot(tl, pre_grad)
    for part, piece in enumerate(halves(gw)):
        for c in range(16):
            g, side = c // 2, c % 2
            gw_ref[part * 16 + c] = piece[g * 16 : (g + 1) * 16, side * BLK : (side + 1) * BLK]


def middle(rep, own, a, b, c, weight, bias, cotangent):
    whole = lambda shape: pl.BlockSpec(shape, lambda i, rep_ref: (0,) * len(shape))
    quarter = (QB, BLK, FIN)
    return pl.pallas_call(
        lambda rep_ref, *refs: middle_kernel(*refs),
        grid_spec=pltpu.PrefetchScalarGridSpec(
            num_scalar_prefetch=1,
            grid=(1,),
            in_specs=[whole(quarter)] * 4
            + [
                whole((FIN, HID)),
                whole((1, HID)),
                pl.BlockSpec((QUARTER, HID), lambda i, rep_ref: (rep_ref[0], 0)),
            ],
            out_specs=[whole((QUARTER, HID)), whole((QB, FIN, BLK)), whole((32, 16, BLK))],
        ),
        out_shape=[
            jax.ShapeDtypeStruct((QUARTER, HID), BF16),
            jax.ShapeDtypeStruct((QB, FIN, BLK), BF16),
            jax.ShapeDtypeStruct((32, 16, BLK), BF16),
        ],
        compiler_params=PARAMS,
        cost_estimate=pl.CostEstimate(flops=2 * 10**10, bytes_accessed=2 * 10**6, transcendentals=0),
        name="middle",
    )(rep, own, a, b, c, weight, bias, cotangent)


def hold_kernel(w_ref, after_ref, held_ref, sem):
    del after_ref
    copy = pltpu.make_async_copy(w_ref, held_ref, sem)
    copy.start()
    copy.wait()


def hold_tiles(weights, after):
    return pl.pallas_call(
        hold_kernel,
        out_shape=pltpu.VMEM((TILES, BLK, BLK), BF16),
        in_specs=[FAR, pl.BlockSpec(memory_space=pl.ANY)],
        out_specs=VM,
        scratch_shapes=[pltpu.SemaphoreType.DMA],
        compiler_params=PARAMS,
        cost_estimate=pl.CostEstimate(flops=0, bytes_accessed=13 * 10**6, transcendentals=0),
        name="hold_tiles",
    )(weights, after)


def backward_product(ys):
    def product(one, two):
        left = jnp.concatenate([ys[one[1]], ys[two[1]]], axis=1)
        return dot(left, jnp.concatenate([one[0], two[0]], axis=0))

    return product


def load_ys(rep, refs, ys):
    for k, ref in enumerate(refs):
        ys[pl.ds(lax.rem(rep + N_REP - k, N_REP) * QB, QB)] = ref[...]
    ys[LOCAL] = jnp.zeros((FIN, BLK), BF16)


def backward_far_kernel(
    plan_ref, rep_ref, y0, y1, y2, y3, gw_ref, w_ref, msg_ref, ys, acc
):
    load_ys(rep_ref[0], (y0, y1, y2, y3), ys)
    acc[...] = jnp.zeros_like(acc)
    run_class(plan_ref, 0, w_ref, None, None, backward_product(ys), acc)
    for q in range(N_REP):
        msg_ref[q, :, pl.ds(0, FQ), :] = acc[pl.ds(0, REMOTE), pl.ds(q * FQ, FQ), :].astype(BF16)
        for m in range(16):
            piece = acc[REMOTE + m // 2, pl.ds(q * FQ + (m % 2) * 16, 16), :]
            msg_ref[q, 2 * m, pl.ds(FQ, 16), :] = piece.astype(BF16)
            if m < 8:
                msg_ref[q, 2 * m + 1, pl.ds(FQ, 16), :] = gw_ref[q * 8 + m]
            else:
                msg_ref[q, 2 * m + 1, pl.ds(FQ, 16), :] = jnp.zeros((16, BLK), BF16)


def backward_far(plan, rep, ys, gw, weights):
    return pl.pallas_call(
        backward_far_kernel,
        out_shape=jax.ShapeDtypeStruct((N_REP, N_DOM, MSG, BLK), BF16),
        in_specs=[SM, SM] + [VM] * 6,
        out_specs=VM,
        scratch_shapes=[
            pltpu.VMEM((LOCAL + 1, FIN, BLK), BF16),
            pltpu.VMEM((REMOTE + HUBS, FIN, BLK), F32),
        ],
        compiler_params=TILE_PARAMS,
        cost_estimate=pl.CostEstimate(flops=4 * 10**9, bytes_accessed=14 * 10**6, transcendentals=0),
        name="backward_far",
    )(plan, rep, *ys, gw, weights)


def backward_near_kernel(
    plan_ref, rep_ref, y0, y1, y2, y3, w_ref, own_ref, s1, s2, s3, ys, acc, held, sems
):
    fetch_first(plan_ref, 1, w_ref, held, sems)
    rep = rep_ref[0]
    load_ys(rep, (y0, y1, y2, y3), ys)
    acc[...] = jnp.zeros_like(acc)
    run_class(plan_ref, 1, w_ref, held, sems, backward_product(ys), acc)

    def rows_of(k):
        start = pl.multiple_of(lax.rem(rep + k, N_REP) * FQ, FQ)
        return acc[:, pl.ds(start, FQ), :]

    own_ref[...] = rows_of(0)
    for k, ref in ((1, s1), (2, s2), (3, s3)):
        ref[...] = rows_of(k).astype(BF16)


def backward_near(plan, rep, ys, weights):
    part = (LOCAL, FQ, BLK)
    return pl.pallas_call(
        backward_near_kernel,
        out_shape=[jax.ShapeDtypeStruct(part, F32)] + [jax.ShapeDtypeStruct(part, BF16)] * 3,
        in_specs=[SM, SM] + [VM] * 4 + [FAR],
        out_specs=[VM] * 4,
        scratch_shapes=[
            pltpu.VMEM((LOCAL + 1, FIN, BLK), BF16),
            pltpu.VMEM((LOCAL, FIN, BLK), F32),
        ]
        + keep(LOCAL * LOCAL, LOCAL),
        compiler_params=TILE_PARAMS,
        cost_estimate=pl.CostEstimate(flops=10**9, bytes_accessed=14 * 10**6, transcendentals=0),
        name="backward_near",
    )(plan, rep, *ys, weights)


SCATTER_PEERS = 8


def scatter_kernel(count_ref, rows_ref, recv_ref, own_ref, a_ref, b_ref, c_ref, out_ref, acc):
    chunks = ROWS // LO
    slot = lax.broadcasted_iota(jnp.int32, (1, BLK), 1)
    acc[...] = jnp.zeros_like(acc)

    def step(i, carry):
        hots, sides = [], []
        for j in range(SCATTER_PEERS):
            p = SCATTER_PEERS * i + j
            row = jnp.where(slot < count_ref[0, p], rows_ref[pl.ds(p, 1), :], -1)
            hots.append(low_onehot(column(row)))
            total = recv_ref[p, pl.ds(0, FQ), :].astype(F32)
            for r in range(1, N_REP):
                total = total + recv_ref[r * N_DOM + p, pl.ds(0, FQ), :].astype(F32)
            high = lax.shift_right_arithmetic(row, 8)
            pieces = [halves(jnp.where(high == c, total, 0.0)) for c in range(chunks)]
            sides.append(jnp.concatenate([h for h, _ in pieces] + [l for _, l in pieces], axis=0))
        acc[...] += dot(jnp.concatenate(sides, axis=1), jnp.concatenate(hots, axis=0))
        return carry

    lax.fori_loop(0, N_DOM // SCATTER_PEERS, step, 0)
    for b in range(LOCAL):
        c, side = b // 2, b % 2
        lanes = pl.ds(side * BLK, BLK)
        here = acc[pl.ds(c * FQ, FQ), lanes] + acc[pl.ds((chunks + c) * FQ, FQ), lanes]
        near = own_ref[b] + a_ref[b].astype(F32) + b_ref[b].astype(F32) + c_ref[b].astype(F32)
        out_ref[b] = (here + near).astype(BF16)


def scatter_rows(counts, rows, received, own, a, b, c):
    return pl.pallas_call(
        scatter_kernel,
        out_shape=jax.ShapeDtypeStruct((LOCAL, FQ, BLK), BF16),
        in_specs=[SM] + [VM] * 6,
        out_specs=VM,
        scratch_shapes=[pltpu.VMEM((2 * FIN * 2, LO), F32)],
        compiler_params=PARAMS,
        cost_estimate=pl.CostEstimate(flops=4 * 10**9, bytes_accessed=4 * 10**6, transcendentals=0),
        name="scatter_rows",
    )(counts, rows, received, own, a, b, c)


def final_kernel(place_ref, hub_ref, m0, m1, m2, m3, shared_ref, gx_ref, gw_ref, blocks, *, scale):
    rep = place_ref[0]
    for k, ref in enumerate((m0, m1, m2, m3)):
        start = pl.multiple_of(lax.rem(rep + N_REP - k, N_REP) * FQ, FQ)
        blocks[:, pl.ds(start, FQ), :] = ref[...].astype(F32)
    for h in range(HUBS):
        block = hub_ref[h]

        @pl.when(lax.shift_right_logical(block, 4) == place_ref[1])
        def _():
            for q in range(N_REP):
                for k in range(2):
                    piece = shared_ref[q * N_DOM + 4 * h + 2 * k].astype(F32)
                    blocks[block & (LOCAL - 1), pl.ds(q * FQ + k * 16, 16), :] += piece

    for b in range(LOCAL):
        gx_ref[pl.ds(b * BLK, BLK), :] = blocks[b].T
    for c in range(16):
        g, side = c // 2, c % 2
        high, low = [shared_ref[(n // 8) * N_DOM + 2 * (n % 8) + 1].astype(F32) for n in (c, 16 + c)]
        gw_ref[pl.ds(g * 16, 16), pl.ds(side * BLK, BLK)] = (high + low) * scale


def finish(place, hubs, parts, shared, scale):
    return pl.pallas_call(
        functools.partial(final_kernel, scale=scale),
        out_shape=[
            jax.ShapeDtypeStruct((ROWS, FIN), F32),
            jax.ShapeDtypeStruct((FIN, HID), F32),
        ],
        in_specs=[SM, SM] + [VM] * 5,
        out_specs=[VM] * 2,
        scratch_shapes=[pltpu.VMEM((LOCAL, FIN, BLK), F32)],
        compiler_params=PARAMS,
        name="finish",
    )(place, hubs, *parts, shared)


def place_kernel(act_ref, out_ref):
    out_ref[...] = act_ref[...]


def place_output(output):
    return pl.pallas_call(
        place_kernel,
        out_shape=jax.ShapeDtypeStruct(output.shape, output.dtype),
        in_specs=[VM],
        out_specs=VM,
        compiler_params=PARAMS,
        name="place_output",
    )(output)


def turn(value, k):
    return lax.ppermute(value, "rep", [(i, (i + k) % N_REP) for i in range(N_REP)])


def around(value):
    return [value] + [turn(value, k) for k in (1, 2, 3)]


def swap(value, axes):
    return lax.all_to_all(value, axes, split_axis=0, concat_axis=0, tiled=True)


def shards(
    features,
    proj_weight,
    bias,
    cotangent,
    send_rows,
    send_count,
    hub_blocks,
    tile_dst,
    tile_src,
    tile_weight,
):
    rep = lax.axis_index("rep").astype(jnp.int32)
    dom = lax.axis_index("dom").astype(jnp.int32)
    place = jnp.stack([rep, dom])
    hub_blocks, send_count = in_hbm(hub_blocks), in_hbm(send_count)
    blocks = features.reshape(LOCAL, BLK, FIN)
    rows = send_rows[0]

    weights = tile_weight[0, 0]
    received = swap(gather_rows(rows, send_count, hub_blocks, features), "dom")
    fwd, bwd = order_tiles(
        tile_dst[0, 0].reshape(TILES // BLK, BLK), tile_src[0, 0].reshape(TILES // BLK, BLK)
    )
    stored = in_hbm(weights)
    near = forward_near(fwd, blocks, stored)
    hubs = swap(hub_piece(place, hub_blocks, received), "dom").reshape(HUBS, BLK, FIN)
    far = forward_remote(fwd, near, received, stored)
    own, s1, s2, s3 = forward_hub(fwd, place, far, hubs, stored)
    a, b, c = turn(s1, 1), turn(s2, 2), turn(s3, 3)
    out_part, y_part, gw = middle(
        place, own, a, b, c, proj_weight, bias.reshape(1, HID), cotangent
    )
    ys = around(y_part)
    message = backward_far(bwd, place, ys, gw, hold_tiles(stored, y_part))
    out_part, message = lax.optimization_barrier((out_part, message))
    output = lax.all_gather(out_part, "rep", axis=0, tiled=True)
    returned = swap(message.reshape(N_REP * N_DOM, MSG, BLK), ("rep", "dom"))
    own, s1, s2, s3 = backward_near(bwd, place, ys, stored)
    a, b, c = turn(s1, 1), turn(s2, 2), turn(s3, 3)

    piece = jnp.sum(returned[:, FQ:, :].astype(F32), axis=0).astype(BF16)
    shared = swap(jnp.broadcast_to(piece[None], (N_REP * N_DOM, 16, BLK)), ("rep", "dom"))
    part = scatter_rows(send_count, rows, returned, own, a, b, c)
    output, _ = lax.optimization_barrier((output, part))
    grad_x, grad_w = finish(place, hub_blocks, around(part), shared, 1.0 / math.sqrt(ROWS * N_DOM))
    return (place_output(output), grad_x, grad_w)


def solution(mesh):
    in_specs = (
        P("dom", None),
        P(),
        P(),
        P("dom", None),
        P("dom", None, None),
        P("dom", None),
        P(),
        P("rep", "dom", None),
        P("rep", "dom", None),
        P("rep", "dom", None, None, None),
    )
    out_specs = (P("dom", None), P("dom", None), P())
    return jax.shard_map(shards, mesh=mesh, in_specs=in_specs, out_specs=out_specs, check_vma=False)
```

```python
import functools
import math

import jax
import jax.numpy as jnp
from jax import lax
from jax.experimental import pallas as pl
from jax.experimental.pallas import tpu as pltpu
from jax.sharding import PartitionSpec as P

F32 = jnp.float32
BF16 = jnp.bfloat16
BLK = 128
N_REP = 4
N_DOM = 32
FIN = 128
HID = 256
ROWS = 2048
LOCAL = ROWS // BLK
HUBS = 8
BLOCKS = LOCAL + N_DOM + HUBS
TILES = 384
REMOTE = N_DOM
CHUNK = 32
FWD_SLOTS = 512
BWD_SLOTS = 512
QUARTER = ROWS // N_REP
QB = LOCAL // N_REP
FQ = FIN // N_REP
MSG = FQ + 16
HUB_ROWS = HUBS * BLK // N_DOM
LO = 256
VMEM_LIMIT = 24 * 1024 * 1024

VM = pl.BlockSpec(memory_space=pltpu.VMEM)
SM = pl.BlockSpec(memory_space=pltpu.SMEM)
FAR = pl.BlockSpec(memory_space=pltpu.HBM)
PARAMS = pltpu.CompilerParams(vmem_limit_bytes=VMEM_LIMIT)
TILE_PARAMS = PARAMS


def in_hbm(x):
    return pltpu.with_memory_space_constraint(x, pltpu.HBM)


def dot(a, b):
    return jnp.dot(a, b, preferred_element_type=F32)


def halves(x):
    high = x.astype(BF16)
    return high, (x - high.astype(F32)).astype(BF16)


def column(row):
    return jnp.broadcast_to(row, (BLK, BLK)).T


def low_onehot(col):
    low = jnp.where(col < 0, -1, col & (LO - 1))
    lane = lax.broadcasted_iota(jnp.int32, (BLK, BLK), 1)
    return jnp.concatenate(
        [jnp.where(low == lane + k * BLK, 1.0, 0.0) for k in range(LO // BLK)], axis=1
    ).astype(BF16)


def sort_tiles(bucket, operand, empty, edges, out_of, slots):
    sub = lax.broadcasted_iota(jnp.int32, (BLK, BLK), 0)
    lane = lax.broadcasted_iota(jnp.int32, (BLK, BLK), 1)
    line = lane[:1]
    parts = len(bucket)
    cols = [column(b) for b in bucket]
    hots = [jnp.where(c == lane, 1.0, 0.0) for c in cols]
    counts = sum(jnp.sum(h, axis=0, keepdims=True) for h in hots).astype(jnp.int32)
    padded = (counts + 1) & -2
    before = jnp.where(sub < lane, column(padded).astype(F32), 0.0)
    starts = jnp.sum(before, axis=0, keepdims=True).astype(jnp.int32)
    first = jnp.zeros((1, BLK), jnp.int32)
    low = 0
    for n, high in enumerate(edges):
        inside = (line >= low) & (line < high)
        size = jnp.sum(jnp.where(inside, padded, 0).astype(F32), axis=1, keepdims=True).astype(jnp.int32)
        gap = ((size + CHUNK - 1) & -CHUNK) - size
        starts = starts + jnp.where(line >= high, gap, 0)
        total = (size + CHUNK - 1) // CHUNK
        first = first + jnp.where(line > n, total, 0)
        low = high
    begin, end = column(starts), column(starts + padded)
    places = []
    for i in range(parts):
        rank = jnp.sum(jnp.where(hots[i] > 0.0, starts.astype(F32), 0.0), axis=1, keepdims=True)
        for j in range(i + 1):
            same = jnp.broadcast_to(bucket[j], (BLK, BLK)) == cols[i]
            if j == i:
                same = same & (lane < sub)
            rank = rank + jnp.sum(jnp.where(same, 1.0, 0.0), axis=1, keepdims=True)
        places.append(jnp.broadcast_to(rank.astype(jnp.int32), (BLK, BLK)))
    shifted = [column(o - empty).astype(F32) for o in operand]
    tiles, blocks, outs = [], [], []
    for s in range(slots // BLK):
        here = lane + s * BLK
        tile = jnp.zeros((1, BLK), F32)
        block = jnp.zeros((1, BLK), F32)
        for i in range(parts):
            hit = places[i] == here
            tile = tile + jnp.sum(jnp.where(hit, (sub + i * BLK).astype(F32), 0.0), axis=0, keepdims=True)
            block = block + jnp.sum(jnp.where(hit, shifted[i], 0.0), axis=0, keepdims=True)
        inside = (begin <= here) & (here < end)
        out = jnp.sum(jnp.where(inside, out_of(sub).astype(F32), 0.0), axis=0, keepdims=True)
        tiles.append(tile.astype(jnp.int32))
        blocks.append(block.astype(jnp.int32) + empty)
        outs.append(out.astype(jnp.int32))
    return tiles, blocks, outs, first


def order_kernel(dst_ref, src_ref, fwd_ref, bwd_ref):
    parts = TILES // BLK
    dst = [dst_ref[pl.ds(i, 1), :] for i in range(parts)]
    src = [src_ref[pl.ds(i, 1), :] for i in range(parts)]
    bucket = [jnp.where(s < LOCAL, d, d + LOCAL) for d, s in zip(dst, src)]
    operand = [jnp.where(s < LOCAL, s, s - LOCAL) for s in src]
    empty = REMOTE + HUBS
    found = sort_tiles(bucket, operand, empty, (LOCAL, 2 * LOCAL), lambda b: b & (LOCAL - 1), FWD_SLOTS)
    for n, rows in enumerate(found[:3]):
        for s, row in enumerate(rows):
            fwd_ref[n, pl.ds(s, 1), :] = row
    fwd_ref[3, pl.ds(0, 1), :] = found[3]
    far = REMOTE + HUBS
    bucket = [jnp.where(s < LOCAL, s + far, s - LOCAL) for s in src]
    found = sort_tiles(
        bucket, dst, LOCAL, (far, far + LOCAL), lambda b: jnp.where(b < far, b, b - far), BWD_SLOTS
    )
    for n, rows in enumerate(found[:3]):
        for s, row in enumerate(rows):
            bwd_ref[n, pl.ds(s, 1), :] = row
    bwd_ref[3, pl.ds(0, 1), :] = found[3]


def order_tiles(dst, src):
    return pl.pallas_call(
        order_kernel,
        out_shape=[
            jax.ShapeDtypeStruct((4, FWD_SLOTS // BLK, BLK), jnp.int32),
            jax.ShapeDtypeStruct((4, BWD_SLOTS // BLK, BLK), jnp.int32),
        ],
        in_specs=[VM, VM],
        out_specs=[VM, VM],
        compiler_params=PARAMS,
        name="order_tiles",
    )(dst, src)


AHEAD = 3


def keep(tiles, buckets):
    chunks = -(-(tiles + buckets) // CHUNK)
    return [pltpu.VMEM((chunks * CHUNK, BLK, BLK), BF16), pltpu.SemaphoreType.DMA((chunks,))]


def extent(plan_ref, number):
    begin = plan_ref[3, 0, number]
    return begin, plan_ref[3, 0, number + 1] - begin


def where(i):
    return i // (BLK // CHUNK), lax.rem(i, BLK // CHUNK) * CHUNK


def fetch(plan_ref, number, c, w_ref, held, sems):
    row, col = where(extent(plan_ref, number)[0] + c)
    for k in range(CHUNK):
        tile = plan_ref[0, row, col + k]
        pltpu.make_async_copy(w_ref.at[tile], held.at[c * CHUNK + k], sems.at[c]).start()


def fetch_first(plan_ref, number, w_ref, held, sems):
    def first(c, carry):
        fetch(plan_ref, number, c, w_ref, held, sems)
        return carry

    lax.fori_loop(0, jnp.minimum(extent(plan_ref, number)[1], AHEAD), first, 0)


def run_class(plan_ref, number, w_ref, held, sems, product, acc):
    begin, count = extent(plan_ref, number)

    def chunk(c, carry):
        row, col = where(begin + c)
        if held is not None:
            slots = held.at[pl.ds(c * CHUNK, CHUNK)]
            pltpu.make_async_copy(w_ref.at[pl.ds(0, CHUNK)], slots, sems.at[c]).wait()

            @pl.when(c + AHEAD < count)
            def _():
                fetch(plan_ref, number, c + AHEAD, w_ref, held, sems)

        found = []
        for k in range(0, CHUNK, 2):
            pair = []
            for j in (k, k + 1):
                tile = w_ref[plan_ref[0, row, col + j]] if held is None else held[c * CHUNK + j]
                pair.append((tile, plan_ref[1, row, col + j]))
            one, two = pair
            found.append((plan_ref[2, row, col + k], product(one, two)))
        for d, value in found:
            acc[d] += value
        return carry

    lax.fori_loop(0, count, chunk, 0)


PEERS = 8


def gather_kernel(rows_hbm, count_ref, feat_hbm, out_ref, rows_ref, feat_ref, sems):
    loads = [
        pltpu.make_async_copy(feat_hbm, feat_ref, sems.at[0]),
        pltpu.make_async_copy(rows_hbm, rows_ref, sems.at[1]),
    ]
    for load in loads:
        load.start()
    for load in loads:
        load.wait()
    slot = lax.broadcasted_iota(jnp.int32, (1, BLK), 1)

    def step(i, carry):
        cols = []
        for j in range(PEERS):
            p = PEERS * i + j
            row = jnp.where(slot < count_ref[0, p], rows_ref[pl.ds(p, 1), :], -1)
            cols.append(column(row))
        hot = jnp.concatenate([low_onehot(c) for c in cols], axis=0)
        high = lax.shift_right_arithmetic(jnp.concatenate(cols, axis=0), 8)
        total = jnp.zeros((PEERS * BLK, FIN), F32)
        for pair in range(ROWS // LO // 2):
            left = feat_ref[pl.ds(2 * pair * LO, LO), :]
            right = feat_ref[pl.ds((2 * pair + 1) * LO, LO), :]
            got = dot(hot, jnp.concatenate([left, right], axis=1))
            total = jnp.where(high == 2 * pair, got[:, :FIN], total)
            total = jnp.where(high == 2 * pair + 1, got[:, FIN:], total)
        out_ref[pl.ds(PEERS * i, PEERS), pl.ds(0, BLK), :] = total.astype(BF16).reshape(PEERS, BLK, FIN)
        return carry

    lax.fori_loop(0, N_DOM // PEERS, step, 0)


def gather_rows(rows, counts, features):
    return pl.pallas_call(
        gather_kernel,
        out_shape=jax.ShapeDtypeStruct((N_DOM, BLK + HUB_ROWS, FIN), BF16),
        in_specs=[FAR, SM, FAR],
        out_specs=VM,
        scratch_shapes=[
            pltpu.VMEM((N_DOM, BLK), jnp.int32),
            pltpu.VMEM((ROWS, FIN), BF16),
            pltpu.SemaphoreType.DMA((2,)),
        ],
        compiler_params=PARAMS,
        cost_estimate=pl.CostEstimate(flops=4 * 10**9, bytes_accessed=2 * 10**6, transcendentals=0),
        name="gather_rows",
    )(in_hbm(rows), counts, in_hbm(features))


def hub_pick_kernel(hub_ref, feat_hbm, out_ref, sem):
    copies = []
    for h in range(HUBS):
        block = hub_ref[h] & (LOCAL - 1)
        copies.append(pltpu.make_async_copy(feat_hbm.at[block], out_ref.at[h], sem.at[h]))
    for copy in copies:
        copy.start()
    for copy in copies:
        copy.wait()


def pick_hubs(hubs, features):
    return pl.pallas_call(
        hub_pick_kernel,
        out_shape=jax.ShapeDtypeStruct((HUBS, BLK, FIN), BF16),
        in_specs=[SM, FAR],
        out_specs=VM,
        scratch_shapes=[pltpu.SemaphoreType.DMA((HUBS,))],
        compiler_params=PARAMS,
        name="pick_hubs",
    )(hubs, in_hbm(features))


def insert_kernel(place_ref, hub_ref, spread_ref, listed_ref, out_ref, wide, sem):
    del listed_ref
    owner = lax.shift_right_logical(hub_ref[place_ref[1] // (BLK // HUB_ROWS)], 4)
    piece = spread_ref[owner]
    for p in range(N_DOM):
        wide[p] = piece
    copy = pltpu.make_async_copy(wide, out_ref.at[:, pl.ds(BLK, HUB_ROWS), :], sem)
    copy.start()
    copy.wait()


def insert_hubs(place, hubs, spread, listed):
    return pl.pallas_call(
        insert_kernel,
        out_shape=jax.ShapeDtypeStruct(listed.shape, BF16),
        in_specs=[SM, SM, VM, pl.BlockSpec(memory_space=pl.ANY)],
        out_specs=pl.BlockSpec(memory_space=pl.ANY),
        scratch_shapes=[pltpu.VMEM((N_DOM, HUB_ROWS, FIN), BF16), pltpu.SemaphoreType.DMA],
        input_output_aliases={3: 0},
        compiler_params=PARAMS,
        name="insert_hubs",
    )(place, hubs, spread, listed)


def forward_product(xs):
    def product(one, two):
        left = jnp.concatenate([one[0], two[0]], axis=1)
        return dot(left, jnp.concatenate([xs[one[1]], xs[two[1]]], axis=0))

    return product


FORWARD_XS = pltpu.VMEM((REMOTE + HUBS + 1, BLK, FIN), BF16)


def forward_near_kernel(plan_ref, feat_ref, w_ref, acc_ref, xs, held, sems):
    fetch_first(plan_ref, 0, w_ref, held, sems)
    xs[pl.ds(0, LOCAL)] = feat_ref[...]
    xs[REMOTE + HUBS] = jnp.zeros((BLK, FIN), BF16)
    acc_ref[...] = jnp.zeros_like(acc_ref)
    run_class(plan_ref, 0, w_ref, held, sems, forward_product(xs), acc_ref)


def forward_far_kernel(plan_ref, place_ref, near_ref, recv_ref, w_ref, own_ref, s1, s2, s3, xs, acc, held, sems):
    fetch_first(plan_ref, 1, w_ref, held, sems)
    xs[pl.ds(0, REMOTE)] = recv_ref[:, pl.ds(0, BLK), :]
    per_hub = BLK // HUB_ROWS
    for p in range(N_DOM):
        rows = pl.ds((p % per_hub) * HUB_ROWS, HUB_ROWS)
        xs[REMOTE + p // per_hub, rows, :] = recv_ref[p, pl.ds(BLK, HUB_ROWS), :]
    xs[REMOTE + HUBS] = jnp.zeros((BLK, FIN), BF16)
    acc[...] = near_ref[...]
    run_class(plan_ref, 1, w_ref, held, sems, forward_product(xs), acc)
    rep = place_ref[0]
    own_ref[...] = acc[pl.ds(rep * QB, QB)]
    for k, ref in ((1, s1), (2, s2), (3, s3)):
        ref[...] = acc[pl.ds(lax.rem(rep + k, N_REP) * QB, QB)].astype(BF16)


def forward_near(plan, features, weights):
    return pl.pallas_call(
        forward_near_kernel,
        out_shape=jax.ShapeDtypeStruct((LOCAL, BLK, FIN), F32),
        in_specs=[SM, VM, FAR],
        out_specs=VM,
        scratch_shapes=[FORWARD_XS] + keep(LOCAL * LOCAL, LOCAL),
        compiler_params=TILE_PARAMS,
        cost_estimate=pl.CostEstimate(flops=10**9, bytes_accessed=4 * 10**6, transcendentals=0),
        name="forward_near",
    )(plan, features, weights)


def forward_far(plan, place, near, received, weights):
    quarter = (QB, BLK, FIN)
    return pl.pallas_call(
        forward_far_kernel,
        out_shape=[jax.ShapeDtypeStruct(quarter, F32)] + [jax.ShapeDtypeStruct(quarter, BF16)] * 3,
        in_specs=[SM, SM, VM, VM, FAR],
        out_specs=[VM] * 4,
        scratch_shapes=[FORWARD_XS, pltpu.VMEM((LOCAL, BLK, FIN), F32)] + keep(TILES, LOCAL),
        compiler_params=TILE_PARAMS,
        cost_estimate=pl.CostEstimate(flops=4 * 10**9, bytes_accessed=12 * 10**6, transcendentals=0),
        name="forward_far",
    )(plan, place, near, received, weights)


def sum_kernel(own_ref, a_ref, b_ref, c_ref, out_ref):
    far = a_ref[...].astype(F32) + b_ref[...].astype(F32) + c_ref[...].astype(F32)
    out_ref[...] = (own_ref[...] + far).astype(BF16)


def sum_quarter(own, a, b, c):
    return pl.pallas_call(
        sum_kernel,
        out_shape=jax.ShapeDtypeStruct((QB, BLK, FIN), BF16),
        in_specs=[VM] * 4,
        out_specs=VM,
        compiler_params=PARAMS,
        name="sum_quarter",
    )(own, a, b, c)


def middle_kernel(place_ref, z0, z1, z2, z3, w_ref, bias_ref, cot_ref, out_ref, y_ref, gw_ref):
    weight = w_ref[...]
    root = math.sqrt(2.0 / math.pi)
    for turned, ref in enumerate((z0, z1, z2, z3)):
        quarter = lax.rem(place_ref[0] + N_REP - turned, N_REP)
        zx = ref[...].reshape(QUARTER, FIN)
        pre = dot(zx, weight) + bias_ref[...]
        square = pre * pre
        bent = jnp.tanh(root * (pre + 0.044715 * (square * pre)))
        cdf = 0.5 * (1.0 + bent)
        rows = pl.ds(pl.multiple_of(quarter * QUARTER, QUARTER), QUARTER)
        out_ref[rows, :] = (pre * cdf).astype(BF16)
        slope = cdf + (0.5 * pre) * ((1.0 - bent * bent) * (root * (1.0 + (3 * 0.044715) * square)))
        pre_grad = (cot_ref[rows, :].astype(F32) * slope).astype(BF16)
        yt = lax.dot_general(weight, pre_grad, (((1,), (1,)), ((), ())), preferred_element_type=F32)
        yt = yt.astype(BF16)
        for k in range(QB):
            y_ref[quarter * QB + k] = yt[:, k * BLK : (k + 1) * BLK]
        if turned == 0:
            gw = dot(zx.T, pre_grad)
            for part, piece in enumerate(halves(gw)):
                for c in range(16):
                    g, side = c // 2, c % 2
                    gw_ref[part * 16 + c] = piece[g * 16 : (g + 1) * 16, side * BLK : (side + 1) * BLK]
    y_ref[LOCAL] = jnp.zeros((FIN, BLK), BF16)


def middle(place, zs, weight, bias, cotangent):
    return pl.pallas_call(
        middle_kernel,
        out_shape=[
            jax.ShapeDtypeStruct((ROWS, HID), BF16),
            jax.ShapeDtypeStruct((LOCAL + 1, FIN, BLK), BF16),
            jax.ShapeDtypeStruct((32, 16, BLK), BF16),
        ],
        in_specs=[SM] + [VM] * 7,
        out_specs=[VM] * 3,
        compiler_params=PARAMS,
        cost_estimate=pl.CostEstimate(flops=5 * 10**9, bytes_accessed=3 * 10**6, transcendentals=0),
        name="middle",
    )(place, *zs, weight, bias, cotangent)


def hold_kernel(w_ref, after_ref, held_ref, sem):
    del after_ref
    copy = pltpu.make_async_copy(w_ref, held_ref, sem)
    copy.start()
    copy.wait()


def hold_tiles(weights, after):
    return pl.pallas_call(
        hold_kernel,
        out_shape=pltpu.VMEM((TILES, BLK, BLK), BF16),
        in_specs=[FAR, pl.BlockSpec(memory_space=pl.ANY)],
        out_specs=VM,
        scratch_shapes=[pltpu.SemaphoreType.DMA],
        compiler_params=PARAMS,
        cost_estimate=pl.CostEstimate(flops=0, bytes_accessed=13 * 10**6, transcendentals=0),
        name="hold_tiles",
    )(weights, after)


def backward_product(ys):
    def product(one, two):
        left = jnp.concatenate([ys[one[1]], ys[two[1]]], axis=1)
        return dot(left, jnp.concatenate([one[0], two[0]], axis=0))

    return product


def backward_far_kernel(plan_ref, ys, gw_ref, w_ref, msg_ref, acc):
    acc[...] = jnp.zeros_like(acc)
    run_class(plan_ref, 0, w_ref, None, None, backward_product(ys), acc)
    for q in range(N_REP):
        msg_ref[q, :, pl.ds(0, FQ), :] = acc[pl.ds(0, REMOTE), pl.ds(q * FQ, FQ), :].astype(BF16)
        for m in range(16):
            piece = acc[REMOTE + m // 2, pl.ds(q * FQ + (m % 2) * 16, 16), :]
            msg_ref[q, 2 * m, pl.ds(FQ, 16), :] = piece.astype(BF16)
            if m < 8:
                msg_ref[q, 2 * m + 1, pl.ds(FQ, 16), :] = gw_ref[q * 8 + m]
            else:
                msg_ref[q, 2 * m + 1, pl.ds(FQ, 16), :] = jnp.zeros((16, BLK), BF16)


def backward_far(plan, ys, gw, weights):
    return pl.pallas_call(
        backward_far_kernel,
        out_shape=jax.ShapeDtypeStruct((N_REP, N_DOM, MSG, BLK), BF16),
        in_specs=[SM] + [VM] * 3,
        out_specs=VM,
        scratch_shapes=[pltpu.VMEM((REMOTE + HUBS, FIN, BLK), F32)],
        compiler_params=TILE_PARAMS,
        cost_estimate=pl.CostEstimate(flops=4 * 10**9, bytes_accessed=14 * 10**6, transcendentals=0),
        name="backward_far",
    )(plan, ys, gw, weights)


def backward_near_kernel(plan_ref, rep_ref, ys, w_ref, own_ref, s1, s2, s3, acc, held, sems):
    fetch_first(plan_ref, 1, w_ref, held, sems)
    rep = rep_ref[0]
    acc[...] = jnp.zeros_like(acc)
    run_class(plan_ref, 1, w_ref, held, sems, backward_product(ys), acc)

    def rows_of(k):
        start = pl.multiple_of(lax.rem(rep + k, N_REP) * FQ, FQ)
        return acc[:, pl.ds(start, FQ), :]

    own_ref[...] = rows_of(0)
    for k, ref in ((1, s1), (2, s2), (3, s3)):
        ref[...] = rows_of(k).astype(BF16)


def backward_near(plan, rep, ys, weights):
    part = (LOCAL, FQ, BLK)
    return pl.pallas_call(
        backward_near_kernel,
        out_shape=[jax.ShapeDtypeStruct(part, F32)] + [jax.ShapeDtypeStruct(part, BF16)] * 3,
        in_specs=[SM, SM, VM, FAR],
        out_specs=[VM] * 4,
        scratch_shapes=[pltpu.VMEM((LOCAL, FIN, BLK), F32)] + keep(LOCAL * LOCAL, LOCAL),
        compiler_params=TILE_PARAMS,
        cost_estimate=pl.CostEstimate(flops=10**9, bytes_accessed=14 * 10**6, transcendentals=0),
        name="backward_near",
    )(plan, rep, ys, weights)


SCATTER_PEERS = 8


def scatter_kernel(count_ref, rows_ref, recv_ref, own_ref, a_ref, b_ref, c_ref, out_ref, acc):
    chunks = ROWS // LO
    slot = lax.broadcasted_iota(jnp.int32, (1, BLK), 1)
    acc[...] = jnp.zeros_like(acc)

    def step(i, carry):
        hots, sides = [], []
        for j in range(SCATTER_PEERS):
            p = SCATTER_PEERS * i + j
            row = jnp.where(slot < count_ref[0, p], rows_ref[pl.ds(p, 1), :], -1)
            hots.append(low_onehot(column(row)))
            total = recv_ref[p, pl.ds(0, FQ), :].astype(F32)
            for r in range(1, N_REP):
                total = total + recv_ref[r * N_DOM + p, pl.ds(0, FQ), :].astype(F32)
            high = lax.shift_right_arithmetic(row, 8)
            pieces = [halves(jnp.where(high == c, total, 0.0)) for c in range(chunks)]
            sides.append(jnp.concatenate([h for h, _ in pieces] + [l for _, l in pieces], axis=0))
        acc[...] += dot(jnp.concatenate(sides, axis=1), jnp.concatenate(hots, axis=0))
        return carry

    lax.fori_loop(0, N_DOM // SCATTER_PEERS, step, 0)
    for b in range(LOCAL):
        c, side = b // 2, b % 2
        lanes = pl.ds(side * BLK, BLK)
        here = acc[pl.ds(c * FQ, FQ), lanes] + acc[pl.ds((chunks + c) * FQ, FQ), lanes]
        near = own_ref[b] + a_ref[b].astype(F32) + b_ref[b].astype(F32) + c_ref[b].astype(F32)
        out_ref[b] = (here + near).astype(BF16)


def scatter_rows(counts, rows, received, own, a, b, c):
    return pl.pallas_call(
        scatter_kernel,
        out_shape=jax.ShapeDtypeStruct((LOCAL, FQ, BLK), BF16),
        in_specs=[SM] + [VM] * 6,
        out_specs=VM,
        scratch_shapes=[pltpu.VMEM((2 * FIN * 2, LO), F32)],
        compiler_params=PARAMS,
        cost_estimate=pl.CostEstimate(flops=4 * 10**9, bytes_accessed=4 * 10**6, transcendentals=0),
        name="scatter_rows",
    )(counts, rows, received, own, a, b, c)


def final_kernel(place_ref, hub_ref, m0, m1, m2, m3, shared_ref, gx_ref, gw_ref, blocks, *, scale):
    rep = place_ref[0]
    for k, ref in enumerate((m0, m1, m2, m3)):
        start = pl.multiple_of(lax.rem(rep + N_REP - k, N_REP) * FQ, FQ)
        blocks[:, pl.ds(start, FQ), :] = ref[...].astype(F32)
    for h in range(HUBS):
        block = hub_ref[h]

        @pl.when(lax.shift_right_logical(block, 4) == place_ref[1])
        def _():
            for q in range(N_REP):
                for k in range(2):
                    piece = shared_ref[q * N_DOM + 4 * h + 2 * k].astype(F32)
                    blocks[block & (LOCAL - 1), pl.ds(q * FQ + k * 16, 16), :] += piece

    for b in range(LOCAL):
        gx_ref[pl.ds(b * BLK, BLK), :] = blocks[b].T
    for c in range(16):
        g, side = c // 2, c % 2
        high, low = [shared_ref[(n // 8) * N_DOM + 2 * (n % 8) + 1].astype(F32) for n in (c, 16 + c)]
        gw_ref[pl.ds(g * 16, 16), pl.ds(side * BLK, BLK)] = (high + low) * scale


def finish(place, hubs, parts, shared, scale):
    return pl.pallas_call(
        functools.partial(final_kernel, scale=scale),
        out_shape=[
            jax.ShapeDtypeStruct((ROWS, FIN), F32),
            jax.ShapeDtypeStruct((FIN, HID), F32),
        ],
        in_specs=[SM, SM] + [VM] * 5,
        out_specs=[VM] * 2,
        scratch_shapes=[pltpu.VMEM((LOCAL, FIN, BLK), F32)],
        compiler_params=PARAMS,
        name="finish",
    )(place, hubs, *parts, shared)


def turn(value, k):
    return lax.ppermute(value, "rep", [(i, (i + k) % N_REP) for i in range(N_REP)])


def around(value):
    return [value] + [turn(value, k) for k in (1, 2, 3)]


def swap(value, axes):
    return lax.all_to_all(value, axes, split_axis=0, concat_axis=0, tiled=True)


def shards(
    features,
    proj_weight,
    bias,
    cotangent,
    send_rows,
    send_count,
    hub_blocks,
    tile_dst,
    tile_src,
    tile_weight,
):
    rep = lax.axis_index("rep").astype(jnp.int32)
    dom = lax.axis_index("dom").astype(jnp.int32)
    place = jnp.stack([rep, dom])
    hub_blocks, send_count = in_hbm(hub_blocks), in_hbm(send_count)
    blocks = features.reshape(LOCAL, BLK, FIN)
    rows = send_rows[0]

    weights = tile_weight[0, 0]
    spread = swap(pick_hubs(hub_blocks, blocks).reshape(N_DOM, HUB_ROWS, FIN), "dom")
    listed = gather_rows(rows, send_count, features)
    received = swap(insert_hubs(place, hub_blocks, spread, listed), "dom")
    fwd, bwd = order_tiles(
        tile_dst[0, 0].reshape(TILES // BLK, BLK), tile_src[0, 0].reshape(TILES // BLK, BLK)
    )
    stored = in_hbm(weights)
    near = forward_near(fwd, blocks, stored)
    own, s1, s2, s3 = forward_far(fwd, place, near, received, stored)
    a, b, c = turn(s1, 1), turn(s2, 2), turn(s3, 3)
    zq = sum_quarter(own, a, b, c)
    held = hold_tiles(stored, zq)
    output, ys, gw = middle(place, around(zq), proj_weight, bias.reshape(1, HID), cotangent)
    message = backward_far(bwd, ys, gw, held)
    returned = swap(message.reshape(N_REP * N_DOM, MSG, BLK), ("rep", "dom"))
    own, s1, s2, s3 = backward_near(bwd, place, ys, stored)
    a, b, c = turn(s1, 1), turn(s2, 2), turn(s3, 3)

    piece = jnp.sum(returned[:, FQ:, :].astype(F32), axis=0).astype(BF16)
    shared = swap(jnp.broadcast_to(piece[None], (N_REP * N_DOM, 16, BLK)), ("rep", "dom"))
    part = scatter_rows(send_count, rows, returned, own, a, b, c)
    grad_x, grad_w = finish(place, hub_blocks, around(part), shared, 1.0 / math.sqrt(ROWS * N_DOM))
    return (output, grad_x, grad_w)


def solution(mesh):
    in_specs = (
        P("dom", None),
        P(),
        P(),
        P("dom", None),
        P("dom", None, None),
        P("dom", None),
        P(),
        P("rep", "dom", None),
        P("rep", "dom", None),
        P("rep", "dom", None, None, None),
    )
    out_specs = (P("dom", None), P("dom", None), P())
    return jax.shard_map(shards, mesh=mesh, in_specs=in_specs, out_specs=out_specs, check_vma=False)
```

```python
import functools
import math

import jax
import jax.numpy as jnp
from jax import lax
from jax.experimental import pallas as pl
from jax.experimental.pallas import tpu as pltpu
from jax.sharding import PartitionSpec as P

F32 = jnp.float32
BF16 = jnp.bfloat16
BLK = 128
N_REP = 4
N_DOM = 32
FIN = 128
HID = 256
ROWS = 2048
LOCAL = ROWS // BLK
HUBS = 8
BLOCKS = LOCAL + N_DOM + HUBS
TILES = 384
REMOTE = N_DOM
CHUNK = 32
FWD_SLOTS = 512
BWD_SLOTS = 512
QUARTER = ROWS // N_REP
QB = LOCAL // N_REP
FQ = FIN // N_REP
MSG = FQ + 16
HUB_ROWS = HUBS * BLK // N_DOM
LO = 256
VMEM_LIMIT = 24 * 1024 * 1024

VM = pl.BlockSpec(memory_space=pltpu.VMEM)
SM = pl.BlockSpec(memory_space=pltpu.SMEM)
FAR = pl.BlockSpec(memory_space=pltpu.HBM)
PARAMS = pltpu.CompilerParams(vmem_limit_bytes=VMEM_LIMIT)
TILE_PARAMS = PARAMS


def in_hbm(x):
    return pltpu.with_memory_space_constraint(x, pltpu.HBM)


def dot(a, b):
    return jnp.dot(a, b, preferred_element_type=F32)


def halves(x):
    high = x.astype(BF16)
    return high, (x - high.astype(F32)).astype(BF16)


def column(row):
    return jnp.broadcast_to(row, (BLK, BLK)).T


def low_onehot(col):
    low = jnp.where(col < 0, -1, col & (LO - 1))
    lane = lax.broadcasted_iota(jnp.int32, (BLK, BLK), 1)
    return jnp.concatenate(
        [jnp.where(low == lane + k * BLK, 1.0, 0.0) for k in range(LO // BLK)], axis=1
    ).astype(BF16)


def sort_tiles(bucket, operand, empty, edges, out_of, slots):
    sub = lax.broadcasted_iota(jnp.int32, (BLK, BLK), 0)
    lane = lax.broadcasted_iota(jnp.int32, (BLK, BLK), 1)
    line = lane[:1]
    parts = len(bucket)
    cols = [column(b) for b in bucket]
    hots = [jnp.where(c == lane, 1.0, 0.0) for c in cols]
    counts = sum(jnp.sum(h, axis=0, keepdims=True) for h in hots).astype(jnp.int32)
    padded = (counts + 1) & -2
    before = jnp.where(sub < lane, column(padded).astype(F32), 0.0)
    starts = jnp.sum(before, axis=0, keepdims=True).astype(jnp.int32)
    first = jnp.zeros((1, BLK), jnp.int32)
    low = 0
    for n, high in enumerate(edges):
        inside = (line >= low) & (line < high)
        size = jnp.sum(jnp.where(inside, padded, 0).astype(F32), axis=1, keepdims=True).astype(jnp.int32)
        gap = ((size + CHUNK - 1) & -CHUNK) - size
        starts = starts + jnp.where(line >= high, gap, 0)
        total = (size + CHUNK - 1) // CHUNK
        first = first + jnp.where(line > n, total, 0)
        low = high
    begin, end = column(starts), column(starts + padded)
    places = []
    for i in range(parts):
        rank = jnp.sum(jnp.where(hots[i] > 0.0, starts.astype(F32), 0.0), axis=1, keepdims=True)
        for j in range(i + 1):
            same = jnp.broadcast_to(bucket[j], (BLK, BLK)) == cols[i]
            if j == i:
                same = same & (lane < sub)
            rank = rank + jnp.sum(jnp.where(same, 1.0, 0.0), axis=1, keepdims=True)
        places.append(jnp.broadcast_to(rank.astype(jnp.int32), (BLK, BLK)))
    shifted = [column(o - empty).astype(F32) for o in operand]
    tiles, blocks, outs = [], [], []
    for s in range(slots // BLK):
        here = lane + s * BLK
        tile = jnp.zeros((1, BLK), F32)
        block = jnp.zeros((1, BLK), F32)
        taken = jnp.zeros((1, BLK), F32)
        for i in range(parts):
            hit = places[i] == here
            taken = taken + jnp.sum(jnp.where(hit, 1.0, 0.0), axis=0, keepdims=True)
            tile = tile + jnp.sum(jnp.where(hit, (sub + i * BLK).astype(F32), 0.0), axis=0, keepdims=True)
            block = block + jnp.sum(jnp.where(hit, shifted[i], 0.0), axis=0, keepdims=True)
        inside = (begin <= here) & (here < end)
        out = jnp.sum(jnp.where(inside, out_of(sub).astype(F32), 0.0), axis=0, keepdims=True)
        tile = tile + (1.0 - taken) * (here[:1] & 255).astype(F32)
        tiles.append(tile.astype(jnp.int32))
        blocks.append(block.astype(jnp.int32) + empty)
        outs.append(out.astype(jnp.int32))
    return tiles, blocks, outs, first


def order_kernel(dst_ref, src_ref, fwd_ref, bwd_ref):
    parts = TILES // BLK
    dst = [dst_ref[pl.ds(i, 1), :] for i in range(parts)]
    src = [src_ref[pl.ds(i, 1), :] for i in range(parts)]
    bucket = [jnp.where(s < LOCAL, d, d + LOCAL) for d, s in zip(dst, src)]
    operand = [jnp.where(s < LOCAL, s, s - LOCAL) for s in src]
    empty = REMOTE + HUBS
    found = sort_tiles(bucket, operand, empty, (LOCAL, 2 * LOCAL), lambda b: b & (LOCAL - 1), FWD_SLOTS)
    for n, rows in enumerate(found[:3]):
        for s, row in enumerate(rows):
            fwd_ref[n, pl.ds(s, 1), :] = row
    fwd_ref[3, pl.ds(0, 1), :] = found[3]
    far = REMOTE + HUBS
    bucket = [jnp.where(s < LOCAL, s + far, s - LOCAL) for s in src]
    found = sort_tiles(
        bucket, dst, LOCAL, (far, far + LOCAL), lambda b: jnp.where(b < far, b, b - far), BWD_SLOTS
    )
    for n, rows in enumerate(found[:3]):
        for s, row in enumerate(rows):
            bwd_ref[n, pl.ds(s, 1), :] = row
    bwd_ref[3, pl.ds(0, 1), :] = found[3]


def order_tiles(dst, src):
    return pl.pallas_call(
        order_kernel,
        out_shape=[
            jax.ShapeDtypeStruct((4, FWD_SLOTS // BLK, BLK), jnp.int32),
            jax.ShapeDtypeStruct((4, BWD_SLOTS // BLK, BLK), jnp.int32),
        ],
        in_specs=[VM, VM],
        out_specs=[VM, VM],
        compiler_params=PARAMS,
        name="order_tiles",
    )(dst, src)


AHEAD = 3


def keep(tiles, buckets):
    chunks = -(-(tiles + buckets) // CHUNK)
    return [pltpu.VMEM((chunks * CHUNK, BLK, BLK), BF16), pltpu.SemaphoreType.DMA((chunks,))]


def extent(plan_ref, number):
    begin = plan_ref[3, 0, number]
    return begin, plan_ref[3, 0, number + 1] - begin


def where(i):
    return i // (BLK // CHUNK), lax.rem(i, BLK // CHUNK) * CHUNK


def fetch(plan_ref, number, c, w_ref, held, sems):
    row, col = where(extent(plan_ref, number)[0] + c)
    for k in range(CHUNK):
        tile = plan_ref[0, row, col + k]
        pltpu.make_async_copy(w_ref.at[tile], held.at[c * CHUNK + k], sems.at[c]).start()


def fetch_first(plan_ref, number, w_ref, held, sems):
    def first(c, carry):
        fetch(plan_ref, number, c, w_ref, held, sems)
        return carry

    lax.fori_loop(0, jnp.minimum(extent(plan_ref, number)[1], AHEAD), first, 0)


def run_class(plan_ref, number, w_ref, held, sems, product, acc):
    begin, count = extent(plan_ref, number)

    def chunk(c, carry):
        row, col = where(begin + c)
        if held is not None:
            slots = held.at[pl.ds(c * CHUNK, CHUNK)]
            pltpu.make_async_copy(w_ref.at[pl.ds(0, CHUNK)], slots, sems.at[c]).wait()

            @pl.when(c + AHEAD < count)
            def _():
                fetch(plan_ref, number, c + AHEAD, w_ref, held, sems)

        found = []
        for k in range(0, CHUNK, 2):
            pair = []
            for j in (k, k + 1):
                tile = w_ref[plan_ref[0, row, col + j]] if held is None else held[c * CHUNK + j]
                pair.append((tile, plan_ref[1, row, col + j]))
            one, two = pair
            found.append((plan_ref[2, row, col + k], product(one, two)))
        for d, value in found:
            acc[d] += value
        return carry

    lax.fori_loop(0, count, chunk, 0)


PEERS = 8


def gather_kernel(rows_hbm, count_ref, feat_hbm, out_ref, rows_ref, feat_ref, sems):
    loads = [
        pltpu.make_async_copy(feat_hbm, feat_ref, sems.at[0]),
        pltpu.make_async_copy(rows_hbm, rows_ref, sems.at[1]),
    ]
    for load in loads:
        load.start()
    for load in loads:
        load.wait()
    slot = lax.broadcasted_iota(jnp.int32, (1, BLK), 1)

    def step(i, carry):
        cols = []
        for j in range(PEERS):
            p = PEERS * i + j
            row = jnp.where(slot < count_ref[0, p], rows_ref[pl.ds(p, 1), :], -1)
            cols.append(column(row))
        hot = jnp.concatenate([low_onehot(c) for c in cols], axis=0)
        high = lax.shift_right_arithmetic(jnp.concatenate(cols, axis=0), 8)
        total = jnp.zeros((PEERS * BLK, FIN), F32)
        for pair in range(ROWS // LO // 2):
            left = feat_ref[pl.ds(2 * pair * LO, LO), :]
            right = feat_ref[pl.ds((2 * pair + 1) * LO, LO), :]
            got = dot(hot, jnp.concatenate([left, right], axis=1))
            total = jnp.where(high == 2 * pair, got[:, :FIN], total)
            total = jnp.where(high == 2 * pair + 1, got[:, FIN:], total)
        out_ref[pl.ds(PEERS * i, PEERS), pl.ds(0, BLK), :] = total.astype(BF16).reshape(PEERS, BLK, FIN)
        return carry

    lax.fori_loop(0, N_DOM // PEERS, step, 0)


def gather_rows(rows, counts, features):
    return pl.pallas_call(
        gather_kernel,
        out_shape=jax.ShapeDtypeStruct((N_DOM, BLK + HUB_ROWS, FIN), BF16),
        in_specs=[FAR, SM, FAR],
        out_specs=VM,
        scratch_shapes=[
            pltpu.VMEM((N_DOM, BLK), jnp.int32),
            pltpu.VMEM((ROWS, FIN), BF16),
            pltpu.SemaphoreType.DMA((2,)),
        ],
        compiler_params=PARAMS,
        cost_estimate=pl.CostEstimate(flops=4 * 10**9, bytes_accessed=2 * 10**6, transcendentals=0),
        name="gather_rows",
    )(in_hbm(rows), counts, in_hbm(features))


def hub_pick_kernel(place_ref, hub_ref, feat_ref, out_ref):
    for h in range(HUBS):
        block = hub_ref[h]
        mine = lax.shift_right_logical(block, 4) == place_ref[1]

        @pl.when(mine)
        def _():
            out_ref[h] = feat_ref[block & (LOCAL - 1)]

        @pl.when(jnp.logical_not(mine))
        def _():
            out_ref[h] = jnp.zeros((BLK, FIN), BF16)


def pick_hubs(place, hubs, features):
    return pl.pallas_call(
        hub_pick_kernel,
        out_shape=jax.ShapeDtypeStruct((HUBS, BLK, FIN), BF16),
        in_specs=[SM, SM, VM],
        out_specs=VM,
        compiler_params=PARAMS,
        name="pick_hubs",
    )(place, hubs, in_hbm(features))


def insert_kernel(spread_ref, listed_ref, out_ref, wide, sem):
    del listed_ref
    piece = spread_ref[0].astype(F32)
    for p in range(1, N_DOM):
        piece = piece + spread_ref[p].astype(F32)
    piece = piece.astype(BF16)
    for p in range(N_DOM):
        wide[p] = piece
    copy = pltpu.make_async_copy(wide, out_ref.at[:, pl.ds(BLK, HUB_ROWS), :], sem)
    copy.start()
    copy.wait()


def insert_hubs(spread, listed):
    return pl.pallas_call(
        insert_kernel,
        out_shape=jax.ShapeDtypeStruct(listed.shape, BF16),
        in_specs=[VM, pl.BlockSpec(memory_space=pl.ANY)],
        out_specs=pl.BlockSpec(memory_space=pl.ANY),
        scratch_shapes=[pltpu.VMEM((N_DOM, HUB_ROWS, FIN), BF16), pltpu.SemaphoreType.DMA],
        input_output_aliases={1: 0},
        compiler_params=PARAMS,
        name="insert_hubs",
    )(spread, listed)


def forward_product(xs):
    def product(one, two):
        left = jnp.concatenate([one[0], two[0]], axis=1)
        return dot(left, jnp.concatenate([xs[one[1]], xs[two[1]]], axis=0))

    return product


FORWARD_XS = pltpu.VMEM((REMOTE + HUBS + 1, BLK, FIN), BF16)


def forward_near_kernel(plan_ref, feat_ref, w_ref, acc_ref, xs, held, sems):
    fetch_first(plan_ref, 0, w_ref, held, sems)
    xs[pl.ds(0, LOCAL)] = feat_ref[...]
    xs[REMOTE + HUBS] = jnp.zeros((BLK, FIN), BF16)
    acc_ref[...] = jnp.zeros_like(acc_ref)
    run_class(plan_ref, 0, w_ref, held, sems, forward_product(xs), acc_ref)


def forward_far_kernel(plan_ref, place_ref, near_ref, recv_ref, w_ref, own_ref, s1, s2, s3, xs, acc, held, sems):
    fetch_first(plan_ref, 1, w_ref, held, sems)
    xs[pl.ds(0, REMOTE)] = recv_ref[:, pl.ds(0, BLK), :]
    per_hub = BLK // HUB_ROWS
    for p in range(N_DOM):
        rows = pl.ds((p % per_hub) * HUB_ROWS, HUB_ROWS)
        xs[REMOTE + p // per_hub, rows, :] = recv_ref[p, pl.ds(BLK, HUB_ROWS), :]
    xs[REMOTE + HUBS] = jnp.zeros((BLK, FIN), BF16)
    acc[...] = near_ref[...]
    run_class(plan_ref, 1, w_ref, held, sems, forward_product(xs), acc)
    rep = place_ref[0]
    own_ref[...] = acc[pl.ds(rep * QB, QB)]
    for k, ref in ((1, s1), (2, s2), (3, s3)):
        ref[...] = acc[pl.ds(lax.rem(rep + k, N_REP) * QB, QB)].astype(BF16)


def forward_near(plan, features, weights):
    return pl.pallas_call(
        forward_near_kernel,
        out_shape=jax.ShapeDtypeStruct((LOCAL, BLK, FIN), F32),
        in_specs=[SM, VM, FAR],
        out_specs=VM,
        scratch_shapes=[FORWARD_XS] + keep(LOCAL * LOCAL, LOCAL),
        compiler_params=TILE_PARAMS,
        cost_estimate=pl.CostEstimate(flops=10**9, bytes_accessed=4 * 10**6, transcendentals=0),
        name="forward_near",
    )(plan, features, weights)


def forward_far(plan, place, near, received, weights):
    quarter = (QB, BLK, FIN)
    return pl.pallas_call(
        forward_far_kernel,
        out_shape=[jax.ShapeDtypeStruct(quarter, F32)] + [jax.ShapeDtypeStruct(quarter, BF16)] * 3,
        in_specs=[SM, SM, VM, VM, FAR],
        out_specs=[VM] * 4,
        scratch_shapes=[FORWARD_XS, pltpu.VMEM((LOCAL, BLK, FIN), F32)] + keep(TILES, LOCAL),
        compiler_params=TILE_PARAMS,
        cost_estimate=pl.CostEstimate(flops=4 * 10**9, bytes_accessed=12 * 10**6, transcendentals=0),
        name="forward_far",
    )(plan, place, near, received, weights)


def sum_kernel(own_ref, a_ref, b_ref, c_ref, out_ref):
    far = a_ref[...].astype(F32) + b_ref[...].astype(F32) + c_ref[...].astype(F32)
    out_ref[...] = (own_ref[...] + far).astype(BF16)


def sum_quarter(own, a, b, c):
    return pl.pallas_call(
        sum_kernel,
        out_shape=jax.ShapeDtypeStruct((QB, BLK, FIN), BF16),
        in_specs=[VM] * 4,
        out_specs=VM,
        compiler_params=PARAMS,
        name="sum_quarter",
    )(own, a, b, c)


def middle_kernel(place_ref, z0, z1, z2, z3, w_ref, bias_ref, cot_ref, out_ref, y_ref, gw_ref):
    weight = w_ref[...]
    root = math.sqrt(2.0 / math.pi)
    for turned, ref in enumerate((z0, z1, z2, z3)):
        quarter = lax.rem(place_ref[0] + N_REP - turned, N_REP)
        zx = ref[...].reshape(QUARTER, FIN)
        pre = dot(zx, weight) + bias_ref[...]
        cubic = (root * 0.044715) * (pre * pre)
        bent = jnp.tanh(pre * (root + cubic))
        half = 0.5 * pre
        cdf = 0.5 * bent + 0.5
        rows = pl.ds(pl.multiple_of(quarter * QUARTER, QUARTER), QUARTER)
        out_ref[rows, :] = (half * bent + half).astype(BF16)
        slope = cdf + half * ((1.0 - bent * bent) * (root + 3.0 * cubic))
        pre_grad = (cot_ref[rows, :].astype(F32) * slope).astype(BF16)
        yt = lax.dot_general(weight, pre_grad, (((1,), (1,)), ((), ())), preferred_element_type=F32)
        yt = yt.astype(BF16)
        for k in range(QB):
            y_ref[quarter * QB + k] = yt[:, k * BLK : (k + 1) * BLK]
        if turned == 0:
            gw = dot(zx.T, pre_grad)
            for part, piece in enumerate(halves(gw)):
                for c in range(16):
                    g, side = c // 2, c % 2
                    gw_ref[part * 16 + c] = piece[g * 16 : (g + 1) * 16, side * BLK : (side + 1) * BLK]
    y_ref[LOCAL] = jnp.zeros((FIN, BLK), BF16)


def middle(place, zs, weight, bias, cotangent):
    return pl.pallas_call(
        middle_kernel,
        out_shape=[
            jax.ShapeDtypeStruct((ROWS, HID), BF16),
            jax.ShapeDtypeStruct((LOCAL + 1, FIN, BLK), BF16),
            jax.ShapeDtypeStruct((32, 16, BLK), BF16),
        ],
        in_specs=[SM] + [VM] * 7,
        out_specs=[VM] * 3,
        compiler_params=PARAMS,
        cost_estimate=pl.CostEstimate(flops=5 * 10**9, bytes_accessed=3 * 10**6, transcendentals=0),
        name="middle",
    )(place, *zs, weight, bias, cotangent)


def hold_kernel(w_ref, after_ref, held_ref, sem):
    del after_ref
    copy = pltpu.make_async_copy(w_ref, held_ref, sem)
    copy.start()
    copy.wait()


def hold_tiles(weights, after):
    return pl.pallas_call(
        hold_kernel,
        out_shape=pltpu.VMEM((TILES, BLK, BLK), BF16),
        in_specs=[FAR, pl.BlockSpec(memory_space=pl.ANY)],
        out_specs=VM,
        scratch_shapes=[pltpu.SemaphoreType.DMA],
        compiler_params=PARAMS,
        cost_estimate=pl.CostEstimate(flops=0, bytes_accessed=13 * 10**6, transcendentals=0),
        name="hold_tiles",
    )(weights, after)


def backward_product(ys):
    def product(one, two):
        left = jnp.concatenate([ys[one[1]], ys[two[1]]], axis=1)
        return dot(left, jnp.concatenate([one[0], two[0]], axis=0))

    return product


def backward_far_kernel(plan_ref, ys, gw_ref, w_ref, msg_ref, acc):
    acc[...] = jnp.zeros_like(acc)
    run_class(plan_ref, 0, w_ref, None, None, backward_product(ys), acc)
    for q in range(N_REP):
        msg_ref[q, :, pl.ds(0, FQ), :] = acc[pl.ds(0, REMOTE), pl.ds(q * FQ, FQ), :].astype(BF16)
        for m in range(16):
            piece = acc[REMOTE + m // 2, pl.ds(q * FQ + (m % 2) * 16, 16), :]
            msg_ref[q, 2 * m, pl.ds(FQ, 16), :] = piece.astype(BF16)
            if m < 8:
                msg_ref[q, 2 * m + 1, pl.ds(FQ, 16), :] = gw_ref[q * 8 + m]
            else:
                msg_ref[q, 2 * m + 1, pl.ds(FQ, 16), :] = jnp.zeros((16, BLK), BF16)


def backward_far(plan, ys, gw, weights):
    return pl.pallas_call(
        backward_far_kernel,
        out_shape=jax.ShapeDtypeStruct((N_REP, N_DOM, MSG, BLK), BF16),
        in_specs=[SM] + [VM] * 3,
        out_specs=VM,
        scratch_shapes=[pltpu.VMEM((REMOTE + HUBS, FIN, BLK), F32)],
        compiler_params=TILE_PARAMS,
        cost_estimate=pl.CostEstimate(flops=4 * 10**9, bytes_accessed=14 * 10**6, transcendentals=0),
        name="backward_far",
    )(plan, ys, gw, weights)


def backward_near_kernel(plan_ref, rep_ref, ys, w_ref, own_ref, s1, s2, s3, acc, held, sems):
    fetch_first(plan_ref, 1, w_ref, held, sems)
    rep = rep_ref[0]
    acc[...] = jnp.zeros_like(acc)
    run_class(plan_ref, 1, w_ref, held, sems, backward_product(ys), acc)

    def rows_of(k):
        start = pl.multiple_of(lax.rem(rep + k, N_REP) * FQ, FQ)
        return acc[:, pl.ds(start, FQ), :]

    own_ref[...] = rows_of(0)
    for k, ref in ((1, s1), (2, s2), (3, s3)):
        ref[...] = rows_of(k).astype(BF16)


def backward_near(plan, rep, ys, weights):
    part = (LOCAL, FQ, BLK)
    return pl.pallas_call(
        backward_near_kernel,
        out_shape=[jax.ShapeDtypeStruct(part, F32)] + [jax.ShapeDtypeStruct(part, BF16)] * 3,
        in_specs=[SM, SM, VM, FAR],
        out_specs=[VM] * 4,
        scratch_shapes=[pltpu.VMEM((LOCAL, FIN, BLK), F32)] + keep(LOCAL * LOCAL, LOCAL),
        compiler_params=TILE_PARAMS,
        cost_estimate=pl.CostEstimate(flops=10**9, bytes_accessed=14 * 10**6, transcendentals=0),
        name="backward_near",
    )(plan, rep, ys, weights)


SCATTER_PEERS = 8


def scatter_kernel(count_ref, rows_ref, recv_ref, own_ref, a_ref, b_ref, c_ref, out_ref, acc):
    chunks = ROWS // LO
    slot = lax.broadcasted_iota(jnp.int32, (1, BLK), 1)
    acc[...] = jnp.zeros_like(acc)

    def step(i, carry):
        hots, sides = [], []
        for j in range(SCATTER_PEERS):
            p = SCATTER_PEERS * i + j
            row = jnp.where(slot < count_ref[0, p], rows_ref[pl.ds(p, 1), :], -1)
            hots.append(low_onehot(column(row)))
            total = recv_ref[p, pl.ds(0, FQ), :].astype(F32)
            for r in range(1, N_REP):
                total = total + recv_ref[r * N_DOM + p, pl.ds(0, FQ), :].astype(F32)
            high = lax.shift_right_arithmetic(row, 8)
            pieces = [halves(jnp.where(high == c, total, 0.0)) for c in range(chunks)]
            sides.append(jnp.concatenate([h for h, _ in pieces] + [l for _, l in pieces], axis=0))
        acc[...] += dot(jnp.concatenate(sides, axis=1), jnp.concatenate(hots, axis=0))
        return carry

    lax.fori_loop(0, N_DOM // SCATTER_PEERS, step, 0)
    for b in range(LOCAL):
        c, side = b // 2, b % 2
        lanes = pl.ds(side * BLK, BLK)
        here = acc[pl.ds(c * FQ, FQ), lanes] + acc[pl.ds((chunks + c) * FQ, FQ), lanes]
        near = own_ref[b] + a_ref[b].astype(F32) + b_ref[b].astype(F32) + c_ref[b].astype(F32)
        out_ref[b] = (here + near).astype(BF16)


def scatter_rows(counts, rows, received, own, a, b, c):
    return pl.pallas_call(
        scatter_kernel,
        out_shape=jax.ShapeDtypeStruct((LOCAL, FQ, BLK), BF16),
        in_specs=[SM] + [VM] * 6,
        out_specs=VM,
        scratch_shapes=[pltpu.VMEM((2 * FIN * 2, LO), F32)],
        compiler_params=PARAMS,
        cost_estimate=pl.CostEstimate(flops=4 * 10**9, bytes_accessed=4 * 10**6, transcendentals=0),
        name="scatter_rows",
    )(counts, rows, received, own, a, b, c)


def final_kernel(place_ref, hub_ref, m0, m1, m2, m3, shared_ref, gx_ref, gw_ref, blocks, *, scale):
    rep = place_ref[0]
    for k, ref in enumerate((m0, m1, m2, m3)):
        start = pl.multiple_of(lax.rem(rep + N_REP - k, N_REP) * FQ, FQ)
        blocks[:, pl.ds(start, FQ), :] = ref[...].astype(F32)
    for h in range(HUBS):
        block = hub_ref[h]

        @pl.when(lax.shift_right_logical(block, 4) == place_ref[1])
        def _():
            for q in range(N_REP):
                for k in range(2):
                    piece = shared_ref[q * N_DOM + 4 * h + 2 * k].astype(F32)
                    blocks[block & (LOCAL - 1), pl.ds(q * FQ + k * 16, 16), :] += piece

    for b in range(LOCAL):
        gx_ref[pl.ds(b * BLK, BLK), :] = blocks[b].T
    for c in range(16):
        g, side = c // 2, c % 2
        high, low = [shared_ref[(n // 8) * N_DOM + 2 * (n % 8) + 1].astype(F32) for n in (c, 16 + c)]
        gw_ref[pl.ds(g * 16, 16), pl.ds(side * BLK, BLK)] = (high + low) * scale


def finish(place, hubs, parts, shared, scale):
    return pl.pallas_call(
        functools.partial(final_kernel, scale=scale),
        out_shape=[
            jax.ShapeDtypeStruct((ROWS, FIN), F32),
            jax.ShapeDtypeStruct((FIN, HID), F32),
        ],
        in_specs=[SM, SM] + [VM] * 5,
        out_specs=[VM] * 2,
        scratch_shapes=[pltpu.VMEM((LOCAL, FIN, BLK), F32)],
        compiler_params=PARAMS,
        name="finish",
    )(place, hubs, *parts, shared)


def turn(value, k):
    return lax.ppermute(value, "rep", [(i, (i + k) % N_REP) for i in range(N_REP)])


def around(value):
    return [value] + [turn(value, k) for k in (1, 2, 3)]


def swap(value, axes):
    return lax.all_to_all(value, axes, split_axis=0, concat_axis=0, tiled=True)


def shards(
    features,
    proj_weight,
    bias,
    cotangent,
    send_rows,
    send_count,
    hub_blocks,
    tile_dst,
    tile_src,
    tile_weight,
):
    rep = lax.axis_index("rep").astype(jnp.int32)
    dom = lax.axis_index("dom").astype(jnp.int32)
    place = jnp.stack([rep, dom])
    hub_blocks, send_count = in_hbm(hub_blocks), in_hbm(send_count)
    blocks = features.reshape(LOCAL, BLK, FIN)
    rows = send_rows[0]

    weights = tile_weight[0, 0]
    spread = swap(pick_hubs(place, hub_blocks, blocks).reshape(N_DOM, HUB_ROWS, FIN), "dom")
    listed = gather_rows(rows, send_count, features)
    received = swap(insert_hubs(spread, listed), "dom")
    fwd, bwd = order_tiles(
        tile_dst[0, 0].reshape(TILES // BLK, BLK), tile_src[0, 0].reshape(TILES // BLK, BLK)
    )
    stored = in_hbm(weights)
    near = forward_near(fwd, blocks, stored)
    own, s1, s2, s3 = forward_far(fwd, place, near, received, stored)
    held = hold_tiles(stored, s1)
    a, b, c = turn(s1, 1), turn(s2, 2), turn(s3, 3)
    a, held = lax.optimization_barrier((a, held))
    zq = sum_quarter(own, a, b, c)
    output, ys, gw = middle(place, around(zq), proj_weight, bias.reshape(1, HID), cotangent)
    message = backward_far(bwd, ys, gw, held)
    returned = swap(message.reshape(N_REP * N_DOM, MSG, BLK), ("rep", "dom"))
    own, s1, s2, s3 = backward_near(bwd, place, ys, stored)
    a, b, c = turn(s1, 1), turn(s2, 2), turn(s3, 3)

    piece = jnp.sum(returned[:, FQ:, :].astype(F32), axis=0).astype(BF16)
    shared = swap(jnp.broadcast_to(piece[None], (N_REP * N_DOM, 16, BLK)), ("rep", "dom"))
    part = scatter_rows(send_count, rows, returned, own, a, b, c)
    grad_x, grad_w = finish(place, hub_blocks, around(part), shared, 1.0 / math.sqrt(ROWS * N_DOM))
    return (output, grad_x, grad_w)


def solution(mesh):
    in_specs = (
        P("dom", None),
        P(),
        P(),
        P("dom", None),
        P("dom", None, None),
        P("dom", None),
        P(),
        P("rep", "dom", None),
        P("rep", "dom", None),
        P("rep", "dom", None, None, None),
    )
    out_specs = (P("dom", None), P("dom", None), P())
    return jax.shard_map(shards, mesh=mesh, in_specs=in_specs, out_specs=out_specs, check_vma=False)
```

```python
import functools
import math

import jax
import jax.numpy as jnp
from jax import lax
from jax.experimental import pallas as pl
from jax.experimental.pallas import tpu as pltpu
from jax.sharding import PartitionSpec as P

F32 = jnp.float32
BF16 = jnp.bfloat16
BLK = 128
N_REP = 4
N_DOM = 32
FIN = 128
HID = 256
ROWS = 2048
LOCAL = ROWS // BLK
HUBS = 8
BLOCKS = LOCAL + N_DOM + HUBS
TILES = 384
REMOTE = N_DOM
CHUNK = 32
FWD_SLOTS = 512
BWD_SLOTS = 512
QUARTER = ROWS // N_REP
QB = LOCAL // N_REP
FQ = FIN // N_REP
MSG = FQ + 16
HUB_ROWS = HUBS * BLK // N_DOM
LO = 256
VMEM_LIMIT = 24 * 1024 * 1024

VM = pl.BlockSpec(memory_space=pltpu.VMEM)
SM = pl.BlockSpec(memory_space=pltpu.SMEM)
FAR = pl.BlockSpec(memory_space=pltpu.HBM)
PARAMS = pltpu.CompilerParams(vmem_limit_bytes=VMEM_LIMIT)
TILE_PARAMS = PARAMS


def in_hbm(x):
    return pltpu.with_memory_space_constraint(x, pltpu.HBM)


def dot(a, b):
    return jnp.dot(a, b, preferred_element_type=F32)


def halves(x):
    high = x.astype(BF16)
    return high, (x - high.astype(F32)).astype(BF16)


def column(row):
    return jnp.broadcast_to(row, (BLK, BLK)).T


def low_onehot(col):
    low = jnp.where(col < 0, -1, col & (LO - 1))
    lane = lax.broadcasted_iota(jnp.int32, (BLK, BLK), 1)
    return jnp.concatenate(
        [jnp.where(low == lane + k * BLK, 1.0, 0.0) for k in range(LO // BLK)], axis=1
    ).astype(BF16)


def sort_tiles(bucket, operand, empty, edges, out_of, slots):
    sub = lax.broadcasted_iota(jnp.int32, (BLK, BLK), 0)
    lane = lax.broadcasted_iota(jnp.int32, (BLK, BLK), 1)
    line = lane[:1]
    parts = len(bucket)
    cols = [column(b) for b in bucket]
    hots = [jnp.where(c == lane, 1.0, 0.0) for c in cols]
    counts = sum(jnp.sum(h, axis=0, keepdims=True) for h in hots).astype(jnp.int32)
    padded = (counts + 1) & -2
    before = jnp.where(sub < lane, column(padded).astype(F32), 0.0)
    starts = jnp.sum(before, axis=0, keepdims=True).astype(jnp.int32)
    first = jnp.zeros((1, BLK), jnp.int32)
    low = 0
    for n, high in enumerate(edges):
        inside = (line >= low) & (line < high)
        size = jnp.sum(jnp.where(inside, padded, 0).astype(F32), axis=1, keepdims=True).astype(jnp.int32)
        gap = ((size + CHUNK - 1) & -CHUNK) - size
        starts = starts + jnp.where(line >= high, gap, 0)
        total = (size + CHUNK - 1) // CHUNK
        first = first + jnp.where(line > n, total, 0)
        low = high
    begin, end = column(starts), column(starts + padded)
    places = []
    for i in range(parts):
        rank = jnp.sum(jnp.where(hots[i] > 0.0, starts.astype(F32), 0.0), axis=1, keepdims=True)
        for j in range(i + 1):
            same = jnp.broadcast_to(bucket[j], (BLK, BLK)) == cols[i]
            if j == i:
                same = same & (lane < sub)
            rank = rank + jnp.sum(jnp.where(same, 1.0, 0.0), axis=1, keepdims=True)
        places.append(jnp.broadcast_to(rank.astype(jnp.int32), (BLK, BLK)))
    shifted = [column(o - empty).astype(F32) for o in operand]
    tiles, blocks, outs = [], [], []
    for s in range(slots // BLK):
        here = lane + s * BLK
        tile = jnp.zeros((1, BLK), F32)
        block = jnp.zeros((1, BLK), F32)
        taken = jnp.zeros((1, BLK), F32)
        for i in range(parts):
            hit = places[i] == here
            taken = taken + jnp.sum(jnp.where(hit, 1.0, 0.0), axis=0, keepdims=True)
            tile = tile + jnp.sum(jnp.where(hit, (sub + i * BLK).astype(F32), 0.0), axis=0, keepdims=True)
            block = block + jnp.sum(jnp.where(hit, shifted[i], 0.0), axis=0, keepdims=True)
        inside = (begin <= here) & (here < end)
        out = jnp.sum(jnp.where(inside, out_of(sub).astype(F32), 0.0), axis=0, keepdims=True)
        tile = tile + (1.0 - taken) * (here[:1] & 255).astype(F32)
        tiles.append(tile.astype(jnp.int32))
        blocks.append(block.astype(jnp.int32) + empty)
        outs.append(out.astype(jnp.int32))
    return tiles, blocks, outs, first


def order_kernel(dst_ref, src_ref, fwd_ref, bwd_ref):
    parts = TILES // BLK
    dst = [dst_ref[pl.ds(i, 1), :] for i in range(parts)]
    src = [src_ref[pl.ds(i, 1), :] for i in range(parts)]
    bucket = [jnp.where(s < LOCAL, d, d + LOCAL) for d, s in zip(dst, src)]
    operand = [jnp.where(s < LOCAL, s, s - LOCAL) for s in src]
    empty = REMOTE + HUBS
    found = sort_tiles(bucket, operand, empty, (LOCAL, 2 * LOCAL), lambda b: b & (LOCAL - 1), FWD_SLOTS)
    for n, rows in enumerate(found[:3]):
        for s, row in enumerate(rows):
            fwd_ref[n, pl.ds(s, 1), :] = row
    fwd_ref[3, pl.ds(0, 1), :] = found[3]
    far = REMOTE + HUBS
    bucket = [jnp.where(s < LOCAL, s + far, s - LOCAL) for s in src]
    found = sort_tiles(
        bucket, dst, LOCAL, (far, far + LOCAL), lambda b: jnp.where(b < far, b, b - far), BWD_SLOTS
    )
    for n, rows in enumerate(found[:3]):
        for s, row in enumerate(rows):
            bwd_ref[n, pl.ds(s, 1), :] = row
    bwd_ref[3, pl.ds(0, 1), :] = found[3]


def order_tiles(dst, src):
    return pl.pallas_call(
        order_kernel,
        out_shape=[
            jax.ShapeDtypeStruct((4, FWD_SLOTS // BLK, BLK), jnp.int32),
            jax.ShapeDtypeStruct((4, BWD_SLOTS // BLK, BLK), jnp.int32),
        ],
        in_specs=[VM, VM],
        out_specs=[VM, VM],
        compiler_params=PARAMS,
        name="order_tiles",
    )(dst, src)


AHEAD = 6


def keep(tiles, buckets):
    chunks = -(-(tiles + buckets) // CHUNK)
    return [pltpu.VMEM((chunks * CHUNK, BLK, BLK), BF16), pltpu.SemaphoreType.DMA((chunks,))]


def extent(plan_ref, number):
    begin = plan_ref[3, 0, number]
    return begin, plan_ref[3, 0, number + 1] - begin


def where(i):
    return i // (BLK // CHUNK), lax.rem(i, BLK // CHUNK) * CHUNK


def fetch(plan_ref, number, c, w_ref, held, sems):
    row, col = where(extent(plan_ref, number)[0] + c)
    for k in range(CHUNK):
        tile = plan_ref[0, row, col + k]
        pltpu.make_async_copy(w_ref.at[tile], held.at[c * CHUNK + k], sems.at[c]).start()


def fetch_first(plan_ref, number, w_ref, held, sems):
    def first(c, carry):
        fetch(plan_ref, number, c, w_ref, held, sems)
        return carry

    lax.fori_loop(0, jnp.minimum(extent(plan_ref, number)[1], AHEAD), first, 0)


def run_class(plan_ref, number, w_ref, held, sems, product, acc):
    begin, count = extent(plan_ref, number)

    def chunk(c, carry):
        row, col = where(begin + c)
        if held is not None:
            slots = held.at[pl.ds(c * CHUNK, CHUNK)]
            pltpu.make_async_copy(w_ref.at[pl.ds(0, CHUNK)], slots, sems.at[c]).wait()

            @pl.when(c + AHEAD < count)
            def _():
                fetch(plan_ref, number, c + AHEAD, w_ref, held, sems)

        found = []
        for k in range(0, CHUNK, 2):
            pair = []
            for j in (k, k + 1):
                tile = w_ref[plan_ref[0, row, col + j]] if held is None else held[c * CHUNK + j]
                pair.append((tile, plan_ref[1, row, col + j]))
            one, two = pair
            found.append((plan_ref[2, row, col + k], product(one, two)))
        for d, value in found:
            acc[d] += value
        return carry

    lax.fori_loop(0, count, chunk, 0)


PEERS = 8


def gather_kernel(rows_hbm, count_ref, feat_hbm, out_ref, rows_ref, feat_ref, sems):
    loads = [
        pltpu.make_async_copy(feat_hbm, feat_ref, sems.at[0]),
        pltpu.make_async_copy(rows_hbm, rows_ref, sems.at[1]),
    ]
    for load in loads:
        load.start()
    for load in loads:
        load.wait()
    slot = lax.broadcasted_iota(jnp.int32, (1, BLK), 1)

    def step(i, carry):
        cols = []
        for j in range(PEERS):
            p = PEERS * i + j
            row = jnp.where(slot < count_ref[0, p], rows_ref[pl.ds(p, 1), :], -1)
            cols.append(column(row))
        hot = jnp.concatenate([low_onehot(c) for c in cols], axis=0)
        high = lax.shift_right_arithmetic(jnp.concatenate(cols, axis=0), 8)
        total = jnp.zeros((PEERS * BLK, FIN), F32)
        for pair in range(ROWS // LO // 2):
            left = feat_ref[pl.ds(2 * pair * LO, LO), :]
            right = feat_ref[pl.ds((2 * pair + 1) * LO, LO), :]
            got = dot(hot, jnp.concatenate([left, right], axis=1))
            total = jnp.where(high == 2 * pair, got[:, :FIN], total)
            total = jnp.where(high == 2 * pair + 1, got[:, FIN:], total)
        out_ref[pl.ds(PEERS * i, PEERS), pl.ds(0, BLK), :] = total.astype(BF16).reshape(PEERS, BLK, FIN)
        return carry

    lax.fori_loop(0, N_DOM // PEERS, step, 0)


def gather_rows(rows, counts, features):
    return pl.pallas_call(
        gather_kernel,
        out_shape=jax.ShapeDtypeStruct((N_DOM, BLK + HUB_ROWS, FIN), BF16),
        in_specs=[FAR, SM, FAR],
        out_specs=VM,
        scratch_shapes=[
            pltpu.VMEM((N_DOM, BLK), jnp.int32),
            pltpu.VMEM((ROWS, FIN), BF16),
            pltpu.SemaphoreType.DMA((2,)),
        ],
        compiler_params=PARAMS,
        cost_estimate=pl.CostEstimate(flops=4 * 10**9, bytes_accessed=2 * 10**6, transcendentals=0),
        name="gather_rows",
    )(in_hbm(rows), counts, in_hbm(features))


def hub_pick_kernel(place_ref, hub_ref, feat_ref, out_ref):
    for h in range(HUBS):
        block = hub_ref[h]
        mine = lax.shift_right_logical(block, 4) == place_ref[1]

        @pl.when(mine)
        def _():
            out_ref[h] = feat_ref[block & (LOCAL - 1)]

        @pl.when(jnp.logical_not(mine))
        def _():
            out_ref[h] = jnp.zeros((BLK, FIN), BF16)


def pick_hubs(place, hubs, features):
    return pl.pallas_call(
        hub_pick_kernel,
        out_shape=jax.ShapeDtypeStruct((HUBS, BLK, FIN), BF16),
        in_specs=[SM, SM, VM],
        out_specs=VM,
        compiler_params=PARAMS,
        name="pick_hubs",
    )(place, hubs, in_hbm(features))


def insert_kernel(spread_ref, listed_ref, out_ref, wide, sem):
    del listed_ref
    piece = spread_ref[0].astype(F32)
    for p in range(1, N_DOM):
        piece = piece + spread_ref[p].astype(F32)
    piece = piece.astype(BF16)
    for p in range(N_DOM):
        wide[p] = piece
    copy = pltpu.make_async_copy(wide, out_ref.at[:, pl.ds(BLK, HUB_ROWS), :], sem)
    copy.start()
    copy.wait()


def insert_hubs(spread, listed):
    return pl.pallas_call(
        insert_kernel,
        out_shape=jax.ShapeDtypeStruct(listed.shape, BF16),
        in_specs=[VM, pl.BlockSpec(memory_space=pl.ANY)],
        out_specs=pl.BlockSpec(memory_space=pl.ANY),
        scratch_shapes=[pltpu.VMEM((N_DOM, HUB_ROWS, FIN), BF16), pltpu.SemaphoreType.DMA],
        input_output_aliases={1: 0},
        compiler_params=PARAMS,
        name="insert_hubs",
    )(spread, listed)


def forward_product(xs):
    def product(one, two):
        left = jnp.concatenate([one[0], two[0]], axis=1)
        return dot(left, jnp.concatenate([xs[one[1]], xs[two[1]]], axis=0))

    return product


FORWARD_XS = pltpu.VMEM((REMOTE + HUBS + 1, BLK, FIN), BF16)


def forward_near_kernel(plan_ref, feat_ref, w_ref, acc_ref, xs, held, sems):
    fetch_first(plan_ref, 0, w_ref, held, sems)
    xs[pl.ds(0, LOCAL)] = feat_ref[...]
    xs[REMOTE + HUBS] = jnp.zeros((BLK, FIN), BF16)
    acc_ref[...] = jnp.zeros_like(acc_ref)
    run_class(plan_ref, 0, w_ref, held, sems, forward_product(xs), acc_ref)


def forward_far_kernel(plan_ref, place_ref, near_ref, recv_ref, w_ref, own_ref, s1, s2, s3, xs, acc, held, sems):
    fetch_first(plan_ref, 1, w_ref, held, sems)
    xs[pl.ds(0, REMOTE)] = recv_ref[:, pl.ds(0, BLK), :]
    per_hub = BLK // HUB_ROWS
    for p in range(N_DOM):
        rows = pl.ds((p % per_hub) * HUB_ROWS, HUB_ROWS)
        xs[REMOTE + p // per_hub, rows, :] = recv_ref[p, pl.ds(BLK, HUB_ROWS), :]
    xs[REMOTE + HUBS] = jnp.zeros((BLK, FIN), BF16)
    acc[...] = near_ref[...]
    run_class(plan_ref, 1, w_ref, held, sems, forward_product(xs), acc)
    rep = place_ref[0]
    own_ref[...] = acc[pl.ds(rep * QB, QB)]
    for k, ref in ((1, s1), (2, s2), (3, s3)):
        ref[...] = acc[pl.ds(lax.rem(rep + k, N_REP) * QB, QB)].astype(BF16)


def forward_near(plan, features, weights):
    return pl.pallas_call(
        forward_near_kernel,
        out_shape=jax.ShapeDtypeStruct((LOCAL, BLK, FIN), F32),
        in_specs=[SM, VM, FAR],
        out_specs=VM,
        scratch_shapes=[FORWARD_XS] + keep(LOCAL * LOCAL, LOCAL),
        compiler_params=TILE_PARAMS,
        cost_estimate=pl.CostEstimate(flops=10**9, bytes_accessed=4 * 10**6, transcendentals=0),
        name="forward_near",
    )(plan, features, weights)


def forward_far(plan, place, near, received, weights):
    quarter = (QB, BLK, FIN)
    return pl.pallas_call(
        forward_far_kernel,
        out_shape=[jax.ShapeDtypeStruct(quarter, F32)] + [jax.ShapeDtypeStruct(quarter, BF16)] * 3,
        in_specs=[SM, SM, VM, VM, FAR],
        out_specs=[VM] * 4,
        scratch_shapes=[FORWARD_XS, pltpu.VMEM((LOCAL, BLK, FIN), F32)] + keep(TILES, LOCAL),
        compiler_params=TILE_PARAMS,
        cost_estimate=pl.CostEstimate(flops=4 * 10**9, bytes_accessed=12 * 10**6, transcendentals=0),
        name="forward_far",
    )(plan, place, near, received, weights)


def sum_kernel(own_ref, a_ref, b_ref, c_ref, out_ref):
    far = a_ref[...].astype(F32) + b_ref[...].astype(F32) + c_ref[...].astype(F32)
    out_ref[...] = (own_ref[...] + far).astype(BF16)


def sum_quarter(own, a, b, c):
    return pl.pallas_call(
        sum_kernel,
        out_shape=jax.ShapeDtypeStruct((QB, BLK, FIN), BF16),
        in_specs=[VM] * 4,
        out_specs=VM,
        compiler_params=PARAMS,
        name="sum_quarter",
    )(own, a, b, c)


def middle_kernel(place_ref, z0, z1, z2, z3, w_ref, bias_ref, cot_ref, out_ref, y_ref, gw_ref):
    weight = w_ref[...]
    root = math.sqrt(2.0 / math.pi)
    for turned, ref in enumerate((z0, z1, z2, z3)):
        quarter = lax.rem(place_ref[0] + N_REP - turned, N_REP)
        zx = ref[...].reshape(QUARTER, FIN)
        pre = dot(zx, weight) + bias_ref[...]
        cubic = (root * 0.044715) * (pre * pre)
        bent = jnp.tanh(pre * (root + cubic))
        half = 0.5 * pre
        cdf = 0.5 * bent + 0.5
        rows = pl.ds(pl.multiple_of(quarter * QUARTER, QUARTER), QUARTER)
        out_ref[rows, :] = (half * bent + half).astype(BF16)
        slope = cdf + half * ((1.0 - bent * bent) * (root + 3.0 * cubic))
        pre_grad = (cot_ref[rows, :].astype(F32) * slope).astype(BF16)
        yt = lax.dot_general(weight, pre_grad, (((1,), (1,)), ((), ())), preferred_element_type=F32)
        yt = yt.astype(BF16)
        for k in range(QB):
            y_ref[quarter * QB + k] = yt[:, k * BLK : (k + 1) * BLK]
        if turned == 0:
            gw = dot(zx.T, pre_grad)
            for part, piece in enumerate(halves(gw)):
                for c in range(16):
                    g, side = c // 2, c % 2
                    gw_ref[part * 16 + c] = piece[g * 16 : (g + 1) * 16, side * BLK : (side + 1) * BLK]
    y_ref[LOCAL] = jnp.zeros((FIN, BLK), BF16)


def middle(place, zs, weight, bias, cotangent):
    return pl.pallas_call(
        middle_kernel,
        out_shape=[
            jax.ShapeDtypeStruct((ROWS, HID), BF16),
            jax.ShapeDtypeStruct((LOCAL + 1, FIN, BLK), BF16),
            jax.ShapeDtypeStruct((32, 16, BLK), BF16),
        ],
        in_specs=[SM] + [VM] * 7,
        out_specs=[VM] * 3,
        compiler_params=PARAMS,
        cost_estimate=pl.CostEstimate(flops=5 * 10**9, bytes_accessed=3 * 10**6, transcendentals=0),
        name="middle",
    )(place, *zs, weight, bias, cotangent)


def hold_kernel(w_ref, after_ref, held_ref, sem):
    del after_ref
    copy = pltpu.make_async_copy(w_ref, held_ref, sem)
    copy.start()
    copy.wait()


def hold_tiles(weights, after):
    return pl.pallas_call(
        hold_kernel,
        out_shape=pltpu.VMEM((TILES, BLK, BLK), BF16),
        in_specs=[FAR, pl.BlockSpec(memory_space=pl.ANY)],
        out_specs=VM,
        scratch_shapes=[pltpu.SemaphoreType.DMA],
        compiler_params=PARAMS,
        cost_estimate=pl.CostEstimate(flops=0, bytes_accessed=13 * 10**6, transcendentals=0),
        name="hold_tiles",
    )(weights, after)


def backward_product(ys):
    def product(one, two):
        left = jnp.concatenate([ys[one[1]], ys[two[1]]], axis=1)
        return dot(left, jnp.concatenate([one[0], two[0]], axis=0))

    return product


def backward_far_kernel(plan_ref, ys, gw_ref, w_ref, msg_ref, acc):
    acc[...] = jnp.zeros_like(acc)
    run_class(plan_ref, 0, w_ref, None, None, backward_product(ys), acc)
    for q in range(N_REP):
        msg_ref[q, :, pl.ds(0, FQ), :] = acc[pl.ds(0, REMOTE), pl.ds(q * FQ, FQ), :].astype(BF16)
        for m in range(16):
            piece = acc[REMOTE + m // 2, pl.ds(q * FQ + (m % 2) * 16, 16), :]
            msg_ref[q, 2 * m, pl.ds(FQ, 16), :] = piece.astype(BF16)
            if m < 8:
                msg_ref[q, 2 * m + 1, pl.ds(FQ, 16), :] = gw_ref[q * 8 + m]
            else:
                msg_ref[q, 2 * m + 1, pl.ds(FQ, 16), :] = jnp.zeros((16, BLK), BF16)


def backward_far(plan, ys, gw, weights):
    return pl.pallas_call(
        backward_far_kernel,
        out_shape=jax.ShapeDtypeStruct((N_REP, N_DOM, MSG, BLK), BF16),
        in_specs=[SM] + [VM] * 3,
        out_specs=VM,
        scratch_shapes=[pltpu.VMEM((REMOTE + HUBS, FIN, BLK), F32)],
        compiler_params=TILE_PARAMS,
        cost_estimate=pl.CostEstimate(flops=4 * 10**9, bytes_accessed=14 * 10**6, transcendentals=0),
        name="backward_far",
    )(plan, ys, gw, weights)


def backward_near_kernel(plan_ref, rep_ref, ys, w_ref, own_ref, s1, s2, s3, acc, held, sems):
    fetch_first(plan_ref, 1, w_ref, held, sems)
    rep = rep_ref[0]
    acc[...] = jnp.zeros_like(acc)
    run_class(plan_ref, 1, w_ref, held, sems, backward_product(ys), acc)

    def rows_of(k):
        start = pl.multiple_of(lax.rem(rep + k, N_REP) * FQ, FQ)
        return acc[:, pl.ds(start, FQ), :]

    own_ref[...] = rows_of(0)
    for k, ref in ((1, s1), (2, s2), (3, s3)):
        ref[...] = rows_of(k).astype(BF16)


def backward_near(plan, rep, ys, weights):
    part = (LOCAL, FQ, BLK)
    return pl.pallas_call(
        backward_near_kernel,
        out_shape=[jax.ShapeDtypeStruct(part, F32)] + [jax.ShapeDtypeStruct(part, BF16)] * 3,
        in_specs=[SM, SM, VM, FAR],
        out_specs=[VM] * 4,
        scratch_shapes=[pltpu.VMEM((LOCAL, FIN, BLK), F32)] + keep(LOCAL * LOCAL, LOCAL),
        compiler_params=TILE_PARAMS,
        cost_estimate=pl.CostEstimate(flops=10**9, bytes_accessed=14 * 10**6, transcendentals=0),
        name="backward_near",
    )(plan, rep, ys, weights)


SCATTER_PEERS = 8


def scatter_kernel(count_ref, rows_ref, recv_ref, own_ref, a_ref, b_ref, c_ref, out_ref, acc):
    chunks = ROWS // LO
    slot = lax.broadcasted_iota(jnp.int32, (1, BLK), 1)
    acc[...] = jnp.zeros_like(acc)

    def step(i, carry):
        hots, sides = [], []
        for j in range(SCATTER_PEERS):
            p = SCATTER_PEERS * i + j
            row = jnp.where(slot < count_ref[0, p], rows_ref[pl.ds(p, 1), :], -1)
            hots.append(low_onehot(column(row)))
            total = recv_ref[p, pl.ds(0, FQ), :].astype(F32)
            for r in range(1, N_REP):
                total = total + recv_ref[r * N_DOM + p, pl.ds(0, FQ), :].astype(F32)
            high = lax.shift_right_arithmetic(row, 8)
            pieces = [halves(jnp.where(high == c, total, 0.0)) for c in range(chunks)]
            sides.append(jnp.concatenate([h for h, _ in pieces] + [l for _, l in pieces], axis=0))
        acc[...] += dot(jnp.concatenate(sides, axis=1), jnp.concatenate(hots, axis=0))
        return carry

    lax.fori_loop(0, N_DOM // SCATTER_PEERS, step, 0)
    for b in range(LOCAL):
        c, side = b // 2, b % 2
        lanes = pl.ds(side * BLK, BLK)
        here = acc[pl.ds(c * FQ, FQ), lanes] + acc[pl.ds((chunks + c) * FQ, FQ), lanes]
        near = own_ref[b] + a_ref[b].astype(F32) + b_ref[b].astype(F32) + c_ref[b].astype(F32)
        out_ref[b] = (here + near).astype(BF16)


def scatter_rows(counts, rows, received, own, a, b, c):
    return pl.pallas_call(
        scatter_kernel,
        out_shape=jax.ShapeDtypeStruct((LOCAL, FQ, BLK), BF16),
        in_specs=[SM] + [VM] * 6,
        out_specs=VM,
        scratch_shapes=[pltpu.VMEM((2 * FIN * 2, LO), F32)],
        compiler_params=PARAMS,
        cost_estimate=pl.CostEstimate(flops=4 * 10**9, bytes_accessed=4 * 10**6, transcendentals=0),
        name="scatter_rows",
    )(counts, rows, received, own, a, b, c)


def piece_kernel(recv_ref, out_ref):
    sums = [recv_ref[n, pl.ds(FQ, 16), :].astype(F32) for n in range(4)]
    for n in range(4, N_REP * N_DOM):
        sums[n % 4] = sums[n % 4] + recv_ref[n, pl.ds(FQ, 16), :].astype(F32)
    piece = ((sums[0] + sums[1]) + (sums[2] + sums[3])).astype(BF16)
    for n in range(N_REP * N_DOM):
        out_ref[n] = piece


def sum_piece(received):
    return pl.pallas_call(
        piece_kernel,
        out_shape=jax.ShapeDtypeStruct((N_REP * N_DOM, 16, BLK), BF16),
        in_specs=[VM],
        out_specs=VM,
        compiler_params=PARAMS,
        name="sum_piece",
    )(received)


def final_kernel(place_ref, hub_ref, m0, m1, m2, m3, shared_ref, gx_ref, gw_ref, blocks, *, scale):
    rep = place_ref[0]
    for k, ref in enumerate((m0, m1, m2, m3)):
        start = pl.multiple_of(lax.rem(rep + N_REP - k, N_REP) * FQ, FQ)
        blocks[:, pl.ds(start, FQ), :] = ref[...].astype(F32)
    for h in range(HUBS):
        block = hub_ref[h]

        @pl.when(lax.shift_right_logical(block, 4) == place_ref[1])
        def _():
            for q in range(N_REP):
                for k in range(2):
                    piece = shared_ref[q * N_DOM + 4 * h + 2 * k].astype(F32)
                    blocks[block & (LOCAL - 1), pl.ds(q * FQ + k * 16, 16), :] += piece

    for b in range(LOCAL):
        gx_ref[pl.ds(b * BLK, BLK), :] = blocks[b].T
    for c in range(16):
        g, side = c // 2, c % 2
        high, low = [shared_ref[(n // 8) * N_DOM + 2 * (n % 8) + 1].astype(F32) for n in (c, 16 + c)]
        gw_ref[pl.ds(g * 16, 16), pl.ds(side * BLK, BLK)] = (high + low) * scale


def finish(place, hubs, parts, shared, scale):
    return pl.pallas_call(
        functools.partial(final_kernel, scale=scale),
        out_shape=[
            jax.ShapeDtypeStruct((ROWS, FIN), F32),
            jax.ShapeDtypeStruct((FIN, HID), F32),
        ],
        in_specs=[SM, SM] + [VM] * 5,
        out_specs=[VM] * 2,
        scratch_shapes=[pltpu.VMEM((LOCAL, FIN, BLK), F32)],
        compiler_params=PARAMS,
        name="finish",
    )(place, hubs, *parts, shared)


def turn(value, k):
    return lax.ppermute(value, "rep", [(i, (i + k) % N_REP) for i in range(N_REP)])


def around(value):
    return [value] + [turn(value, k) for k in (1, 2, 3)]


def swap(value, axes):
    return lax.all_to_all(value, axes, split_axis=0, concat_axis=0, tiled=True)


def shards(
    features,
    proj_weight,
    bias,
    cotangent,
    send_rows,
    send_count,
    hub_blocks,
    tile_dst,
    tile_src,
    tile_weight,
):
    rep = lax.axis_index("rep").astype(jnp.int32)
    dom = lax.axis_index("dom").astype(jnp.int32)
    place = jnp.stack([rep, dom])
    hub_blocks, send_count = in_hbm(hub_blocks), in_hbm(send_count)
    blocks = features.reshape(LOCAL, BLK, FIN)
    rows = send_rows[0]

    weights = tile_weight[0, 0]
    spread = swap(pick_hubs(place, hub_blocks, blocks).reshape(N_DOM, HUB_ROWS, FIN), "dom")
    listed = gather_rows(rows, send_count, features)
    received = swap(insert_hubs(spread, listed), "dom")
    fwd, bwd = order_tiles(
        tile_dst[0, 0].reshape(TILES // BLK, BLK), tile_src[0, 0].reshape(TILES // BLK, BLK)
    )
    stored = in_hbm(weights)
    near = forward_near(fwd, blocks, stored)
    own, s1, s2, s3 = forward_far(fwd, place, near, received, stored)
    held = hold_tiles(stored, s1)
    a, b, c = turn(s1, 1), turn(s2, 2), turn(s3, 3)
    a, held = lax.optimization_barrier((a, held))
    zq = sum_quarter(own, a, b, c)
    output, ys, gw = middle(place, around(zq), proj_weight, bias.reshape(1, HID), cotangent)
    message = backward_far(bwd, ys, gw, held)
    returned = swap(message.reshape(N_REP * N_DOM, MSG, BLK), ("rep", "dom"))
    own, s1, s2, s3 = backward_near(bwd, place, ys, stored)
    a, b, c = turn(s1, 1), turn(s2, 2), turn(s3, 3)

    shared = swap(sum_piece(returned), ("rep", "dom"))
    part = scatter_rows(send_count, rows, returned, own, a, b, c)
    grad_x, grad_w = finish(place, hub_blocks, around(part), shared, 1.0 / math.sqrt(ROWS * N_DOM))
    return (output, grad_x, grad_w)


def solution(mesh):
    in_specs = (
        P("dom", None),
        P(),
        P(),
        P("dom", None),
        P("dom", None, None),
        P("dom", None),
        P(),
        P("rep", "dom", None),
        P("rep", "dom", None),
        P("rep", "dom", None, None, None),
    )
    out_specs = (P("dom", None), P("dom", None), P())
    return jax.shard_map(shards, mesh=mesh, in_specs=in_specs, out_specs=out_specs, check_vma=False)
```

```python
import functools
import math

import jax
import jax.numpy as jnp
from jax import lax
from jax.experimental import pallas as pl
from jax.experimental.pallas import tpu as pltpu
from jax.sharding import PartitionSpec as P

F32 = jnp.float32
BF16 = jnp.bfloat16
BLK = 128
N_REP = 4
N_DOM = 32
FIN = 128
HID = 256
ROWS = 2048
LOCAL = ROWS // BLK
HUBS = 8
BLOCKS = LOCAL + N_DOM + HUBS
TILES = 384
REMOTE = N_DOM
CHUNK = 32
FWD_SLOTS = 512
BWD_SLOTS = 512
QUARTER = ROWS // N_REP
QB = LOCAL // N_REP
FQ = FIN // N_REP
MSG = FQ + 16
HUB_ROWS = HUBS * BLK // N_DOM
LO = 256
VMEM_LIMIT = 24 * 1024 * 1024

VM = pl.BlockSpec(memory_space=pltpu.VMEM)
SM = pl.BlockSpec(memory_space=pltpu.SMEM)
FAR = pl.BlockSpec(memory_space=pltpu.HBM)
PARAMS = pltpu.CompilerParams(vmem_limit_bytes=VMEM_LIMIT)
TILE_PARAMS = PARAMS


def in_hbm(x):
    return pltpu.with_memory_space_constraint(x, pltpu.HBM)


def dot(a, b):
    return jnp.dot(a, b, preferred_element_type=F32)


def halves(x):
    high = x.astype(BF16)
    return high, (x - high.astype(F32)).astype(BF16)


def column(row):
    return jnp.broadcast_to(row, (BLK, BLK)).T


def low_onehot(col):
    low = jnp.where(col < 0, -1, col & (LO - 1))
    lane = lax.broadcasted_iota(jnp.int32, (BLK, BLK), 1)
    return jnp.concatenate(
        [jnp.where(low == lane + k * BLK, 1.0, 0.0) for k in range(LO // BLK)], axis=1
    ).astype(BF16)


def sort_tiles(bucket, operand, empty, edges, out_of, slots):
    sub = lax.broadcasted_iota(jnp.int32, (BLK, BLK), 0)
    lane = lax.broadcasted_iota(jnp.int32, (BLK, BLK), 1)
    line = lane[:1]
    parts = len(bucket)
    cols = [column(b) for b in bucket]
    hots = [jnp.where(c == lane, 1.0, 0.0) for c in cols]
    counts = sum(jnp.sum(h, axis=0, keepdims=True) for h in hots).astype(jnp.int32)
    padded = (counts + 1) & -2
    before = jnp.where(sub < lane, column(padded).astype(F32), 0.0)
    starts = jnp.sum(before, axis=0, keepdims=True).astype(jnp.int32)
    first = jnp.zeros((1, BLK), jnp.int32)
    low = 0
    for n, high in enumerate(edges):
        inside = (line >= low) & (line < high)
        size = jnp.sum(jnp.where(inside, padded, 0).astype(F32), axis=1, keepdims=True).astype(jnp.int32)
        gap = ((size + CHUNK - 1) & -CHUNK) - size
        starts = starts + jnp.where(line >= high, gap, 0)
        total = (size + CHUNK - 1) // CHUNK
        first = first + jnp.where(line > n, total, 0)
        low = high
    begin, end = column(starts), column(starts + padded)
    places = []
    for i in range(parts):
        rank = jnp.sum(jnp.where(hots[i] > 0.0, starts.astype(F32), 0.0), axis=1, keepdims=True)
        for j in range(i + 1):
            same = jnp.broadcast_to(bucket[j], (BLK, BLK)) == cols[i]
            if j == i:
                same = same & (lane < sub)
            rank = rank + jnp.sum(jnp.where(same, 1.0, 0.0), axis=1, keepdims=True)
        places.append(jnp.broadcast_to(rank.astype(jnp.int32), (BLK, BLK)))
    shifted = [column(o - empty).astype(F32) for o in operand]
    tiles, blocks, outs = [], [], []
    for s in range(slots // BLK):
        here = lane + s * BLK
        tile = jnp.zeros((1, BLK), F32)
        block = jnp.zeros((1, BLK), F32)
        taken = jnp.zeros((1, BLK), F32)
        for i in range(parts):
            hit = places[i] == here
            taken = taken + jnp.sum(jnp.where(hit, 1.0, 0.0), axis=0, keepdims=True)
            tile = tile + jnp.sum(jnp.where(hit, (sub + i * BLK).astype(F32), 0.0), axis=0, keepdims=True)
            block = block + jnp.sum(jnp.where(hit, shifted[i], 0.0), axis=0, keepdims=True)
        inside = (begin <= here) & (here < end)
        out = jnp.sum(jnp.where(inside, out_of(sub).astype(F32), 0.0), axis=0, keepdims=True)
        tile = tile + (1.0 - taken) * (here[:1] & 255).astype(F32)
        tiles.append(tile.astype(jnp.int32))
        blocks.append(block.astype(jnp.int32) + empty)
        outs.append(out.astype(jnp.int32))
    return tiles, blocks, outs, first


def order_kernel(dst_ref, src_ref, fwd_ref, bwd_ref):
    parts = TILES // BLK
    dst = [dst_ref[pl.ds(i, 1), :] for i in range(parts)]
    src = [src_ref[pl.ds(i, 1), :] for i in range(parts)]
    bucket = [jnp.where(s < LOCAL, d, d + LOCAL) for d, s in zip(dst, src)]
    operand = [jnp.where(s < LOCAL, s, s - LOCAL) for s in src]
    empty = REMOTE + HUBS
    found = sort_tiles(bucket, operand, empty, (LOCAL, 2 * LOCAL), lambda b: b & (LOCAL - 1), FWD_SLOTS)
    for n, rows in enumerate(found[:3]):
        for s, row in enumerate(rows):
            fwd_ref[n, pl.ds(s, 1), :] = row
    fwd_ref[3, pl.ds(0, 1), :] = found[3]
    far = REMOTE + HUBS
    bucket = [jnp.where(s < LOCAL, s + far, s - LOCAL) for s in src]
    found = sort_tiles(
        bucket, dst, LOCAL, (far, far + LOCAL), lambda b: jnp.where(b < far, b, b - far), BWD_SLOTS
    )
    for n, rows in enumerate(found[:3]):
        for s, row in enumerate(rows):
            bwd_ref[n, pl.ds(s, 1), :] = row
    bwd_ref[3, pl.ds(0, 1), :] = found[3]


def order_tiles(dst, src):
    return pl.pallas_call(
        order_kernel,
        out_shape=[
            jax.ShapeDtypeStruct((4, FWD_SLOTS // BLK, BLK), jnp.int32),
            jax.ShapeDtypeStruct((4, BWD_SLOTS // BLK, BLK), jnp.int32),
        ],
        in_specs=[VM, VM],
        out_specs=[VM, VM],
        compiler_params=PARAMS,
        name="order_tiles",
    )(dst, src)


AHEAD = 6


def keep(tiles, buckets):
    chunks = -(-(tiles + buckets) // CHUNK)
    return [pltpu.VMEM((chunks * CHUNK, BLK, BLK), BF16), pltpu.SemaphoreType.DMA((chunks,))]


def extent(plan_ref, number):
    begin = plan_ref[3, 0, number]
    return begin, plan_ref[3, 0, number + 1] - begin


def where(i):
    return i // (BLK // CHUNK), lax.rem(i, BLK // CHUNK) * CHUNK


def fetch(plan_ref, number, c, w_ref, held, sems):
    row, col = where(extent(plan_ref, number)[0] + c)
    for k in range(CHUNK):
        tile = plan_ref[0, row, col + k]
        pltpu.make_async_copy(w_ref.at[tile], held.at[c * CHUNK + k], sems.at[c]).start()


def fetch_first(plan_ref, number, w_ref, held, sems):
    def first(c, carry):
        fetch(plan_ref, number, c, w_ref, held, sems)
        return carry

    lax.fori_loop(0, jnp.minimum(extent(plan_ref, number)[1], AHEAD), first, 0)


def run_class(plan_ref, number, w_ref, held, sems, product, acc):
    begin, count = extent(plan_ref, number)

    def chunk(c, carry):
        row, col = where(begin + c)
        if held is not None:
            slots = held.at[pl.ds(c * CHUNK, CHUNK)]
            pltpu.make_async_copy(w_ref.at[pl.ds(0, CHUNK)], slots, sems.at[c]).wait()

            @pl.when(c + AHEAD < count)
            def _():
                fetch(plan_ref, number, c + AHEAD, w_ref, held, sems)

        found = []
        for k in range(0, CHUNK, 2):
            pair = []
            for j in (k, k + 1):
                tile = w_ref[plan_ref[0, row, col + j]] if held is None else held[c * CHUNK + j]
                pair.append((tile, plan_ref[1, row, col + j]))
            one, two = pair
            found.append((plan_ref[2, row, col + k], product(one, two)))
        for d, value in found:
            acc[d] += value
        return carry

    lax.fori_loop(0, count, chunk, 0)


PEERS = 8


def gather_kernel(rows_hbm, count_ref, feat_hbm, out_ref, rows_ref, feat_ref, sems):
    loads = [
        pltpu.make_async_copy(feat_hbm, feat_ref, sems.at[0]),
        pltpu.make_async_copy(rows_hbm, rows_ref, sems.at[1]),
    ]
    for load in loads:
        load.start()
    for load in loads:
        load.wait()
    slot = lax.broadcasted_iota(jnp.int32, (1, BLK), 1)

    def step(i, carry):
        cols = []
        for j in range(PEERS):
            p = PEERS * i + j
            row = jnp.where(slot < count_ref[0, p], rows_ref[pl.ds(p, 1), :], -1)
            cols.append(column(row))
        hot = jnp.concatenate([low_onehot(c) for c in cols], axis=0)
        high = lax.shift_right_arithmetic(jnp.concatenate(cols, axis=0), 8)
        total = jnp.zeros((PEERS * BLK, FIN), F32)
        for pair in range(ROWS // LO // 2):
            left = feat_ref[pl.ds(2 * pair * LO, LO), :]
            right = feat_ref[pl.ds((2 * pair + 1) * LO, LO), :]
            got = dot(hot, jnp.concatenate([left, right], axis=1))
            total = jnp.where(high == 2 * pair, got[:, :FIN], total)
            total = jnp.where(high == 2 * pair + 1, got[:, FIN:], total)
        out_ref[pl.ds(PEERS * i, PEERS), pl.ds(0, BLK), :] = total.astype(BF16).reshape(PEERS, BLK, FIN)
        return carry

    lax.fori_loop(0, N_DOM // PEERS, step, 0)


def gather_rows(rows, counts, features):
    return pl.pallas_call(
        gather_kernel,
        out_shape=jax.ShapeDtypeStruct((N_DOM, BLK + HUB_ROWS, FIN), BF16),
        in_specs=[FAR, SM, FAR],
        out_specs=VM,
        scratch_shapes=[
            pltpu.VMEM((N_DOM, BLK), jnp.int32),
            pltpu.VMEM((ROWS, FIN), BF16),
            pltpu.SemaphoreType.DMA((2,)),
        ],
        compiler_params=PARAMS,
        cost_estimate=pl.CostEstimate(flops=4 * 10**9, bytes_accessed=2 * 10**6, transcendentals=0),
        name="gather_rows",
    )(in_hbm(rows), counts, in_hbm(features))


def hub_pick_kernel(place_ref, hub_ref, feat_ref, out_ref):
    for h in range(HUBS):
        block = hub_ref[h]
        mine = lax.shift_right_logical(block, 4) == place_ref[1]

        @pl.when(mine)
        def _():
            out_ref[h] = feat_ref[block & (LOCAL - 1)]

        @pl.when(jnp.logical_not(mine))
        def _():
            out_ref[h] = jnp.zeros((BLK, FIN), BF16)


def pick_hubs(place, hubs, features):
    return pl.pallas_call(
        hub_pick_kernel,
        out_shape=jax.ShapeDtypeStruct((HUBS, BLK, FIN), BF16),
        in_specs=[SM, SM, VM],
        out_specs=VM,
        compiler_params=PARAMS,
        name="pick_hubs",
    )(place, hubs, in_hbm(features))


def insert_kernel(spread_ref, listed_ref, out_ref, wide, sem):
    del listed_ref
    piece = spread_ref[0].astype(F32)
    for p in range(1, N_DOM):
        piece = piece + spread_ref[p].astype(F32)
    piece = piece.astype(BF16)
    for p in range(N_DOM):
        wide[p] = piece
    copy = pltpu.make_async_copy(wide, out_ref.at[:, pl.ds(BLK, HUB_ROWS), :], sem)
    copy.start()
    copy.wait()


def insert_hubs(spread, listed):
    return pl.pallas_call(
        insert_kernel,
        out_shape=jax.ShapeDtypeStruct(listed.shape, BF16),
        in_specs=[VM, pl.BlockSpec(memory_space=pl.ANY)],
        out_specs=pl.BlockSpec(memory_space=pl.ANY),
        scratch_shapes=[pltpu.VMEM((N_DOM, HUB_ROWS, FIN), BF16), pltpu.SemaphoreType.DMA],
        input_output_aliases={1: 0},
        compiler_params=PARAMS,
        name="insert_hubs",
    )(spread, listed)


def forward_product(xs):
    def product(one, two):
        left = jnp.concatenate([one[0], two[0]], axis=1)
        return dot(left, jnp.concatenate([xs[one[1]], xs[two[1]]], axis=0))

    return product


FORWARD_XS = pltpu.VMEM((REMOTE + HUBS + 1, BLK, FIN), BF16)


def forward_near_kernel(plan_ref, feat_ref, w_ref, acc_ref, xs, held, sems):
    fetch_first(plan_ref, 0, w_ref, held, sems)
    xs[pl.ds(0, LOCAL)] = feat_ref[...]
    xs[REMOTE + HUBS] = jnp.zeros((BLK, FIN), BF16)
    acc_ref[...] = jnp.zeros_like(acc_ref)
    run_class(plan_ref, 0, w_ref, held, sems, forward_product(xs), acc_ref)


def forward_far_kernel(plan_ref, place_ref, near_ref, recv_ref, w_ref, own_ref, s1, s2, s3, xs, acc, held, sems):
    fetch_first(plan_ref, 1, w_ref, held, sems)
    xs[pl.ds(0, REMOTE)] = recv_ref[:, pl.ds(0, BLK), :]
    per_hub = BLK // HUB_ROWS
    for p in range(N_DOM):
        rows = pl.ds((p % per_hub) * HUB_ROWS, HUB_ROWS)
        xs[REMOTE + p // per_hub, rows, :] = recv_ref[p, pl.ds(BLK, HUB_ROWS), :]
    xs[REMOTE + HUBS] = jnp.zeros((BLK, FIN), BF16)
    acc[...] = near_ref[...]
    run_class(plan_ref, 1, w_ref, held, sems, forward_product(xs), acc)
    rep = place_ref[0]
    own_ref[...] = acc[pl.ds(rep * QB, QB)]
    for k, ref in ((1, s1), (2, s2), (3, s3)):
        ref[...] = acc[pl.ds(lax.rem(rep + k, N_REP) * QB, QB)].astype(BF16)


def forward_near(plan, features, weights):
    return pl.pallas_call(
        forward_near_kernel,
        out_shape=jax.ShapeDtypeStruct((LOCAL, BLK, FIN), F32),
        in_specs=[SM, VM, FAR],
        out_specs=VM,
        scratch_shapes=[FORWARD_XS] + keep(LOCAL * LOCAL, LOCAL),
        compiler_params=TILE_PARAMS,
        cost_estimate=pl.CostEstimate(flops=10**9, bytes_accessed=4 * 10**6, transcendentals=0),
        name="forward_near",
    )(plan, features, weights)


def forward_far(plan, place, near, received, weights):
    quarter = (QB, BLK, FIN)
    return pl.pallas_call(
        forward_far_kernel,
        out_shape=[jax.ShapeDtypeStruct(quarter, F32)] + [jax.ShapeDtypeStruct(quarter, BF16)] * 3,
        in_specs=[SM, SM, VM, VM, FAR],
        out_specs=[VM] * 4,
        scratch_shapes=[FORWARD_XS, pltpu.VMEM((LOCAL, BLK, FIN), F32)] + keep(TILES, LOCAL),
        compiler_params=TILE_PARAMS,
        cost_estimate=pl.CostEstimate(flops=4 * 10**9, bytes_accessed=12 * 10**6, transcendentals=0),
        name="forward_far",
    )(plan, place, near, received, weights)


def sum_kernel(own_ref, a_ref, b_ref, c_ref, out_ref):
    far = a_ref[...].astype(F32) + b_ref[...].astype(F32) + c_ref[...].astype(F32)
    out_ref[...] = (own_ref[...] + far).astype(BF16)


def sum_quarter(own, a, b, c):
    return pl.pallas_call(
        sum_kernel,
        out_shape=jax.ShapeDtypeStruct((QB, BLK, FIN), BF16),
        in_specs=[VM] * 4,
        out_specs=VM,
        compiler_params=PARAMS,
        name="sum_quarter",
    )(own, a, b, c)


def middle_kernel(place_ref, z0, z1, z2, z3, w_ref, bias_ref, cot_ref, out_ref, y_ref, gw_ref):
    weight = w_ref[...]
    root = math.sqrt(2.0 / math.pi)
    for turned, ref in enumerate((z0, z1, z2, z3)):
        quarter = lax.rem(place_ref[0] + N_REP - turned, N_REP)
        zx = ref[...].reshape(QUARTER, FIN)
        pre = dot(zx, weight) + bias_ref[...]
        cubic = (root * 0.044715) * (pre * pre)
        bent = jnp.tanh(pre * (root + cubic))
        half = 0.5 * pre
        cdf = 0.5 * bent + 0.5
        rows = pl.ds(pl.multiple_of(quarter * QUARTER, QUARTER), QUARTER)
        out_ref[rows, :] = (half * bent + half).astype(BF16)
        slope = cdf + half * ((1.0 - bent * bent) * (root + 3.0 * cubic))
        pre_grad = (cot_ref[rows, :].astype(F32) * slope).astype(BF16)
        yt = lax.dot_general(weight, pre_grad, (((1,), (1,)), ((), ())), preferred_element_type=F32)
        yt = yt.astype(BF16)
        for k in range(QB):
            y_ref[quarter * QB + k] = yt[:, k * BLK : (k + 1) * BLK]
        if turned == 0:
            gw = dot(zx.T, pre_grad)
            for part, piece in enumerate(halves(gw)):
                for c in range(16):
                    g, side = c // 2, c % 2
                    gw_ref[part * 16 + c] = piece[g * 16 : (g + 1) * 16, side * BLK : (side + 1) * BLK]
    y_ref[LOCAL] = jnp.zeros((FIN, BLK), BF16)


def middle(place, zs, weight, bias, cotangent):
    return pl.pallas_call(
        middle_kernel,
        out_shape=[
            jax.ShapeDtypeStruct((ROWS, HID), BF16),
            jax.ShapeDtypeStruct((LOCAL + 1, FIN, BLK), BF16),
            jax.ShapeDtypeStruct((32, 16, BLK), BF16),
        ],
        in_specs=[SM] + [VM] * 7,
        out_specs=[VM] * 3,
        compiler_params=PARAMS,
        cost_estimate=pl.CostEstimate(flops=5 * 10**9, bytes_accessed=3 * 10**6, transcendentals=0),
        name="middle",
    )(place, *zs, weight, bias, cotangent)


def hold_kernel(w_ref, after_ref, held_ref, sem):
    del after_ref
    copy = pltpu.make_async_copy(w_ref, held_ref, sem)
    copy.start()
    copy.wait()


def hold_tiles(weights, after):
    return pl.pallas_call(
        hold_kernel,
        out_shape=pltpu.VMEM((TILES, BLK, BLK), BF16),
        in_specs=[FAR, pl.BlockSpec(memory_space=pl.ANY)],
        out_specs=VM,
        scratch_shapes=[pltpu.SemaphoreType.DMA],
        compiler_params=PARAMS,
        cost_estimate=pl.CostEstimate(flops=0, bytes_accessed=13 * 10**6, transcendentals=0),
        name="hold_tiles",
    )(weights, after)


def backward_product(ys):
    def product(one, two):
        left = jnp.concatenate([ys[one[1]], ys[two[1]]], axis=1)
        return dot(left, jnp.concatenate([one[0], two[0]], axis=0))

    return product


def backward_far_kernel(plan_ref, ys, gw_ref, w_ref, msg_hbm, acc, msg_ref, stored):
    acc[...] = jnp.zeros_like(acc)
    run_class(plan_ref, 0, w_ref, None, None, backward_product(ys), acc)
    stores = []
    for q in range(N_REP):
        msg_ref[q, :, pl.ds(0, FQ), :] = acc[pl.ds(0, REMOTE), pl.ds(q * FQ, FQ), :].astype(BF16)
        for m in range(16):
            piece = acc[REMOTE + m // 2, pl.ds(q * FQ + (m % 2) * 16, 16), :]
            msg_ref[q, 2 * m, pl.ds(FQ, 16), :] = piece.astype(BF16)
            if m < 8:
                msg_ref[q, 2 * m + 1, pl.ds(FQ, 16), :] = gw_ref[q * 8 + m]
            else:
                msg_ref[q, 2 * m + 1, pl.ds(FQ, 16), :] = jnp.zeros((16, BLK), BF16)
        stores.append(pltpu.make_async_copy(msg_ref.at[q], msg_hbm.at[q], stored.at[q]))
        stores[-1].start()
    for store in stores:
        store.wait()


def backward_far(plan, ys, gw, weights):
    return pl.pallas_call(
        backward_far_kernel,
        out_shape=jax.ShapeDtypeStruct((N_REP, N_DOM, MSG, BLK), BF16),
        in_specs=[SM] + [VM] * 3,
        out_specs=pl.BlockSpec(memory_space=pl.ANY),
        scratch_shapes=[
            pltpu.VMEM((REMOTE + HUBS, FIN, BLK), F32),
            pltpu.VMEM((N_REP, N_DOM, MSG, BLK), BF16),
            pltpu.SemaphoreType.DMA((N_REP,)),
        ],
        compiler_params=TILE_PARAMS,
        cost_estimate=pl.CostEstimate(flops=4 * 10**9, bytes_accessed=14 * 10**6, transcendentals=0),
        name="backward_far",
    )(plan, ys, gw, weights)


def backward_near_kernel(plan_ref, rep_ref, ys, w_ref, own_ref, s1, s2, s3, acc, held, sems):
    fetch_first(plan_ref, 1, w_ref, held, sems)
    rep = rep_ref[0]
    acc[...] = jnp.zeros_like(acc)
    run_class(plan_ref, 1, w_ref, held, sems, backward_product(ys), acc)

    def rows_of(k):
        start = pl.multiple_of(lax.rem(rep + k, N_REP) * FQ, FQ)
        return acc[:, pl.ds(start, FQ), :]

    own_ref[...] = rows_of(0)
    for k, ref in ((1, s1), (2, s2), (3, s3)):
        ref[...] = rows_of(k).astype(BF16)


def backward_near(plan, rep, ys, weights):
    part = (LOCAL, FQ, BLK)
    return pl.pallas_call(
        backward_near_kernel,
        out_shape=[jax.ShapeDtypeStruct(part, F32)] + [jax.ShapeDtypeStruct(part, BF16)] * 3,
        in_specs=[SM, SM, VM, FAR],
        out_specs=[VM] * 4,
        scratch_shapes=[pltpu.VMEM((LOCAL, FIN, BLK), F32)] + keep(LOCAL * LOCAL, LOCAL),
        compiler_params=TILE_PARAMS,
        cost_estimate=pl.CostEstimate(flops=10**9, bytes_accessed=14 * 10**6, transcendentals=0),
        name="backward_near",
    )(plan, rep, ys, weights)


SCATTER_PEERS = 8


def scatter_kernel(count_ref, rows_ref, recv_ref, own_ref, a_ref, b_ref, c_ref, out_ref, acc):
    chunks = ROWS // LO
    slot = lax.broadcasted_iota(jnp.int32, (1, BLK), 1)
    acc[...] = jnp.zeros_like(acc)

    def step(i, carry):
        hots, sides = [], []
        for j in range(SCATTER_PEERS):
            p = SCATTER_PEERS * i + j
            row = jnp.where(slot < count_ref[0, p], rows_ref[pl.ds(p, 1), :], -1)
            hots.append(low_onehot(column(row)))
            total = recv_ref[p, pl.ds(0, FQ), :].astype(F32)
            for r in range(1, N_REP):
                total = total + recv_ref[r * N_DOM + p, pl.ds(0, FQ), :].astype(F32)
            high = lax.shift_right_arithmetic(row, 8)
            pieces = [halves(jnp.where(high == c, total, 0.0)) for c in range(chunks)]
            sides.append(jnp.concatenate([h for h, _ in pieces] + [l for _, l in pieces], axis=0))
        acc[...] += dot(jnp.concatenate(sides, axis=1), jnp.concatenate(hots, axis=0))
        return carry

    lax.fori_loop(0, N_DOM // SCATTER_PEERS, step, 0)
    for b in range(LOCAL):
        c, side = b // 2, b % 2
        lanes = pl.ds(side * BLK, BLK)
        here = acc[pl.ds(c * FQ, FQ), lanes] + acc[pl.ds((chunks + c) * FQ, FQ), lanes]
        near = own_ref[b] + a_ref[b].astype(F32) + b_ref[b].astype(F32) + c_ref[b].astype(F32)
        out_ref[b] = (here + near).astype(BF16)


def scatter_rows(counts, rows, received, own, a, b, c):
    return pl.pallas_call(
        scatter_kernel,
        out_shape=jax.ShapeDtypeStruct((LOCAL, FQ, BLK), BF16),
        in_specs=[SM] + [VM] * 6,
        out_specs=VM,
        scratch_shapes=[pltpu.VMEM((2 * FIN * 2, LO), F32)],
        compiler_params=PARAMS,
        cost_estimate=pl.CostEstimate(flops=4 * 10**9, bytes_accessed=4 * 10**6, transcendentals=0),
        name="scatter_rows",
    )(counts, rows, received, own, a, b, c)


def piece_kernel(recv_ref, out_ref):
    sums = [recv_ref[n, pl.ds(FQ, 16), :].astype(F32) for n in range(4)]
    for n in range(4, N_REP * N_DOM):
        sums[n % 4] = sums[n % 4] + recv_ref[n, pl.ds(FQ, 16), :].astype(F32)
    piece = ((sums[0] + sums[1]) + (sums[2] + sums[3])).astype(BF16)
    for n in range(N_REP * N_DOM):
        out_ref[n] = piece


def sum_piece(received):
    return pl.pallas_call(
        piece_kernel,
        out_shape=jax.ShapeDtypeStruct((N_REP * N_DOM, 16, BLK), BF16),
        in_specs=[VM],
        out_specs=VM,
        compiler_params=PARAMS,
        name="sum_piece",
    )(received)


def final_kernel(place_ref, hub_ref, m0, m1, m2, m3, shared_ref, gx_ref, gw_ref, blocks, *, scale):
    rep = place_ref[0]
    for k, ref in enumerate((m0, m1, m2, m3)):
        start = pl.multiple_of(lax.rem(rep + N_REP - k, N_REP) * FQ, FQ)
        blocks[:, pl.ds(start, FQ), :] = ref[...].astype(F32)
    for h in range(HUBS):
        block = hub_ref[h]

        @pl.when(lax.shift_right_logical(block, 4) == place_ref[1])
        def _():
            for q in range(N_REP):
                for k in range(2):
                    piece = shared_ref[q * N_DOM + 4 * h + 2 * k].astype(F32)
                    blocks[block & (LOCAL - 1), pl.ds(q * FQ + k * 16, 16), :] += piece

    for b in range(LOCAL):
        gx_ref[pl.ds(b * BLK, BLK), :] = blocks[b].T
    for c in range(16):
        g, side = c // 2, c % 2
        high, low = [shared_ref[(n // 8) * N_DOM + 2 * (n % 8) + 1].astype(F32) for n in (c, 16 + c)]
        gw_ref[pl.ds(g * 16, 16), pl.ds(side * BLK, BLK)] = (high + low) * scale


def finish(place, hubs, parts, shared, scale):
    return pl.pallas_call(
        functools.partial(final_kernel, scale=scale),
        out_shape=[
            jax.ShapeDtypeStruct((ROWS, FIN), F32),
            jax.ShapeDtypeStruct((FIN, HID), F32),
        ],
        in_specs=[SM, SM] + [VM] * 5,
        out_specs=[VM] * 2,
        scratch_shapes=[pltpu.VMEM((LOCAL, FIN, BLK), F32)],
        compiler_params=PARAMS,
        name="finish",
    )(place, hubs, *parts, shared)


def turn(value, k):
    return lax.ppermute(value, "rep", [(i, (i + k) % N_REP) for i in range(N_REP)])


def around(value):
    return [value] + [turn(value, k) for k in (1, 2, 3)]


def swap(value, axes):
    return lax.all_to_all(value, axes, split_axis=0, concat_axis=0, tiled=True)


def shards(
    features,
    proj_weight,
    bias,
    cotangent,
    send_rows,
    send_count,
    hub_blocks,
    tile_dst,
    tile_src,
    tile_weight,
):
    rep = lax.axis_index("rep").astype(jnp.int32)
    dom = lax.axis_index("dom").astype(jnp.int32)
    place = jnp.stack([rep, dom])
    hub_blocks, send_count = in_hbm(hub_blocks), in_hbm(send_count)
    blocks = features.reshape(LOCAL, BLK, FIN)
    rows = send_rows[0]

    weights = tile_weight[0, 0]
    spread = swap(pick_hubs(place, hub_blocks, blocks).reshape(N_DOM, HUB_ROWS, FIN), "dom")
    listed = gather_rows(rows, send_count, features)
    received = swap(insert_hubs(spread, listed), "dom")
    fwd, bwd = order_tiles(
        tile_dst[0, 0].reshape(TILES // BLK, BLK), tile_src[0, 0].reshape(TILES // BLK, BLK)
    )
    stored = in_hbm(weights)
    near = forward_near(fwd, blocks, stored)
    own, s1, s2, s3 = forward_far(fwd, place, near, received, stored)
    held = hold_tiles(stored, s1)
    a, b, c = turn(s1, 1), turn(s2, 2), turn(s3, 3)
    a, held = lax.optimization_barrier((a, held))
    zq = sum_quarter(own, a, b, c)
    output, ys, gw = middle(place, around(zq), proj_weight, bias.reshape(1, HID), cotangent)
    message = backward_far(bwd, ys, gw, held)
    returned = swap(message.reshape(N_REP * N_DOM, MSG, BLK), ("rep", "dom"))
    own, s1, s2, s3 = backward_near(bwd, place, ys, stored)
    a, b, c = turn(s1, 1), turn(s2, 2), turn(s3, 3)

    shared = swap(sum_piece(returned), ("rep", "dom"))
    part = scatter_rows(send_count, rows, returned, own, a, b, c)
    grad_x, grad_w = finish(place, hub_blocks, around(part), shared, 1.0 / math.sqrt(ROWS * N_DOM))
    return (output, grad_x, grad_w)


def solution(mesh):
    in_specs = (
        P("dom", None),
        P(),
        P(),
        P("dom", None),
        P("dom", None, None),
        P("dom", None),
        P(),
        P("rep", "dom", None),
        P("rep", "dom", None),
        P("rep", "dom", None, None, None),
    )
    out_specs = (P("dom", None), P("dom", None), P())
    return jax.shard_map(shards, mesh=mesh, in_specs=in_specs, out_specs=out_specs, check_vma=False)
```
